32 devices in a mesh: stream: 8 (over y, x, core), dp: 4 (over z).
Axes of the slice: x: 2, y: 2, z: 4, core: 2. Of those that a mesh axis runs over, the one named last changes fastest.
Arguments:
- regions: bfloat16 [16384, 768], P(('stream', 'dp')), may hold values from -6 to 6
- cotangent: bfloat16 [16384, 768], P(('stream', 'dp')), may hold values from -6 to 6
- page_lens: int32 [16, 16], replicated, may hold values from 1 to 96, 512 in all within a row
- qkv_weight: float32 [1536, 2304], P('stream'), may hold values from -0.21875 to 0.21875
- out_weight: float32 [1536, 768], P('stream'), may hold values from -1.25 to 1.25
- up_weight: float32 [1536, 3072], P('stream'), may hold values from -0.21875 to 0.21875
- down_weight: float32 [6144, 768], P('stream'), may hold values from -0.109375 to 0.109375
- ln1_gain: float32 [1536], P('stream'), may hold values from 0.5 to 1.5
- ln1_bias: float32 [1536], P('stream'), may hold values from -3 to 3
- ln2_gain: float32 [1536], P('stream'), may hold values from 0.5 to 1.5
- ln2_bias: float32 [1536], P('stream'), may hold values from -3 to 3
- up_bias: float32 [6144], P('stream'), may hold values from -3 to 3
- down_bias: float32 [1536], P('stream'), may hold values from -3 to 3
- gate_own: float32 [1536], P('stream'), may hold values from -0.21875 to 0.21875
- gate_other: float32 [1536], P('stream'), may hold values from -0.21875 to 0.21875
Outputs:
- mixed_rows: bfloat16 [16384, 768], P(('stream', 'dp'))
- region_grad: float32 [16384, 768], P(('stream', 'dp'))
- qkv_weight_grad: float32 [1536, 2304], P('stream')
- out_weight_grad: float32 [1536, 768], P('stream')
- up_weight_grad: float32 [1536, 3072], P('stream')
- down_weight_grad: float32 [6144, 768], P('stream')
- ln1_gain_grad: float32 [1536], P('stream')
- ln1_bias_grad: float32 [1536], P('stream')
- ln2_gain_grad: float32 [1536], P('stream')
- ln2_bias_grad: float32 [1536], P('stream')
- up_bias_grad: float32 [6144], P('stream')
- down_bias_grad: float32 [1536], P('stream')
- gate_own_grad: float32 [1536], P('stream')
- gate_other_grad: float32 [1536], P('stream')
The draws below stay inside these ranges and needn't reach their ends.
Inputs may be any that keep to these rules, and one draw needn't show every extreme that they name: `page_lens`: each row holds the region counts of the pages packed into one row of 512 regions, in order; a row sums to 512 and its largest count is 96.
All inputs are finite; a program needn't handle non-finite values.
Results may differ from the reference program's by a relative error of at most 0.014.
The reference program's roundings to bfloat16 on the way count: a program that leaves them out, or rounds other values in their place, can miss the bound.
Values may be sent and summed in bfloat16 or wider, within the bound.
No kernel may reach another device: no remote copies, remote signals or barrier semaphores. Data moves between devices by JAX's collectives and lax.ppermute only.
A program may use at most 256 MiB of HBM per device.

```python
import math
import jax
import jax.numpy as jnp
import numpy as np
from jax import lax

D = 768
HEADS = 12
HEAD_DIM = 64
FF = 3072
SEQ = 512
PAGES = 16
PAGE_MOST = 96
TOKENS = 8192
PACKS = 16


def block_levels(rng, extent, cuts, least, high):
    def one(position, blocks):
        draws = jax.random.uniform(jax.random.fold_in(jax.random.fold_in(rng, 6), position), (blocks,), jnp.float32, least / len(cuts), high / len(cuts))
        return jnp.repeat(jnp.exp(draws), extent[position] // blocks).reshape((-1,) + (1,) * (len(extent) - position - 1))

    level = one(*cuts[0])
    for cut in cuts[1:]:
        level = level * one(*cut)
    return level


def length_profile(count, total, limit, lean):
    portions = [(1 << 20) // math.isqrt(grade ** lean) + 1 for grade in range(2, count + 1)]
    rest, counts = total - limit - (count - 1), [1] * (count - 1)
    while rest > 0:
        movable = [i for i in range(count - 1) if counts[i] < limit]
        mass, budget = sum([portions[i] for i in movable]), rest
        for i in movable:
            addition = min(limit - counts[i], max(1, budget * portions[i] // mass), rest)
            counts[i] = counts[i] + addition
            rest = rest - addition
    return np.array([limit] + counts)


def uneven_parts(key, number_of, total, most, skew):
    if number_of == 2:
        one = jax.random.randint(key, (), max(1, total - most), min(most, total - 1) + 1)
        return jnp.stack([one, total - one])
    tallies = jnp.asarray(length_profile(number_of, total, most, skew), jnp.int32)
    twos = (number_of - 1) // 2
    giver, taker = tallies[1:1 + 2 * twos:2], tallies[2:2 + 2 * twos:2]
    room = jnp.minimum(giver - 1, most - taker)
    moved = jax.random.randint(jax.random.fold_in(key, 1), (twos,), 0, 1 << 20) % (room + 1)
    tallies = tallies.at[1:1 + 2 * twos:2].set(giver - moved).at[2:2 + 2 * twos:2].set(taker + moved)
    return tallies[jax.random.permutation(jax.random.fold_in(key, 2), number_of)]


def normal_values(own_key, dims, deviation, most, split=(), kind=jnp.bfloat16):
    loudness = block_levels(own_key, dims, split, -0.22, 0.18) if split else 1.0
    array = jax.random.normal(own_key, dims, jnp.float32) * deviation * loudness
    return jnp.minimum(jnp.maximum(array, -most), most).astype(kind)


def setup_inputs(seed: int = 0) -> dict:
    seeds = jax.random.split(jax.random.key(seed), 16)
    regions = normal_values(seeds[0], (2 * TOKENS, D), 1.0, 6.0, ((0, 32),))
    cotangent = normal_values(seeds[1], (2 * TOKENS, D), 1.0, 6.0, ((0, 32),))
    page_lens = jax.vmap(lambda own: uneven_parts(own, PAGES, SEQ, PAGE_MOST, 2))(jax.random.split(seeds[2], PACKS)).reshape((PACKS, PAGES)).astype(jnp.int32)
    qkv_weight = normal_values(seeds[3], (2 * D, 3 * D), D ** -0.5, 0.21875, ((0, 8),), jnp.float32)
    out_weight = normal_values(seeds[4], (2 * D, D), (D // 32) ** -0.5, 1.25, ((0, 8),), jnp.float32)
    up_weight = normal_values(seeds[5], (2 * D, FF), D ** -0.5, 0.21875, ((0, 8),), jnp.float32)
    down_weight = normal_values(seeds[6], (2 * FF, D), FF ** -0.5, 0.109375, ((0, 8),), jnp.float32)
    ln1_gain = jnp.clip(1.0 + 0.1 * jax.random.normal(seeds[7], (2 * D,), jnp.float32), 0.5, 1.5)
    ln1_bias = normal_values(seeds[8], (2 * D,), 0.5, 3.0, ((0, 8),), jnp.float32)
    ln2_gain = jnp.clip(1.0 + 0.1 * jax.random.normal(seeds[9], (2 * D,), jnp.float32), 0.5, 1.5)
    ln2_bias = normal_values(seeds[10], (2 * D,), 0.5, 3.0, ((0, 8),), jnp.float32)
    up_bias = normal_values(seeds[11], (2 * FF,), 0.5, 3.0, ((0, 8),), jnp.float32)
    down_bias = normal_values(seeds[12], (2 * D,), 0.5, 3.0, ((0, 8),), jnp.float32)
    gate_own = normal_values(seeds[13], (2 * D,), D ** -0.5, 0.21875, ((0, 8),), jnp.float32)
    gate_other = normal_values(seeds[14], (2 * D,), D ** -0.5, 0.21875, ((0, 8),), jnp.float32)
    return {"regions": regions, "cotangent": cotangent, "page_lens": page_lens, "qkv_weight": qkv_weight, "out_weight": out_weight, "up_weight": up_weight, "down_weight": down_weight, "ln1_gain": ln1_gain, "ln1_bias": ln1_bias, "ln2_gain": ln2_gain, "ln2_bias": ln2_bias, "up_bias": up_bias, "down_bias": down_bias, "gate_own": gate_own, "gate_other": gate_other}


@jax.custom_vjp
def low(v):
    return lax.optimization_barrier(v.astype(jnp.bfloat16)).astype(jnp.float32)

@jax.custom_vjp
def low_back(v):
    return v

def low_keep(v):
    return (low(v), None)

def low_pass(kept, grad):
    return (grad,)

def back_keep(v):
    return (v, None)

def back_low(kept, grad):
    return (low(grad),)
low.defvjp(low_keep, low_pass)
low_back.defvjp(back_keep, back_low)
epsilon = 1e-05
masked_score = -1e+30
highest = lax.Precision.HIGHEST

def layer_norm(values, norm_gain, norm_bias):
    average = lax.optimization_barrier(jnp.mean(values, axis=-1, keepdims=True))
    centred = values - average
    spread = lax.optimization_barrier(jnp.mean(centred * centred, axis=-1, keepdims=True))
    return centred * lax.rsqrt(spread + epsilon) * norm_gain + norm_bias

def matmul(left, right):
    return jnp.dot(left, right, precision=highest, preferred_element_type=jnp.float32)

def gelu_tanh(values):
    return jax.nn.gelu(values, approximate=True)

def page_allowed(lengths):
    positions = jnp.arange(SEQ, dtype=jnp.int32)
    page_ends = jnp.cumsum(lengths, dtype=jnp.int32)
    page_index = lax.optimization_barrier(jnp.sum((page_ends[None, :] <= positions[:, None]).astype(jnp.int32), axis=1, dtype=jnp.int32))
    same_page = page_index[:, None] == page_index[None, :]
    return jnp.concatenate([same_page, same_page], axis=1)

def attend(pieces):
    queries, own_pairs, other_pairs, allowed = pieces
    key_rows = jnp.concatenate([own_pairs[:, :D], other_pairs[:, :D]], axis=0).reshape(2 * SEQ, HEADS, HEAD_DIM)
    value_rows = jnp.concatenate([own_pairs[:, D:], other_pairs[:, D:]], axis=0).reshape(2 * SEQ, HEADS, HEAD_DIM)
    scores = jnp.einsum('qhd,khd->hqk', queries.reshape(SEQ, HEADS, HEAD_DIM), key_rows, precision=highest) * HEAD_DIM ** (-0.5)
    scores = jnp.where(allowed[None], low_back(scores), masked_score)
    largest = lax.optimization_barrier(jnp.max(scores, axis=-1, keepdims=True))
    exponent = jnp.exp(scores - largest)
    shares = exponent / lax.optimization_barrier(jnp.sum(exponent, axis=-1, keepdims=True))
    context = jnp.einsum('hqk,khd->qhd', low(shares), value_rows, precision=highest)
    return low(low_back(context.reshape(SEQ, D)))

def modal_forward(modal_rows, params, allowed):
    rounded = tuple((low(member).reshape((2, member.shape[0] // 2) + member.shape[1:]) for member in params))
    w_qkv, w_out, w_up, w_down, first_gain, first_bias, second_gain, second_bias, hidden_bias, output_bias, gate_self, gate_cross = rounded
    block_rows = modal_rows.shape[1]
    pack_count = block_rows // SEQ
    projected = []
    for modality in range(2):
        normed = low(layer_norm(modal_rows[modality], first_gain[modality], first_bias[modality]))
        projected.append(low(low_back(matmul(normed, w_qkv[modality]))))
    outputs = []
    for modality in range(2):
        partner = 1 - modality
        queries = projected[modality][:, :D].reshape(pack_count, SEQ, D)
        own_pairs = projected[modality][:, D:].reshape(pack_count, SEQ, 2 * D)
        other_pairs = projected[partner][:, D:].reshape(pack_count, SEQ, 2 * D)
        context = lax.map(jax.checkpoint(attend), (queries, own_pairs, other_pairs, allowed)).reshape(block_rows, D)
        middle = modal_rows[modality] + low_back(matmul(context, w_out[modality]))
        normed = low(layer_norm(middle, second_gain[modality], second_bias[modality]))
        upper_in = low_back(matmul(normed, w_up[modality])) + hidden_bias[modality]
        hidden = low(gelu_tanh(upper_in))
        branch = low_back(matmul(hidden, w_down[modality])) + output_bias[modality]
        outputs.append(low(middle + branch))
    mixed = []
    for modality in range(2):
        own_rows = outputs[modality]
        other_rows = outputs[1 - modality]
        logits = lax.optimization_barrier(jnp.sum(own_rows * gate_self[modality], axis=-1)) + lax.optimization_barrier(jnp.sum(other_rows * gate_cross[modality], axis=-1))
        gate_rows = jax.nn.sigmoid(logits)[:, None]
        mixed.append(own_rows + gate_rows * other_rows)
    return jnp.stack(mixed)

def reference(regions, cotangent, page_lens, qkv_weight, out_weight, up_weight, down_weight, ln1_gain, ln1_bias, ln2_gain, ln2_bias, up_bias, down_bias, gate_own, gate_other):
    params = (qkv_weight, out_weight, up_weight, down_weight, ln1_gain, ln1_bias, ln2_gain, ln2_bias, up_bias, down_bias, gate_own, gate_other)
    group_packs = math.gcd(PACKS, 8)
    block_count = PACKS // group_packs
    block_rows = group_packs * SEQ

    def by_blocks(stacked):
        return stacked.astype(jnp.float32).reshape(2, block_count, block_rows, D).transpose(1, 0, 2, 3)
    lens_blocks = page_lens.reshape(block_count, group_packs, PAGES)

    def one_block(totals, pieces):
        modal_rows, tangent_rows, lengths = pieces
        allowed = jax.vmap(page_allowed)(lengths)

        def forward(rows_in, weights):
            return modal_forward(rows_in, weights, allowed)
        mixed, pullback = jax.vjp(forward, modal_rows, params)
        row_grad, param_grad = pullback(tangent_rows)
        return (jax.tree.map(jnp.add, totals, param_grad), (mixed.astype(jnp.bfloat16), row_grad))
    starting = jax.tree.map(jnp.zeros_like, params)
    totals, (mixed, row_grad) = lax.scan(one_block, starting, (by_blocks(regions), by_blocks(cotangent), lens_blocks))

    def unblock(blocked):
        return blocked.transpose(1, 0, 2, 3).reshape(2 * TOKENS, D)
    return (unblock(mixed), unblock(row_grad), totals[0], totals[1], totals[2], totals[3], totals[4], totals[5], totals[6], totals[7], totals[8], totals[9], totals[10], totals[11])
```

```python
import functools
import math

import jax
import jax.numpy as jnp
from jax import lax
from jax.experimental import pallas as pl
from jax.experimental.pallas import tpu as pltpu
from jax.sharding import PartitionSpec as P

D = 768
HEADS = 12
HEAD_DIM = 64
FF = 3072
SEQ = 512
GROUPS = 3
WIDE = D // GROUPS
PAIR = 2 * HEAD_DIM
BLOCK = 128
REACH = 96
ROWS = 256
MIB = 1024 * 1024

epsilon = 1e-05
masked_score = -1e30
score_scale = HEAD_DIM ** (-0.5)
gelu_scale = math.sqrt(2.0 / math.pi)
gelu_cubic = 0.044715

f32 = jnp.float32
bf16 = jnp.bfloat16

WINDOWS = [
    (max(0, start - REACH), min(SEQ, start + BLOCK + REACH)) for start in range(0, SEQ, BLOCK)
]
WINDOW = BLOCK + 2 * REACH

in_smem = pl.BlockSpec(memory_space=pltpu.SMEM)
in_vmem = pl.BlockSpec(memory_space=pltpu.VMEM)
in_any = pl.BlockSpec(memory_space=pl.ANY)


def shape_of(dims, dtype):
    return jax.ShapeDtypeStruct(dims, dtype)


def params(limit):
    return pltpu.CompilerParams(vmem_limit_bytes=limit * MIB)


def dot(left, right):
    return lax.dot_general(left, right, (((1,), (0,)), ((), ())), preferred_element_type=f32)


def dot_nt(left, right):
    return lax.dot_general(left, right, (((1,), (1,)), ((), ())), preferred_element_type=f32)


def dot_tn(left, right):
    return lax.dot_general(left, right, (((0,), (0,)), ((), ())), preferred_element_type=f32)


def normalise(values):
    average = jnp.mean(values, axis=-1, keepdims=True)
    centred = values - average
    spread = jnp.mean(centred * centred, axis=-1, keepdims=True)
    root = lax.rsqrt(spread + epsilon)
    return centred * root, root


def norm_back(scaled, root, gain, incoming):
    weighted = incoming * gain
    average = jnp.mean(weighted, axis=-1, keepdims=True)
    slope = jnp.mean(weighted * scaled, axis=-1, keepdims=True)
    return root * (weighted - average - scaled * slope)


def column_sums(values):
    return jnp.sum(values, axis=0, keepdims=True)


def part_copies(places, parts, whole, sems):
    rows = whole.shape[0] // len(parts)
    return [
        pltpu.make_async_copy(
            part.at[pl.ds(0, rows)],
            whole.at[pl.ds(pl.multiple_of(places[k] * rows, 16), rows)],
            sems.at[k],
        )
        for k, part in enumerate(parts)
    ]


def start_all(copies):
    for copy in copies:
        copy.start()


def wait_all(copies):
    for copy in copies:
        copy.wait()


def project_kernel(count, places, rows, gain, bias, *rest):
    parts = rest[:count]
    query_out, pair_outs, normed_out = rest[count], rest[count + 1 : count + 4], rest[count + 4]
    weight, sems = rest[count + 5 :]
    copies = part_copies(places, parts, weight, sems)
    start_all(copies)
    scaled, _ = normalise(rows[...].astype(f32))
    normed_out[...] = (scaled * gain[...] + bias[...]).astype(bf16)
    wait_all(copies)
    normed = normed_out[...]

    def block(column):
        return dot(normed, weight[:, column : column + WIDE]).astype(bf16)

    for group in range(GROUPS):
        first = group * WIDE
        pair_outs[group][0] = block(D + first)
        pair_outs[group][1] = block(2 * D + first)
    for group in range(GROUPS):
        first = group * WIDE
        query_out[:, first : first + WIDE] = block(first)


def project(places, rows, gain, bias, parts):
    count = len(parts)
    outs = pl.pallas_call(
        functools.partial(project_kernel, count),
        out_shape=[shape_of((SEQ, D), bf16)]
        + [shape_of((2, SEQ, WIDE), bf16)] * GROUPS
        + [shape_of((SEQ, D), bf16)],
        in_specs=[in_smem] + [in_vmem] * 3 + [in_any] * count,
        out_specs=[in_vmem] * (GROUPS + 2),
        scratch_shapes=[pltpu.VMEM((D, 3 * D), bf16), pltpu.SemaphoreType.DMA((count,))],
        compiler_params=params(24),
        cost_estimate=pl.CostEstimate(
            flops=2 * SEQ * D * 3 * D, bytes_accessed=7 * MIB, transcendentals=0
        ),
        name="project",
    )(places, rows, gain, bias, *parts)
    return outs[0], outs[1:4], outs[4]


def fill_page_bias(page_row, page_column, bias):
    for index, (low, high) in enumerate(WINDOWS):
        start = index * BLOCK
        same = page_column[low:high] == page_row[:, start : start + BLOCK]
        bias[index, : high - low] = jnp.where(same, 0.0, masked_score)


def two_heads(block):
    lane = lax.broadcasted_iota(jnp.int32, block.shape, 1)
    zero = jnp.zeros_like(block)
    return jnp.concatenate(
        [jnp.where(lane < HEAD_DIM, block, zero), jnp.where(lane < HEAD_DIM, zero, block)], axis=0
    )


def head_rows(both):
    return jnp.concatenate([both[:HEAD_DIM, :BLOCK], both[HEAD_DIM:, BLOCK:]], axis=0).T


def page_bias(bias, index, size):
    block = bias[index, :size]
    return jnp.concatenate([block, block], axis=1)


def attend_kernel(
    query, key, value, key_two, value_two, page_row, page_column, context, log_total, bias
):
    @pl.when(pl.program_id(0) == 0)
    def _():
        fill_page_bias(page_row, page_column, bias)

    for index, (low, high) in enumerate(WINDOWS):
        start = index * BLOCK
        queries = two_heads(query[start : start + BLOCK] * score_scale)
        allowed = page_bias(bias, index, high - low)
        scores = dot_nt(key[0, low:high], queries) + allowed
        scores_two = dot_nt(key_two[0, low:high], queries) + allowed
        largest = jnp.maximum(
            jnp.max(scores, axis=0, keepdims=True), jnp.max(scores_two, axis=0, keepdims=True)
        )
        exponent = jnp.exp(scores - largest)
        exponent_two = jnp.exp(scores_two - largest)
        total = column_sums(exponent) + column_sums(exponent_two)
        inverse = 1.0 / total
        shares = (exponent * inverse).astype(bf16)
        shares_two = (exponent_two * inverse).astype(bf16)
        both = dot_tn(value[0, low:high], shares) + dot_tn(value_two[0, low:high], shares_two)
        context[start : start + BLOCK] = head_rows(both).astype(bf16)
        log_row = largest + jnp.log(total)
        log_total[0, 0:1, start : start + BLOCK] = log_row[:, :BLOCK]
        log_total[0, 1:2, start : start + BLOCK] = log_row[:, BLOCK:]


def attention_specs(group):
    steps = WIDE // PAIR
    wide_query = pl.BlockSpec((SEQ, PAIR), lambda step: (0, steps * group + step))
    key = pl.BlockSpec((1, SEQ, PAIR), lambda step: (0, 0, step))
    value = pl.BlockSpec((1, SEQ, PAIR), lambda step: (1, 0, step))
    page_row = pl.BlockSpec((1, SEQ), lambda step: (0, 0))
    page_column = pl.BlockSpec((SEQ, 1), lambda step: (0, 0))
    narrow = pl.BlockSpec((SEQ, PAIR), lambda step: (0, step))
    logs = pl.BlockSpec((1, 2, SEQ), lambda step: (step, 0, 0))
    return wide_query, key, value, page_row, page_column, narrow, logs


def attend(group, queries, own, other, page_row, page_column):
    steps = WIDE // PAIR
    wide_query, key, value, row_spec, column_spec, narrow, logs = attention_specs(group)
    return pl.pallas_call(
        attend_kernel,
        grid=(steps,),
        out_shape=[shape_of((SEQ, WIDE), bf16), shape_of((steps, 2, SEQ), f32)],
        in_specs=[wide_query, key, value, key, value, row_spec, column_spec],
        out_specs=[narrow, logs],
        scratch_shapes=[pltpu.VMEM((len(WINDOWS), WINDOW, BLOCK), f32)],
        compiler_params=params(24),
        cost_estimate=pl.CostEstimate(
            flops=4 * SEQ * SEQ * WIDE, bytes_accessed=2 * MIB, transcendentals=SEQ * SEQ
        ),
        name="attend",
    )(queries, own, own, other, other, page_row, page_column)


def attend_back_kernel(
    query,
    key,
    value,
    key_two,
    value_two,
    context_grad,
    log_total,
    page_row,
    page_column,
    query_grad,
    own_grad,
    other_grad,
    bias,
    other_sum,
):
    @pl.when(pl.program_id(0) == 0)
    def _():
        fill_page_bias(page_row, page_column, bias)

    own_grad[...] = jnp.zeros_like(own_grad)
    other_sum[...] = jnp.zeros_like(other_sum)
    for index, (low, high) in enumerate(WINDOWS):
        start = index * BLOCK
        queries = two_heads(query[start : start + BLOCK] * score_scale)
        grads = two_heads(context_grad[start : start + BLOCK])
        log_row = jnp.concatenate(
            [
                log_total[0, 0:1, start : start + BLOCK],
                log_total[0, 1:2, start : start + BLOCK],
            ],
            axis=1,
        )
        allowed = page_bias(bias, index, high - low)
        keys, keys_two = key[0, low:high], key_two[0, low:high]
        shares = jnp.exp(dot_nt(keys, queries) + allowed - log_row)
        shares_two = jnp.exp(dot_nt(keys_two, queries) + allowed - log_row)
        share_grad = dot_nt(value[0, low:high], grads)
        share_grad_two = dot_nt(value_two[0, low:high], grads)
        centre = column_sums(shares * share_grad) + column_sums(shares_two * share_grad_two)
        score_grad = (shares * (share_grad - centre)).astype(bf16)
        score_grad_two = (shares_two * (share_grad_two - centre)).astype(bf16)
        own_grad[0, low:high] += dot(score_grad, queries)
        own_grad[1, low:high] += dot(shares.astype(bf16), grads)
        other_sum[0, low:high] += dot(score_grad_two, queries)
        other_sum[1, low:high] += dot(shares_two.astype(bf16), grads)
        both = dot_tn(keys, score_grad) + dot_tn(keys_two, score_grad_two)
        query_grad[start : start + BLOCK] = (head_rows(both) * score_scale).astype(bf16)
    other_grad[...] = other_sum[...].astype(bf16)


def attend_back(group, queries, own, other, context_grad, log_total, page_row, page_column):
    steps = WIDE // PAIR
    wide_query, key, value, row_spec, column_spec, narrow, logs = attention_specs(group)
    pair = pl.BlockSpec((2, SEQ, PAIR), lambda step: (0, 0, step))
    return pl.pallas_call(
        attend_back_kernel,
        grid=(steps,),
        out_shape=[
            shape_of((SEQ, WIDE), bf16),
            shape_of((2, SEQ, WIDE), f32),
            shape_of((2, SEQ, WIDE), bf16),
        ],
        in_specs=[wide_query, key, value, key, value, wide_query, logs, row_spec, column_spec],
        out_specs=[narrow, pair, pair],
        scratch_shapes=[
            pltpu.VMEM((len(WINDOWS), WINDOW, BLOCK), f32),
            pltpu.VMEM((2, SEQ, PAIR), f32),
        ],
        compiler_params=params(24),
        cost_estimate=pl.CostEstimate(
            flops=10 * SEQ * SEQ * WIDE, bytes_accessed=4 * MIB, transcendentals=SEQ * SEQ
        ),
        name="attend_back",
    )(queries, own, own, other, other, context_grad, log_total, page_row, page_column)


def middle_kernel(count, places, rows, contexts, partner_tangent, vectors, hidden_bias, *rest):
    out_parts, up_parts, down_parts = (rest[k * count : (k + 1) * count] for k in range(3))
    middle_out, second_out, hidden_out, slope_out, modal_out, inner_out = rest[3 * count : 3 * count + 6]
    w_out, w_up, w_down, sems = rest[3 * count + 6 :]
    out_copies = part_copies(places, out_parts, w_out, sems.at[0])
    up_copies = part_copies(places, up_parts, w_up, sems.at[1])
    down_copies = part_copies(places, down_parts, w_down, sems.at[2])
    first_step = pl.program_id(0) == 0

    @pl.when(first_step)
    def _():
        start_all(out_copies)
        start_all(up_copies)
        start_all(down_copies)
        wait_all(out_copies)

    middle = rows[...].astype(f32)
    for group in range(GROUPS):
        middle += dot(contexts[group], w_out[group * WIDE : (group + 1) * WIDE])
    middle_out[...] = middle
    scaled, _ = normalise(middle)
    second = (scaled * vectors[0:1] + vectors[1:2]).astype(bf16)
    second_out[...] = second

    @pl.when(first_step)
    def _():
        wait_all(up_copies)
        wait_all(down_copies)

    branch = jnp.zeros((ROWS, D), f32) + vectors[2:3]
    size = 512
    for first in range(0, FF, size):
        part = slice(first, first + size)
        upper = dot(second, w_up[:, part]) + hidden_bias[:, part]
        square = upper * upper
        angle = jnp.tanh(gelu_scale * (upper + gelu_cubic * (square * upper)))
        half = 0.5 * (1.0 + angle)
        hidden = (upper * half).astype(bf16)
        hidden_out[:, part] = hidden
        bend = gelu_scale + (3.0 * gelu_cubic * gelu_scale) * square
        slope_out[:, part] = (half + 0.5 * upper * (1.0 - angle * angle) * bend).astype(bf16)
        branch += dot(hidden, w_down[part])
    modal = (middle + branch).astype(bf16)
    modal_out[...] = modal
    modal = modal.astype(f32)
    own = jnp.sum(modal * vectors[3:4], axis=1, keepdims=True)
    cross = jnp.sum(modal * vectors[4:5], axis=1, keepdims=True)
    met = jnp.sum(modal * partner_tangent[...].astype(f32), axis=1, keepdims=True)
    lane = lax.broadcasted_iota(jnp.int32, (ROWS, 128), 1)
    columns = jnp.where(lane == 0, own, jnp.where(lane == 1, cross, met))
    inner_out[...] = columns.T[:8]


def middle_pass(places, rows, contexts, partner_tangent, vectors, hidden_bias, outs, ups, downs):
    count = len(outs)
    by_rows = lambda width: pl.BlockSpec((ROWS, width), lambda step: (step, 0))
    whole = lambda dims: pl.BlockSpec(dims, lambda step: (0, 0))

    def kernel(places_ref, rows_ref, c0, c1, c2, *rest):
        middle_kernel(count, places_ref, rows_ref, (c0[...], c1[...], c2[...]), *rest)

    return pl.pallas_call(
        kernel,
        grid=(SEQ // ROWS,),
        out_shape=[
            shape_of((SEQ, D), f32),
            shape_of((SEQ, D), bf16),
            shape_of((SEQ, FF), bf16),
            shape_of((SEQ, FF), bf16),
            shape_of((SEQ, D), bf16),
            shape_of((8, SEQ), f32),
        ],
        in_specs=[in_smem, by_rows(D)]
        + [by_rows(WIDE)] * GROUPS
        + [by_rows(D), whole((8, D)), whole((1, FF))]
        + [in_any] * (3 * count),
        out_specs=[
            by_rows(D),
            by_rows(D),
            by_rows(FF),
            by_rows(FF),
            by_rows(D),
            pl.BlockSpec((8, ROWS), lambda step: (0, step)),
        ],
        scratch_shapes=[
            pltpu.VMEM((D, D), bf16),
            pltpu.VMEM((D, FF), bf16),
            pltpu.VMEM((FF, D), bf16),
            pltpu.SemaphoreType.DMA((3, count)),
        ],
        compiler_params=params(44),
        cost_estimate=pl.CostEstimate(
            flops=2 * SEQ * D * (D + 2 * FF), bytes_accessed=21 * MIB, transcendentals=SEQ * FF
        ),
        name="middle",
    )(places, rows, *contexts, partner_tangent, vectors, hidden_bias, *outs, *ups, *downs)


def gate_kernel(own, other, tangent, partner_tangent, vectors, grad_out, low_out, columns_out, sums):
    gate = jax.nn.sigmoid(own[0:1] + other[1:2])
    gate_two = jax.nn.sigmoid(other[0:1] + own[1:2])
    logit = other[2:3] * gate * (1.0 - gate)
    logit_two = own[2:3] * gate_two * (1.0 - gate_two)
    padding = jnp.zeros((124, SEQ), f32)
    columns = jnp.concatenate([gate, logit, gate_two, logit_two, padding], axis=0).T
    columns_out[...] = columns
    grad = (
        tangent[...].astype(f32)
        + columns[:, 1:2] * vectors[3:4]
        + partner_tangent[...].astype(f32) * columns[:, 2:3]
        + columns[:, 3:4] * vectors[4:5]
    )
    grad_out[...] = grad
    low_out[...] = grad.astype(bf16)
    sums[...] = column_sums(grad)


def gate_pass(own, other, tangent, partner_tangent, vectors):
    return pl.pallas_call(
        gate_kernel,
        out_shape=[
            shape_of((SEQ, D), f32),
            shape_of((SEQ, D), bf16),
            shape_of((SEQ, 128), f32),
            shape_of((1, D), f32),
        ],
        in_specs=[in_vmem] * 5,
        out_specs=[in_vmem] * 4,
        compiler_params=params(24),
        cost_estimate=pl.CostEstimate(
            flops=8 * SEQ * D, bytes_accessed=5 * MIB, transcendentals=2 * SEQ
        ),
        name="gate",
    )(own, other, tangent, partner_tangent, vectors)


def mix_kernel(own, other, columns, mixed, own_sums, other_sums):
    own_rows = own[...].astype(f32)
    other_rows = other[...].astype(f32)
    mixed[...] = (own_rows + columns[:, 0:1] * other_rows).astype(bf16)
    own_sums[...] = column_sums(columns[:, 1:2] * own_rows)
    other_sums[...] = column_sums(columns[:, 1:2] * other_rows)


def mix_pass(own, other, columns):
    return pl.pallas_call(
        mix_kernel,
        out_shape=[shape_of((SEQ, D), bf16), shape_of((1, D), f32), shape_of((1, D), f32)],
        in_specs=[in_vmem] * 3,
        out_specs=[in_vmem] * 3,
        compiler_params=params(24),
        cost_estimate=pl.CostEstimate(
            flops=6 * SEQ * D, bytes_accessed=3 * MIB, transcendentals=0
        ),
        name="mix",
    )(own, other, columns)


def chain_kernel(count, places, low, grad, slope, middle, gain, *rest):
    out_parts, up_parts, down_parts = (rest[k * count : (k + 1) * count] for k in range(3))
    upper_out, total_out, total_low_out, context_out, upper_sums, gain_sums, bias_sums = rest[
        3 * count : 3 * count + 7
    ]
    w_out, w_up, w_down, sems = rest[3 * count + 7 :]
    out_copies = part_copies(places, out_parts, w_out, sems.at[0])
    up_copies = part_copies(places, up_parts, w_up, sems.at[1])
    down_copies = part_copies(places, down_parts, w_down, sems.at[2])
    first_step = pl.program_id(0) == 0

    @pl.when(first_step)
    def _():
        start_all(down_copies)
        start_all(up_copies)
        start_all(out_copies)
        upper_sums[...] = jnp.zeros_like(upper_sums)
        gain_sums[...] = jnp.zeros_like(gain_sums)
        bias_sums[...] = jnp.zeros_like(bias_sums)
        wait_all(down_copies)
        wait_all(up_copies)

    incoming = low[...]
    normed_grad = jnp.zeros((ROWS, D), f32)
    size = 512
    for first in range(0, FF, size):
        part = slice(first, first + size)
        upper = dot_nt(incoming, w_down[part]) * slope[:, part].astype(f32)
        upper_sums[:, part] += column_sums(upper)
        upper_low = upper.astype(bf16)
        upper_out[:, part] = upper_low
        normed_grad += dot_nt(upper_low, w_up[:, part])
    scaled, root = normalise(middle[...])
    gain_sums[...] += column_sums(normed_grad * scaled)
    bias_sums[...] += column_sums(normed_grad)
    total = grad[...] + norm_back(scaled, root, gain[...], normed_grad)
    total_out[...] = total
    total_low = total.astype(bf16)
    total_low_out[...] = total_low

    @pl.when(first_step)
    def _():
        wait_all(out_copies)

    context_out[...] = dot_nt(total_low, w_out[...]).astype(bf16)


def chain_pass(places, low, grad, slope, middle, gain, outs, ups, downs):
    count = len(outs)
    by_rows = lambda width: pl.BlockSpec((ROWS, width), lambda step: (step, 0))
    whole = lambda dims: pl.BlockSpec(dims, lambda step: (0, 0))
    return pl.pallas_call(
        functools.partial(chain_kernel, count),
        grid=(SEQ // ROWS,),
        out_shape=[
            shape_of((SEQ, FF), bf16),
            shape_of((SEQ, D), f32),
            shape_of((SEQ, D), bf16),
            shape_of((SEQ, D), bf16),
            shape_of((1, FF), f32),
            shape_of((1, D), f32),
            shape_of((1, D), f32),
        ],
        in_specs=[in_smem, by_rows(D), by_rows(D), by_rows(FF), by_rows(D), whole((1, D))]
        + [in_any] * (3 * count),
        out_specs=[by_rows(FF), by_rows(D), by_rows(D), by_rows(D)]
        + [whole((1, FF)), whole((1, D)), whole((1, D))],
        scratch_shapes=[
            pltpu.VMEM((D, D), bf16),
            pltpu.VMEM((D, FF), bf16),
            pltpu.VMEM((FF, D), bf16),
            pltpu.SemaphoreType.DMA((3, count)),
        ],
        compiler_params=params(44),
        cost_estimate=pl.CostEstimate(
            flops=2 * SEQ * D * (D + 2 * FF), bytes_accessed=21 * MIB, transcendentals=0
        ),
        name="chain",
    )(places, low, grad, slope, middle, gain, *outs, *ups, *downs)


def slots_of(count):
    return (list(range(0, count, 2)), list(range(1, count, 2)))


def row_grads_kernel(count, widths, summed, places, left, *rest):
    sources = rest[: 2 if summed else 1]
    rest = rest[len(sources) :]
    if summed:
        pair_low = rest[0]
        rest = rest[1:]
    outs, whole = rest[:-1], rest[-1]
    near, far = slots_of(count)
    rows = D // count
    turned = left[...].T
    first = 0
    each = 2 if far else 1
    if summed:
        total = (sources[0][...] + sources[1][...].astype(f32)).astype(bf16)
        pair_low[...] = total
    for index, width in enumerate(widths):
        for low in range(first, first + width, WIDE):
            if summed:
                right = pair_low[low // WIDE]
            else:
                right = sources[0][:, low : low + WIDE]
            whole[:, low - first : low - first + WIDE] = dot(turned, right).astype(bf16)
        for out, slots in zip(outs[each * index : each * index + each], (near, far)):
            for place, slot in enumerate(slots):
                begin = pl.multiple_of(places[slot] * rows, 16)
                out[place] = whole[pl.ds(begin, rows), :width]
        first += width


def row_grads(places, left, sources, widths, count):
    near, far = slots_of(count)
    rows = D // count
    outs = []
    for width in widths:
        outs.append(shape_of((len(near), rows, width), bf16))
        if far:
            outs.append(shape_of((len(far), rows, width), bf16))
    summed = len(sources) == 2
    low = [shape_of((2, SEQ, WIDE), bf16)] if summed else []
    total = sum(widths)
    return pl.pallas_call(
        functools.partial(row_grads_kernel, count, widths, summed),
        out_shape=low + outs,
        in_specs=[in_smem] + [in_vmem] * (1 + len(sources)),
        out_specs=[in_vmem] * len(low + outs),
        scratch_shapes=[pltpu.VMEM((D, max(widths)), bf16)],
        compiler_params=params(32),
        cost_estimate=pl.CostEstimate(
            flops=2 * SEQ * D * total, bytes_accessed=2 * D * total + 2 * MIB, transcendentals=0
        ),
        name="row_grads",
    )(places, left, *sources)


def down_grads_kernel(count, heights, places, low, hidden, *outs):
    near, far = slots_of(count)
    width = FF // count
    each = 2 if far else 1
    first = 0
    for index, height in enumerate(heights):
        turned = low[:, first : first + height].T
        for out, slots in zip(outs[each * index : each * index + each], (near, far)):
            for place, slot in enumerate(slots):
                begin = pl.multiple_of(places[slot] * width, 128)
                out[place] = dot(turned, hidden[:, pl.ds(begin, width)]).astype(bf16)
        first += height


def down_grads(places, low, hidden, heights, count):
    near, far = slots_of(count)
    width = FF // count
    outs = []
    for height in heights:
        outs.append(shape_of((len(near), height, width), bf16))
        if far:
            outs.append(shape_of((len(far), height, width), bf16))
    return pl.pallas_call(
        functools.partial(down_grads_kernel, count, heights),
        out_shape=outs,
        in_specs=[in_smem] + [in_vmem] * 2,
        out_specs=[in_vmem] * len(outs),
        compiler_params=params(32),
        cost_estimate=pl.CostEstimate(
            flops=2 * SEQ * D * FF, bytes_accessed=9 * MIB, transcendentals=0
        ),
        name="down_grads",
    )(places, low, hidden)


def first_kernel(count, places, queries, pairs, total, rows, gain, *rest):
    parts = rest[:count]
    grad_out, gain_sums, bias_sums, weight, sems = rest[count:]
    copies = part_copies(places, parts, weight, sems)

    @pl.when(pl.program_id(0) == 0)
    def _():
        start_all(copies)
        gain_sums[...] = jnp.zeros_like(gain_sums)
        bias_sums[...] = jnp.zeros_like(bias_sums)
        wait_all(copies)

    normed_grad = jnp.zeros((ROWS, D), f32)
    for group in range(GROUPS):
        first = group * WIDE
        normed_grad += dot_nt(queries[group][...], weight[:, first : first + WIDE])
        for kind in range(2):
            start = (kind + 1) * D + first
            normed_grad += dot_nt(pairs[group][kind], weight[:, start : start + WIDE])
    scaled, root = normalise(rows[...].astype(f32))
    gain_sums[...] += column_sums(normed_grad * scaled)
    bias_sums[...] += column_sums(normed_grad)
    grad_out[...] = total[...] + norm_back(scaled, root, gain[...], normed_grad)


def first_pass(places, queries, pairs, total, rows, gain, parts):
    count = len(parts)
    by_rows = lambda width: pl.BlockSpec((ROWS, width), lambda step: (step, 0))
    whole = lambda dims: pl.BlockSpec(dims, lambda step: (0, 0))
    pair = pl.BlockSpec((2, ROWS, WIDE), lambda step: (0, step, 0))

    def kernel(places_ref, q0, q1, q2, p0, p1, p2, *rest):
        first_kernel(count, places_ref, (q0, q1, q2), (p0, p1, p2), *rest)

    return pl.pallas_call(
        kernel,
        grid=(SEQ // ROWS,),
        out_shape=[shape_of((SEQ, D), f32), shape_of((1, D), f32), shape_of((1, D), f32)],
        in_specs=[in_smem]
        + [by_rows(WIDE)] * GROUPS
        + [pair] * GROUPS
        + [by_rows(D), by_rows(D), whole((1, D))]
        + [in_any] * count,
        out_specs=[by_rows(D), whole((1, D)), whole((1, D))],
        scratch_shapes=[pltpu.VMEM((D, 3 * D), bf16), pltpu.SemaphoreType.DMA((count,))],
        compiler_params=params(24),
        cost_estimate=pl.CostEstimate(
            flops=2 * SEQ * D * 3 * D, bytes_accessed=10 * MIB, transcendentals=0
        ),
        name="first",
    )(places, *queries, *pairs, total, rows, gain, *parts)


def swap_bit(value, axis, bit):
    size = lax.axis_size(axis)
    return lax.ppermute(value, axis, [(source, source ^ (1 << bit)) for source in range(size)])


def from_partner(value):
    size = lax.axis_size("stream")
    half = size // 2
    return lax.ppermute(value, "stream", [(source, (source + half) % size) for source in range(size)])


def add_low(left, right):
    return (left.astype(f32) + right.astype(f32)).astype(left.dtype)


def line_sum(value, inner):
    received = lax.ppermute(value, "dp", [(0, 1), (3, 2)])
    near = add_low(value, received)
    across = lax.ppermute(near, "dp", [(1, 2), (2, 1)])
    total = add_low(near, across)
    returned = lax.ppermute(total, "dp", [(1, 0), (2, 3)])
    return jnp.where(inner, total, returned)


def modality_groups():
    size = lax.axis_size("stream")
    half = size // 2
    return [list(range(half)), list(range(half, size))]


def body(
    regions,
    cotangent,
    page_lens,
    qkv_weight,
    out_weight,
    up_weight,
    down_weight,
    ln1_gain,
    ln1_bias,
    ln2_gain,
    ln2_bias,
    up_bias,
    down_bias,
    gate_own,
    gate_other,
):
    half = lax.axis_size("stream") // 2
    depth = lax.axis_size("dp")
    paired = half == 4 and depth == 4
    side = lax.axis_index("stream") % half
    floor = lax.axis_index("dp")
    inner = jnp.logical_and(floor > 0, floor < depth - 1)
    count = 4 if paired else 1
    slots = jnp.arange(count, dtype=jnp.int32)
    places = jnp.bitwise_xor(side.astype(jnp.int32), slots) if paired else slots

    def gather(shard):
        if not paired:
            return [
                lax.all_gather(shard, "stream", axis_index_groups=modality_groups(), tiled=True)
            ]
        across = swap_bit(shard, "stream", 1)
        return [shard, swap_bit(shard, "stream", 0), across, swap_bit(across, "stream", 0)]

    short = (ln1_gain, ln1_bias, ln2_gain, ln2_bias, down_bias, gate_own, gate_other, up_bias)
    packed = jnp.concatenate([member.astype(bf16) for member in short])[None]
    qkv_low = qkv_weight.astype(bf16)
    if paired:
        padded = jnp.pad(packed, ((0, 15), (0, 3 * D - packed.shape[1])))
        qkv_parts = gather(jnp.concatenate([qkv_low, padded], axis=0))
        rows_qkv = qkv_low.shape[0]
        found = jnp.stack([part[rows_qkv, : packed.shape[1]] for part in qkv_parts]).astype(f32)
        picks = places[None, :] == slots[:, None]
        found = jnp.sum(jnp.where(picks[:, :, None], found[None], 0.0), axis=1)
    else:
        qkv_parts = gather(qkv_low)
        found = gather(packed)[0].astype(f32)
    partner_tangent = from_partner(cotangent)
    out_parts = gather(out_weight.astype(bf16))
    up_parts = gather(up_weight.astype(bf16))
    down_parts = gather(down_weight.astype(bf16))
    vectors = []
    offset = 0
    for member in short:
        vectors.append(found[:, offset : offset + member.size].reshape(1, -1))
        offset += member.size
    gain_one, bias_one, gain_two, bias_two, output_bias, gate_self, gate_cross, hidden_bias = vectors
    partner_cross = from_partner(gate_cross.astype(bf16)).astype(f32)
    middle_vectors = jnp.concatenate(
        [gain_two, bias_two, output_bias, gate_self, partner_cross, jnp.zeros((3, D), f32)], axis=0
    )

    lengths = lax.dynamic_slice_in_dim(page_lens, side * depth + floor, 1, 0)
    positions = jnp.arange(SEQ, dtype=jnp.int32)
    page_ends = jnp.cumsum(lengths[0], dtype=jnp.int32)
    pages = jnp.sum((page_ends[:, None] <= positions[None, :]).astype(jnp.int32), axis=0)
    page_row, page_column = pages[None, :], pages[:, None]

    queries, own_pairs, normed = project(places, regions, gain_one, bias_one, qkv_parts)
    other_pairs = [from_partner(pair) for pair in own_pairs]
    contexts, logs = [], []
    for group in range(GROUPS):
        context, log_total = attend(
            group, queries, own_pairs[group], other_pairs[group], page_row, page_column
        )
        contexts.append(context)
        logs.append(log_total)
    middle, second, hidden, slope, modal, inner_own = middle_pass(
        places,
        regions,
        contexts,
        partner_tangent,
        middle_vectors,
        hidden_bias,
        out_parts,
        up_parts,
        down_parts,
    )
    inner_other = from_partner(inner_own)
    modal_grad, modal_low, columns, output_bias_grad = gate_pass(
        inner_own, inner_other, cotangent, partner_tangent, middle_vectors
    )
    partner_modal = from_partner(modal)
    mixed_rows, gate_self_grad, gate_cross_grad = mix_pass(modal, partner_modal, columns)

    def settle(near, far=None):
        if far is None:
            return near
        received = swap_bit(far, "stream", 0)
        away = add_low(near[1], received[1])
        across = swap_bit(away, "stream", 1)
        mine = add_low(add_low(near[0], received[0]), across)
        return line_sum(mine, inner)

    def settle_all(flat):
        each = 2 if paired else 1
        return [settle(*flat[k : k + each]) for k in range(0, len(flat), each)]

    heights = [384, 384] if paired else [D]
    down_sums = settle_all(down_grads(places, modal_low, hidden, heights, count))
    upper_low, middle_grad, middle_low, context_grad, hidden_bias_grad, gain_two_grad, bias_two_grad = (
        chain_pass(
            places,
            modal_low,
            modal_grad,
            slope,
            middle,
            gain_two,
            out_parts,
            up_parts,
            down_parts,
        )
    )
    widths = [FF // 2, FF // 2] if paired else [FF]
    up_sums = settle_all(row_grads(places, second, [upper_low], widths, count))
    context_all = jnp.concatenate(contexts, axis=1)
    out_sums = settle_all(row_grads(places, context_all, [middle_low], [D], count))
    query_grads, own_grads, returned = [], [], []
    for group in range(GROUPS):
        query_grad, own_grad, other_grad = attend_back(
            group,
            queries,
            own_pairs[group],
            other_pairs[group],
            context_grad,
            logs[group],
            page_row,
            page_column,
        )
        query_grads.append(query_grad)
        own_grads.append(own_grad)
        returned.append(from_partner(other_grad))
    query_all = jnp.concatenate(query_grads, axis=1)
    query_sums = settle_all(row_grads(places, normed, [query_all], [D], count))
    pair_grads, pair_sums = [], []
    for group in range(GROUPS):
        pair_grad, *flat = row_grads(
            places, normed, [own_grads[group], returned[group]], [2 * WIDE], count
        )
        pair_grads.append(pair_grad)
        pair_sums += settle_all(flat)
    region_grad, gain_one_grad, bias_one_grad = first_pass(
        places, query_grads, pair_grads, middle_grad, regions, gain_one, qkv_parts
    )

    short_grads = (
        gain_one_grad,
        bias_one_grad,
        gain_two_grad,
        bias_two_grad,
        output_bias_grad,
        gate_self_grad,
        gate_cross_grad,
        hidden_bias_grad,
    )
    short_sum = jnp.concatenate([member.reshape(half, -1) for member in short_grads], axis=1)
    if paired:
        short_sum = short_sum + swap_bit(short_sum, "stream", 0)
        short_sum = short_sum + swap_bit(short_sum, "stream", 1)
        short_sum = line_sum(short_sum, inner)
    else:
        short_sum = lax.psum(
            lax.psum(short_sum, "stream", axis_index_groups=modality_groups()), "dp"
        )
    short_own = lax.dynamic_slice_in_dim(short_sum, side, 1, 0)[0]
    short_outs = []
    offset = 0
    for member in short:
        short_outs.append(short_own[offset : offset + member.size])
        offset += member.size

    def finish(blocks):
        if paired:
            return blocks
        groups = modality_groups()
        return [
            lax.psum(
                lax.psum_scatter(
                    block[0].astype(f32), "stream", axis_index_groups=groups, tiled=True
                ),
                "dp",
            )
            for block in blocks
        ]

    if paired:
        down_grad = jnp.concatenate(down_sums, axis=0).T.astype(f32)
    else:
        down_grad = finish([down_sums[0].transpose(0, 2, 1)])[0]
    up_grad = jnp.concatenate(finish(up_sums), axis=1).astype(f32)
    out_grad = jnp.concatenate(finish(out_sums), axis=1).astype(f32)
    pair_sums = finish(pair_sums)
    qkv_grad = jnp.concatenate(
        finish(query_sums)
        + [block[:, :WIDE] for block in pair_sums]
        + [block[:, WIDE:] for block in pair_sums],
        axis=1,
    ).astype(f32)
    short_by = short_outs[:6]
    return (
        mixed_rows,
        region_grad,
        qkv_grad,
        out_grad,
        up_grad,
        down_grad,
        short_outs[0],
        short_outs[1],
        short_outs[2],
        short_outs[3],
        short_outs[7],
        short_outs[4],
        short_outs[5],
        short_outs[6],
    )


def solution(mesh):
    in_specs = (
        P(("stream", "dp"), None),
        P(("stream", "dp"), None),
        P(),
        P("stream", None),
        P("stream", None),
        P("stream", None),
        P("stream", None),
        P("stream"),
        P("stream"),
        P("stream"),
        P("stream"),
        P("stream"),
        P("stream"),
        P("stream"),
        P("stream"),
    )
    out_specs = (
        P(("stream", "dp"), None),
        P(("stream", "dp"), None),
        P("stream", None),
        P("stream", None),
        P("stream", None),
        P("stream", None),
        P("stream"),
        P("stream"),
        P("stream"),
        P("stream"),
        P("stream"),
        P("stream"),
        P("stream"),
        P("stream"),
    )
    return jax.shard_map(body, mesh=mesh, in_specs=in_specs, out_specs=out_specs, check_vma=False)
```

```python
import functools
import math

import jax
import jax.numpy as jnp
from jax import lax
from jax.experimental import pallas as pl
from jax.experimental.pallas import tpu as pltpu
from jax.sharding import PartitionSpec as P

D = 768
HEADS = 12
HEAD_DIM = 64
FF = 3072
SEQ = 512
GROUPS = 3
THIRD = D // GROUPS
WIDE = 512
NARROW = D - WIDE
PAIR = 2 * HEAD_DIM
BLOCK = 128
REACH = 96
ROWS = 256
MIB = 1024 * 1024

epsilon = 1e-05
masked_score = -1e30
score_scale = HEAD_DIM ** (-0.5)
gelu_scale = math.sqrt(2.0 / math.pi)
gelu_cubic = 0.044715

f32 = jnp.float32
bf16 = jnp.bfloat16

WINDOWS = [
    (max(0, start - REACH), min(SEQ, start + BLOCK + REACH)) for start in range(0, SEQ, BLOCK)
]
WINDOW = BLOCK + 2 * REACH

in_smem = pl.BlockSpec(memory_space=pltpu.SMEM)
in_vmem = pl.BlockSpec(memory_space=pltpu.VMEM)
in_any = pl.BlockSpec(memory_space=pl.ANY)


def shape_of(dims, dtype):
    return jax.ShapeDtypeStruct(dims, dtype)


def dot(left, right):
    return lax.dot_general(left, right, (((1,), (0,)), ((), ())), preferred_element_type=f32)


def dot_nt(left, right):
    return lax.dot_general(left, right, (((1,), (1,)), ((), ())), preferred_element_type=f32)


def dot_tn(left, right):
    return lax.dot_general(left, right, (((0,), (0,)), ((), ())), preferred_element_type=f32)


def normalise(values):
    average = jnp.mean(values, axis=-1, keepdims=True)
    centred = values - average
    spread = jnp.mean(centred * centred, axis=-1, keepdims=True)
    root = lax.rsqrt(spread + epsilon)
    return centred * root, root


def norm_back(scaled, root, gain, incoming):
    weighted = incoming * gain
    average = jnp.mean(weighted, axis=-1, keepdims=True)
    slope = jnp.mean(weighted * scaled, axis=-1, keepdims=True)
    return root * (weighted - average - scaled * slope)


def column_sums(values):
    return jnp.sum(values, axis=0, keepdims=True)


class Order:
    def __init__(self):
        self.token = []

    def call(
        self,
        kernel,
        args,
        in_specs,
        outs,
        out_specs,
        scratch=(),
        grid=(),
        limit=24,
        name=None,
        prefetch=None,
        waits=(),
        aliases=None,
        cost=0,
    ):
        given = len(args)
        extra = list(self.token) + list(waits)
        ahead = [] if prefetch is None else [prefetch]
        count = len(ahead)

        def wrapped(*refs):
            kernel(*refs[: count + given], *refs[count + given + len(extra) :])

        results = pl.pallas_call(
            wrapped,
            out_shape=outs,
            grid_spec=pltpu.PrefetchScalarGridSpec(
                num_scalar_prefetch=count,
                grid=grid,
                in_specs=list(in_specs) + [in_any] * len(extra),
                out_specs=out_specs,
                scratch_shapes=list(scratch),
            ),
            compiler_params=pltpu.CompilerParams(vmem_limit_bytes=limit * MIB),
            cost_estimate=pl.CostEstimate(flops=1 + cost * 10**9, bytes_accessed=1 + cost * MIB, transcendentals=cost * 10**6),
            input_output_aliases=aliases or {},
            name=name,
        )(*ahead, *args, *extra)
        self.token = [min(results, key=lambda out: out.size)]
        return results

    def hold(self, arrays, waits=()):
        return self.call(
            lambda *refs: None,
            arrays,
            [in_any] * len(arrays),
            [shape_of(array.shape, array.dtype) for array in arrays],
            [in_any] * len(arrays),
            name="hold",
            waits=waits,
            aliases={k: k for k in range(len(arrays))},
        )


def part_copies(places, parts, whole, sems, columns=None):
    rows = whole.shape[0] // len(parts)
    width = slice(None) if columns is None else columns
    return [
        pltpu.make_async_copy(
            part.at[pl.ds(0, rows), width],
            whole.at[pl.ds(pl.multiple_of(places[k] * rows, 16), rows)],
            sems.at[k],
        )
        for k, part in enumerate(parts)
    ]


def start_all(copies):
    for copy in copies:
        copy.start()


def wait_all(copies):
    for copy in copies:
        copy.wait()


def sums_pass(order, places, folds=(), adds=(), pays=(), waits=()):
    args, outs, steps = [], [], []

    def give(*arrays):
        args.extend(arrays)
        return list(range(len(args) - len(arrays), len(args)))

    def make(dims, dtype):
        outs.append(shape_of(dims, dtype))
        return len(outs) - 1

    for pairs in folds:
        rows, dtype = pairs[0][0].shape[1], pairs[0][0].dtype
        width = sum(near.shape[2] for near, _ in pairs)
        given = [give(near, received) for near, received in pairs]
        steps.append(("fold", given, [make((rows, width), dtype) for _ in range(2)]))
    for left, right in adds:
        steps.append(("add", give(left, right), [make(left.shape, left.dtype)]))
    for mine, received, older, crossed in pays:
        given = give(mine, received, older, crossed)
        steps.append(("pay", given, [make(mine.shape, mine.dtype) for _ in range(2)]))
    count = len(args)

    def kernel(places_ref, *refs):
        ins, results = refs[:count], refs[count:]
        inner = jnp.logical_and(places_ref[4] > 0, places_ref[4] < 3)
        for kind, given, made in steps:
            if kind == "fold":
                first = 0
                for near, received in given:
                    width = ins[near].shape[2]
                    for slot, out in enumerate(made):
                        total = ins[near][slot].astype(f32) + ins[received][slot].astype(f32)
                        results[out][:, first : first + width] = total.astype(results[out].dtype)
                    first += width
            elif kind == "add":
                total = ins[given[0]][...].astype(f32) + ins[given[1]][...].astype(f32)
                results[made[0]][...] = total.astype(results[made[0]].dtype)
            else:
                fresh = ins[given[0]][...].astype(f32) + ins[given[1]][...].astype(f32)
                older = ins[given[2]][...].astype(f32) + ins[given[3]][...].astype(f32)
                results[made[0]][...] = fresh.astype(results[made[0]].dtype)
                results[made[1]][...] = jnp.where(inner, older, fresh).astype(results[made[1]].dtype)

    found = order.call(
        kernel,
        [places, *args],
        [in_smem] + [in_vmem] * len(args),
        outs,
        [in_vmem] * len(outs),
        limit=40,
        name="sums",
        waits=waits,
    )
    found = list(found)
    return found[0] if len(found) == 1 else found


def cast_kernel(count, *refs):
    for source, target in zip(refs[:count], refs[count:]):
        target[...] = source[...].astype(bf16)


def cast_pass(order, arrays):
    return order.call(
        functools.partial(cast_kernel, len(arrays)),
        arrays,
        [in_vmem] * len(arrays),
        [shape_of(array.shape, bf16) for array in arrays],
        [in_vmem] * len(arrays),
        limit=32,
        name="cast",
    )


def pack_kernel(sizes, places, down, short, down_out, slice_out, short_out, rows):
    down_out[...] = down[...].astype(bf16)
    height = down.shape[0] // 4
    first = pl.multiple_of(places[4] * height, 16)
    slice_out[...] = down[pl.ds(first, height)].astype(bf16)
    rows[...] = jnp.zeros_like(rows)
    offset = 0
    for line, size in enumerate(sizes):
        rows[line : line + 1, :size] = short[:, offset : offset + size]
        offset += size
    short_out[...] = rows[...].astype(bf16)


def pack_pass(order, places, down, short, sizes):
    return order.call(
        functools.partial(pack_kernel, sizes),
        [places, down, short],
        [in_smem, in_vmem, in_vmem],
        [
            shape_of(down.shape, bf16),
            shape_of((down.shape[0] // 4, down.shape[1]), bf16),
            shape_of((16, D), bf16),
        ],
        [in_vmem] * 3,
        scratch=[pltpu.VMEM((16, D), f32)],
        limit=32,
        name="pack",
    )


def wide_cast_kernel(left, right, out):
    out[:, :D] = left[...].astype(bf16)
    out[:, D:] = right[...].astype(bf16)


def wide_cast_pass(order, left, right):
    return order.call(
        wide_cast_kernel,
        [left, right],
        [in_vmem] * 2,
        [shape_of((left.shape[0], D + FF), bf16)],
        [in_vmem],
        limit=32,
        name="wide_cast",
    )[0]


def stack_kernel(first, second, out):
    out[0] = first[...]
    out[1] = second[...]


def stack_pass(order, first, second, waits=()):
    return order.call(
        stack_kernel,
        [first, second],
        [in_vmem] * 2,
        [shape_of((2,) + first.shape, first.dtype)],
        [in_vmem],
        name="stack",
        waits=waits,
    )[0]


def line_kernel(places, own, up_one, up_two, up_three, down_one, down_two, down_three, out, sems):
    floor = places[4]
    size = own.shape[0]

    def copy(piece, level, index):
        target = out.at[pl.ds(pl.multiple_of(level * size, 16), size)]
        return pltpu.make_async_copy(piece, target, sems.at[index])

    copies = [(None, copy(own, floor, 0))]
    for step, piece in enumerate((up_one, up_two, up_three), 1):
        copies.append((floor >= step, copy(piece, floor - step, step)))
    for step, piece in enumerate((down_one, down_two, down_three), 1):
        copies.append((floor + step <= 3, copy(piece, floor + step, step + 3)))
    for act in ("start", "wait"):
        for valid, one in copies:
            if valid is None:
                getattr(one, act)()
            else:
                pl.when(valid)(getattr(one, act))


def line_pass(order, places, pieces, waits=()):
    rows, width = pieces[0].shape
    return order.call(
        line_kernel,
        [places, *pieces],
        [in_smem] + [in_any] * 7,
        [shape_of((4 * rows, width), bf16)],
        [in_any],
        scratch=[pltpu.SemaphoreType.DMA((7,))],
        name="line",
        waits=waits,
    )[0]


def project_kernel(count, packed, places, rows, short, *rest):
    if not packed:
        given_hidden, rest = rest[0], rest[1:]
    else:
        other_short, rest = rest[0], rest[1:]
    parts, rest = rest[:count], rest[count:]
    query_out, wide_out, narrow_out, normed_out, vectors_out, hidden_out, weight, sems = rest
    copies = part_copies(places, parts, weight, sems)
    start_all(copies)
    shard = D // count
    if packed:
        vectors = jnp.zeros((8, D), f32)
        line = lax.broadcasted_iota(jnp.int32, (8, D), 0)
        for k in range(count):
            block = (other_short if k % 2 else short)[k // 2].astype(f32)[:8]
            vectors += pltpu.roll(jnp.where(line < 7, block, 0.0), places[k] * shard, 1)
            start = pl.multiple_of(places[k] * D, 128)
            hidden_out[:, pl.ds(start, D)] = block[7:8]
    else:
        vectors = short[...]
        hidden_out[...] = given_hidden[...]
    vectors_out[...] = vectors
    scaled, _ = normalise(rows[...].astype(f32))
    normed_out[...] = (scaled * vectors[0:1] + vectors[1:2]).astype(bf16)
    wait_all(copies)

    def block(column, width):
        return dot(normed_out[...], weight[:, column : column + width]).astype(bf16)

    for kind in range(2):
        for first in range(0, WIDE, 256):
            wide_out[kind, :, first : first + 256] = block((kind + 1) * D + first, 256)
    for kind in range(2):
        for first in range(0, NARROW, 256):
            narrow_out[kind, :, first : first + 256] = block((kind + 1) * D + WIDE + first, 256)
    for first in range(0, D, 256):
        query_out[:, first : first + 256] = block(first, 256)


def project(order, places, rows, parts, given, waits=()):
    count = len(parts)
    return order.call(
        functools.partial(project_kernel, count, count > 1),
        [places, rows, *given, *parts],
        [in_smem] + [in_vmem] * 3 + [in_any] * count,
        [
            shape_of((SEQ, D), bf16),
            shape_of((2, SEQ, WIDE), bf16),
            shape_of((2, SEQ, NARROW), bf16),
            shape_of((SEQ, D), bf16),
            shape_of((8, D), f32),
            shape_of((1, FF), f32),
        ],
        [in_vmem] * 6,
        scratch=[pltpu.VMEM((D, 3 * D), bf16), pltpu.SemaphoreType.DMA((count,))],
        name="project",
        waits=waits,
    )


def fill_page_bias(page_row, page_column, bias):
    for index, (low, high) in enumerate(WINDOWS):
        start = index * BLOCK
        same = page_column[low:high] == page_row[:, start : start + BLOCK]
        bias[index, : high - low] = jnp.where(same, 0.0, masked_score)


def two_heads(block):
    lane = lax.broadcasted_iota(jnp.int32, block.shape, 1)
    zero = jnp.zeros_like(block)
    return jnp.concatenate(
        [jnp.where(lane < HEAD_DIM, block, zero), jnp.where(lane < HEAD_DIM, zero, block)], axis=0
    )


def head_rows(both):
    return jnp.concatenate([both[:HEAD_DIM, :BLOCK], both[HEAD_DIM:, BLOCK:]], axis=0).T


def page_bias(bias, index, size):
    block = bias[index, :size]
    return jnp.concatenate([block, block], axis=1)


def attend_kernel(
    query, key, value, key_two, value_two, page_row, page_column, context, log_total, bias
):
    @pl.when(pl.program_id(0) == 0)
    def _():
        fill_page_bias(page_row, page_column, bias)

    for index, (low, high) in enumerate(WINDOWS):
        start = index * BLOCK
        queries = two_heads(query[start : start + BLOCK] * score_scale)
        allowed = page_bias(bias, index, high - low)
        scores = dot_nt(key[0, low:high], queries) + allowed
        scores_two = dot_nt(key_two[0, low:high], queries) + allowed
        largest = jnp.maximum(
            jnp.max(scores, axis=0, keepdims=True), jnp.max(scores_two, axis=0, keepdims=True)
        )
        exponent = jnp.exp(scores - largest)
        exponent_two = jnp.exp(scores_two - largest)
        total = column_sums(exponent) + column_sums(exponent_two)
        inverse = 1.0 / total
        shares = (exponent * inverse).astype(bf16)
        shares_two = (exponent_two * inverse).astype(bf16)
        both = dot_tn(value[0, low:high], shares) + dot_tn(value_two[0, low:high], shares_two)
        context[start : start + BLOCK] = head_rows(both).astype(bf16)
        log_row = largest + jnp.log(total)
        log_total[0, 0:1, start : start + BLOCK] = log_row[:, :BLOCK]
        log_total[0, 1:2, start : start + BLOCK] = log_row[:, BLOCK:]


def pair_specs(query_first, key_first):
    query = pl.BlockSpec((SEQ, PAIR), lambda step: (0, query_first + step))
    key = pl.BlockSpec((1, SEQ, PAIR), lambda step: (0, 0, key_first + step))
    value = pl.BlockSpec((1, SEQ, PAIR), lambda step: (1, 0, key_first + step))
    page_row = pl.BlockSpec((1, SEQ), lambda step: (0, 0))
    page_column = pl.BlockSpec((SEQ, 1), lambda step: (0, 0))
    narrow = pl.BlockSpec((SEQ, PAIR), lambda step: (0, step))
    logs = pl.BlockSpec((1, 2, SEQ), lambda step: (key_first + step, 0, 0))
    return query, key, value, page_row, page_column, narrow, logs


def attend(order, query_first, queries, own, other, page_row, page_column, cost=0):
    width = own.shape[2]
    steps = width // PAIR
    query, key, value, row_spec, column_spec, narrow, logs = pair_specs(query_first, 0)
    return order.call(
        attend_kernel,
        [queries, own, own, other, other, page_row, page_column],
        [query, key, value, key, value, row_spec, column_spec],
        [shape_of((SEQ, width), bf16), shape_of((steps, 2, SEQ), f32)],
        [narrow, logs],
        scratch=[pltpu.VMEM((len(WINDOWS), WINDOW, BLOCK), f32)],
        grid=(steps,),
        name="attend",
        cost=cost,
    )


def attend_back_kernel(
    query,
    key,
    value,
    key_two,
    value_two,
    context_grad,
    log_total,
    page_row,
    page_column,
    query_grad,
    own_grad,
    other_grad,
    bias,
    other_sum,
):
    @pl.when(pl.program_id(0) == 0)
    def _():
        fill_page_bias(page_row, page_column, bias)

    own_grad[...] = jnp.zeros_like(own_grad)
    other_sum[...] = jnp.zeros_like(other_sum)
    for index, (low, high) in enumerate(WINDOWS):
        start = index * BLOCK
        queries = two_heads(query[start : start + BLOCK] * score_scale)
        grads = two_heads(context_grad[start : start + BLOCK])
        log_row = jnp.concatenate(
            [
                log_total[0, 0:1, start : start + BLOCK],
                log_total[0, 1:2, start : start + BLOCK],
            ],
            axis=1,
        )
        allowed = page_bias(bias, index, high - low)
        keys, keys_two = key[0, low:high], key_two[0, low:high]
        shares = jnp.exp(dot_nt(keys, queries) + allowed - log_row)
        shares_two = jnp.exp(dot_nt(keys_two, queries) + allowed - log_row)
        share_grad = dot_nt(value[0, low:high], grads)
        share_grad_two = dot_nt(value_two[0, low:high], grads)
        centre = column_sums(shares * share_grad) + column_sums(shares_two * share_grad_two)
        score_grad = (shares * (share_grad - centre)).astype(bf16)
        score_grad_two = (shares_two * (share_grad_two - centre)).astype(bf16)
        own_grad[0, low:high] += dot(score_grad, queries)
        own_grad[1, low:high] += dot(shares.astype(bf16), grads)
        other_sum[0, low:high] += dot(score_grad_two, queries)
        other_sum[1, low:high] += dot(shares_two.astype(bf16), grads)
        both = dot_tn(keys, score_grad) + dot_tn(keys_two, score_grad_two)
        query_grad[start : start + BLOCK] = (head_rows(both) * score_scale).astype(bf16)
    other_grad[...] = other_sum[...].astype(bf16)


def attend_back(
    order, query_first, key_first, queries, own, other, context_grad, logs, page_row, page_column
):
    steps = THIRD // PAIR
    query, key, value, row_spec, column_spec, narrow, log_spec = pair_specs(query_first, key_first)
    pair = pl.BlockSpec((2, SEQ, PAIR), lambda step: (0, 0, step))
    return order.call(
        attend_back_kernel,
        [queries, own, own, other, other, context_grad, logs, page_row, page_column],
        [query, key, value, key, value, query, log_spec, row_spec, column_spec],
        [
            shape_of((SEQ, THIRD), bf16),
            shape_of((2, SEQ, THIRD), f32),
            shape_of((2, SEQ, THIRD), bf16),
        ],
        [narrow, pair, pair],
        scratch=[
            pltpu.VMEM((len(WINDOWS), WINDOW, BLOCK), f32),
            pltpu.VMEM((2, SEQ, PAIR), f32),
        ],
        grid=(steps,),
        name="attend_back",
    )


def wide_copies(places, parts, w_out, w_up, out_sems, up_sems):
    count = len(parts)
    rows, slot = D // count, FF // count
    out_copies, up_copies = [], []
    for k, part in enumerate(parts):
        target = pl.ds(pl.multiple_of(places[k] * rows, 16), rows)
        out_copies.append(
            pltpu.make_async_copy(part.at[pl.ds(0, rows), pl.ds(0, D)], w_out.at[target], out_sems.at[k])
        )
    for c in range(count):
        columns = pl.ds(pl.multiple_of(D + places[c] * slot, 128), slot)
        one = []
        for k, part in enumerate(parts):
            target = pl.ds(pl.multiple_of(places[k] * rows, 16), rows)
            one.append(
                pltpu.make_async_copy(
                    part.at[pl.ds(0, rows), columns], w_up.at[c, target], up_sems.at[c, k]
                )
            )
        up_copies.append(one)
    return out_copies, up_copies


def down_copies(parts, w_down, sems):
    return [pltpu.make_async_copy(part, w_down.at[k], sems.at[k]) for k, part in enumerate(parts)]


def weight_scratch(count):
    return [
        pltpu.VMEM((D, D), bf16),
        pltpu.VMEM((count, D, FF // count), bf16),
        pltpu.VMEM((count, FF // count, D), bf16),
        pltpu.SemaphoreType.DMA((count,)),
        pltpu.SemaphoreType.DMA((count, count)),
        pltpu.SemaphoreType.DMA((count,)),
    ]


def same_block(dims):
    return pl.BlockSpec(dims, lambda step, places: (0,) * len(dims))


def slot_block(rows, slot):
    return pl.BlockSpec((rows, slot), lambda step, places: (0, places[step]))


def middle_kernel(count, places, rows, context, context_two, tangent, vectors, partner, hidden_bias, *rest):
    wide_parts, down_parts, rest = rest[:count], rest[count : 2 * count], rest[2 * count :]
    middle_out, second_out, hidden_out, slope_out, modal_out, inner_out = rest[:6]
    total, w_out, w_up, w_down, out_sems, up_sems, down_sems = rest[6:]
    out_copies, up_copies = wide_copies(places, wide_parts, w_out, w_up, out_sems, up_sems)
    last_copies = down_copies(down_parts, w_down, down_sems)
    step = pl.program_id(0)

    @pl.when(step == 0)
    def _():
        start_all(out_copies)
        for one in up_copies:
            start_all(one)
        start_all(last_copies)
        wait_all(out_copies)
        middle = rows[...].astype(f32) + dot(context[...], w_out[:WIDE])
        middle += dot(context_two[...], w_out[WIDE:])
        middle_out[...] = middle
        scaled, _ = normalise(middle)
        second_out[...] = (scaled * vectors[2:3] + vectors[3:4]).astype(bf16)
        total[...] = middle + vectors[4:5]

    for k in range(count):

        @pl.when(step == k)
        def _():
            wait_all(up_copies[k])
            last_copies[k].wait()

    slot = FF // count
    size = 256
    for first in range(0, slot, size):
        part = slice(first, first + size)
        upper = dot(second_out[...], w_up[step, :, part]) + hidden_bias[:, part]
        square = upper * upper
        angle = jnp.tanh(upper * (gelu_scale + (gelu_cubic * gelu_scale) * square))
        half = 0.5 + 0.5 * angle
        hidden_out[:, part] = (upper * half).astype(bf16)
        bend = 2.0 * gelu_scale + (6.0 * gelu_cubic * gelu_scale) * square
        slope_out[:, part] = (half + half * (1.0 - half) * (upper * bend)).astype(bf16)
    total[...] += dot(hidden_out[...], w_down[step])

    @pl.when(step == count - 1)
    def _():
        modal_out[...] = total[...].astype(bf16)
        modal = modal_out[...].astype(f32)
        own = jnp.sum(modal * vectors[5:6], axis=1, keepdims=True)
        cross = jnp.sum(modal * partner[6:7], axis=1, keepdims=True)
        met = jnp.sum(modal * tangent[...].astype(f32), axis=1, keepdims=True)
        lane = lax.broadcasted_iota(jnp.int32, (SEQ, 128), 1)
        columns = jnp.where(lane == 0, own, jnp.where(lane == 1, cross, met))
        inner_out[...] = columns.T[:8]


def middle_pass(
    order, places, rows, contexts, tangent, vectors, partner, hidden_bias, wides, downs
):
    count = len(downs)
    slot = FF // count
    return order.call(
        functools.partial(middle_kernel, count),
        [rows, *contexts, tangent, vectors, partner, hidden_bias, *wides, *downs],
        [same_block((SEQ, D)), same_block((SEQ, WIDE)), same_block((SEQ, NARROW))]
        + [same_block((SEQ, D)), same_block((8, D)), same_block((8, D)), slot_block(1, slot)]
        + [in_any] * (2 * count),
        [
            shape_of((SEQ, D), f32),
            shape_of((SEQ, D), bf16),
            shape_of((SEQ, FF), bf16),
            shape_of((SEQ, FF), bf16),
            shape_of((SEQ, D), bf16),
            shape_of((8, SEQ), f32),
        ],
        [
            same_block((SEQ, D)),
            same_block((SEQ, D)),
            slot_block(SEQ, slot),
            slot_block(SEQ, slot),
            same_block((SEQ, D)),
            same_block((8, SEQ)),
        ],
        scratch=[pltpu.VMEM((SEQ, D), f32)] + weight_scratch(count),
        grid=(count,),
        limit=52,
        name="middle",
        prefetch=places,
    )


def gate_kernel(
    own, other, tangent, partner_tangent, vectors, partner, grad_out, low_out, columns_out, sums
):
    gate = jax.nn.sigmoid(own[0:1] + other[1:2])
    gate_two = jax.nn.sigmoid(other[0:1] + own[1:2])
    logit = other[2:3] * gate * (1.0 - gate)
    logit_two = own[2:3] * gate_two * (1.0 - gate_two)
    padding = jnp.zeros((124, SEQ), f32)
    columns = jnp.concatenate([gate, logit, gate_two, logit_two, padding], axis=0).T
    columns_out[...] = columns
    grad = (
        tangent[...].astype(f32)
        + columns[:, 1:2] * vectors[5:6]
        + partner_tangent[...].astype(f32) * columns[:, 2:3]
        + columns[:, 3:4] * partner[6:7]
    )
    grad_out[...] = grad
    low_out[...] = grad.astype(bf16)
    sums[...] = column_sums(grad)


def gate_pass(order, own, other, tangent, partner_tangent, vectors, partner):
    return order.call(
        gate_kernel,
        [own, other, tangent, partner_tangent, vectors, partner],
        [in_vmem] * 6,
        [
            shape_of((SEQ, D), f32),
            shape_of((SEQ, D), bf16),
            shape_of((SEQ, 128), f32),
            shape_of((1, D), f32),
        ],
        [in_vmem] * 4,
        name="gate",
    )


def mix_kernel(own, other, columns, mixed, own_sums, other_sums):
    own_rows = own[...].astype(f32)
    other_rows = other[...].astype(f32)
    mixed[...] = (own_rows + columns[:, 0:1] * other_rows).astype(bf16)
    own_sums[...] = column_sums(columns[:, 1:2] * own_rows)
    other_sums[...] = column_sums(columns[:, 1:2] * other_rows)


def mix_pass(order, own, other, columns):
    return order.call(
        mix_kernel,
        [own, other, columns],
        [in_vmem] * 3,
        [shape_of((SEQ, D), bf16), shape_of((1, D), f32), shape_of((1, D), f32)],
        [in_vmem] * 3,
        name="mix",
    )


def chain_kernel(count, places, low, grad, slope, middle, vectors, *rest):
    wide_parts, down_parts, rest = rest[:count], rest[count : 2 * count], rest[2 * count :]
    upper_out, upper_sums, total_out, total_low_out, context_out, gain_sums, bias_sums = rest[:7]
    normed_grad, w_out, w_up, w_down, out_sems, up_sems, down_sems = rest[7:]
    out_copies, up_copies = wide_copies(places, wide_parts, w_out, w_up, out_sems, up_sems)
    first_copies = down_copies(down_parts, w_down, down_sems)
    step = pl.program_id(0)

    @pl.when(step == 0)
    def _():
        for k in range(count):
            first_copies[k].start()
            start_all(up_copies[k])
        start_all(out_copies)
        normed_grad[...] = jnp.zeros_like(normed_grad)

    for k in range(count):

        @pl.when(step == k)
        def _():
            first_copies[k].wait()
            wait_all(up_copies[k])

    slot = FF // count
    size = 256
    for first in range(0, slot, size):
        part = slice(first, first + size)
        upper = dot_nt(low[...], w_down[step, part]) * slope[:, part].astype(f32)
        upper_sums[:, part] = column_sums(upper)
        upper_out[:, part] = upper.astype(bf16)
    normed_grad[...] += dot_nt(upper_out[...], w_up[step])

    @pl.when(step == count - 1)
    def _():
        wait_all(out_copies)
        scaled, root = normalise(middle[...])
        incoming = normed_grad[...]
        gain_sums[...] = column_sums(incoming * scaled)
        bias_sums[...] = column_sums(incoming)
        total = grad[...] + norm_back(scaled, root, vectors[2:3], incoming)
        total_out[...] = total
        total_low_out[...] = total.astype(bf16)
        context_out[...] = dot_nt(total_low_out[...], w_out[...]).astype(bf16)


def chain_pass(order, places, low, grad, slope, middle, vectors, wides, downs):
    count = len(downs)
    slot = FF // count
    return order.call(
        functools.partial(chain_kernel, count),
        [low, grad, slope, middle, vectors, *wides, *downs],
        [same_block((SEQ, D)), same_block((SEQ, D)), slot_block(SEQ, slot)]
        + [same_block((SEQ, D)), same_block((8, D))]
        + [in_any] * (2 * count),
        [
            shape_of((SEQ, FF), bf16),
            shape_of((1, FF), f32),
            shape_of((SEQ, D), f32),
            shape_of((SEQ, D), bf16),
            shape_of((SEQ, D), bf16),
            shape_of((1, D), f32),
            shape_of((1, D), f32),
        ],
        [slot_block(SEQ, slot), slot_block(1, slot)]
        + [same_block((SEQ, D))] * 3
        + [same_block((1, D))] * 2,
        scratch=[pltpu.VMEM((SEQ, D), f32)] + weight_scratch(count),
        grid=(count,),
        limit=52,
        name="chain",
        prefetch=places,
    )


def slots_of(count):
    return (list(range(0, count, 2)), list(range(1, count, 2)))


def row_grads_kernel(count, widths, lefts, rights, summed, places, *rest):
    left, rest = rest[:lefts], rest[lefts:]
    sources, rest = rest[:rights], rest[rights:]
    if summed:
        pair_low, rest = rest[0], rest[1:]
        pair_low[...] = (sources[0][...] + sources[1][...].astype(f32)).astype(bf16)
        blocks = [pair_low[kind] for kind in range(2)]
    else:
        blocks = []
        for source in sources:
            step = min(source.shape[1], 512)
            blocks += [source[:, k : k + step] for k in range(0, source.shape[1], step)]
    outs, whole = rest[:-1], rest[-1]
    near, far = slots_of(count)
    rows = D // count
    turned = jnp.concatenate([one[...].T for one in left], axis=0)
    each = 2 if far else 1
    for index, width in enumerate(widths):
        low = 0
        while low < width:
            right = blocks.pop(0)
            whole[:, low : low + right.shape[1]] = dot(turned, right).astype(bf16)
            low += right.shape[1]
        for out, slots in zip(outs[each * index : each * index + each], (near, far)):
            for place, slot in enumerate(slots):
                begin = pl.multiple_of(places[slot] * rows, 16)
                out[place] = whole[pl.ds(begin, rows), :width]


def row_grads(order, places, left, sources, widths, count, summed=False):
    near, far = slots_of(count)
    rows = D // count
    outs = []
    for width in widths:
        outs.append(shape_of((len(near), rows, width), bf16))
        if far:
            outs.append(shape_of((len(far), rows, width), bf16))
    low = [shape_of(sources[0].shape, bf16)] if summed else []
    return order.call(
        functools.partial(row_grads_kernel, count, widths, len(left), len(sources), summed),
        [places, *left, *sources],
        [in_smem] + [in_vmem] * (len(left) + len(sources)),
        low + outs,
        [in_vmem] * len(low + outs),
        scratch=[pltpu.VMEM((D, max(widths)), bf16)],
        limit=32,
        name="row_grads",
    )


def down_grads_kernel(count, first, height, fold, places, low, hidden, *outs):
    near, far = slots_of(count)
    width = FF // count
    turned = low[:, first : first + height].T
    rows = height // fold
    for out, slots in zip(outs, (near, far)):
        for place, slot in enumerate(slots):
            begin = pl.multiple_of(places[slot] * width, 128)
            block = dot(turned, hidden[:, pl.ds(begin, width)]).astype(bf16)
            for k in range(fold):
                out[place, :, k * width : (k + 1) * width] = block[k * rows : (k + 1) * rows]


def down_grads(order, places, low, hidden, first, height, fold, count):
    near, far = slots_of(count)
    width = FF // count
    outs = [shape_of((len(near), height // fold, fold * width), bf16)]
    if far:
        outs.append(shape_of((len(far), height // fold, fold * width), bf16))
    return order.call(
        functools.partial(down_grads_kernel, count, first, height, fold),
        [places, low, hidden],
        [in_smem, in_vmem, in_vmem],
        outs,
        [in_vmem] * len(outs),
        limit=32,
        name="down_grads",
    )


def by_rows(width):
    return pl.BlockSpec((ROWS, width), lambda step: (step, 0))


def whole_block(dims):
    return pl.BlockSpec(dims, lambda step: (0,) * len(dims))


def first_kernel(count, places, queries, pairs, total, rows, vectors, short, *rest):
    parts, rest = rest[:count], rest[count:]
    grad_out, short_out, weight, sems = rest
    copies = part_copies(places, parts, weight, sems)

    @pl.when(pl.program_id(0) == 0)
    def _():
        start_all(copies)
        short_out[...] = jnp.zeros_like(short_out)
        gain_two, bias_two, output_bias, gate_self, gate_cross, hidden_bias = short
        for line, member in enumerate((gain_two, bias_two, output_bias, gate_self, gate_cross)):
            short_out[line + 2 : line + 3] = member[...]
        for line in range(FF // D):
            short_out[line + 8 : line + 9] = hidden_bias[:, line * D : (line + 1) * D]
        wait_all(copies)

    normed_grad = jnp.zeros((ROWS, D), f32)
    for group in range(GROUPS):
        first = group * THIRD
        normed_grad += dot_nt(queries[group][...], weight[:, first : first + THIRD])
        for kind in range(2):
            start = (kind + 1) * D + first
            normed_grad += dot_nt(pairs[group][kind], weight[:, start : start + THIRD])
    scaled, root = normalise(rows[...].astype(f32))
    short_out[0:1] += column_sums(normed_grad * scaled)
    short_out[1:2] += column_sums(normed_grad)
    grad_out[...] = total[...] + norm_back(scaled, root, vectors[0:1], normed_grad)


def first_pass(order, places, queries, pairs, total, rows, vectors, short, parts):
    count = len(parts)
    pair = pl.BlockSpec((2, ROWS, THIRD), lambda step: (0, step, 0))
    shorts = len(short)

    def kernel(places_ref, q0, q1, q2, p0, p1, p2, total_ref, rows_ref, vectors_ref, *rest):
        first_kernel(
            count,
            places_ref,
            (q0, q1, q2),
            (p0, p1, p2),
            total_ref,
            rows_ref,
            vectors_ref,
            rest[:shorts],
            *rest[shorts:],
        )

    return order.call(
        kernel,
        [places, *queries, *pairs, total, rows, vectors, *short, *parts],
        [in_smem]
        + [by_rows(THIRD)] * GROUPS
        + [pair] * GROUPS
        + [by_rows(D), by_rows(D), whole_block((8, D))]
        + [whole_block(member.shape) for member in short]
        + [in_any] * count,
        [shape_of((SEQ, D), f32), shape_of((16, D), f32)],
        [by_rows(D), whole_block((16, D))],
        scratch=[pltpu.VMEM((D, 3 * D), bf16), pltpu.SemaphoreType.DMA((count,))],
        grid=(SEQ // ROWS,),
        limit=28,
        name="first",
    )


def settle_kernel(kind, count, places, *refs):
    totals, returned, outs = refs[:count], refs[count : 2 * count], refs[2 * count :]
    inner = jnp.logical_and(places[4] > 0, places[4] < 3)
    values = [jnp.where(inner, a[...], b[...]).astype(f32) for a, b in zip(totals, returned)]
    out = outs[0]
    if kind == "turn":
        first = 0
        for value in values:
            rows = value.shape[0]
            for k in range(0, value.shape[1], D):
                out[:, first : first + rows] = value[:, k : k + D].T
                first += rows
    elif kind == "columns":
        first = 0
        for value in values:
            out[:, first : first + value.shape[1]] = value
            first += value.shape[1]
    else:
        outs[1][...] = values[0][:, :D]
        out[:, :D] = values[0][:, D:]
        for group in range(GROUPS):
            for part in range(2):
                start = (part + 1) * D + group * THIRD
                block = values[1 + group][:, part * THIRD : (part + 1) * THIRD]
                out[:, start : start + THIRD] = block


def settle(order, kind, places, blocks, dims):
    count = len(blocks)
    found = order.call(
        functools.partial(settle_kernel, kind, count),
        [places] + [block[0] for block in blocks] + [block[1] for block in blocks],
        [in_smem] + [in_vmem] * (2 * count),
        [shape_of(each, f32) for each in dims],
        [in_vmem] * len(dims),
        name="settle",
    )
    return found[0] if len(dims) == 1 else found


def swap_bit(value, axis, bit):
    size = lax.axis_size(axis)
    return lax.ppermute(value, axis, [(source, source ^ (1 << bit)) for source in range(size)])


def from_partner(value):
    size = lax.axis_size("stream")
    half = size // 2
    return lax.ppermute(value, "stream", [(source, (source + half) % size) for source in range(size)])


def along(value, pairs):
    return lax.ppermute(value, "dp", pairs)


def up_line(value, steps):
    return along(value, [(floor, floor + 1) for floor in range(steps - 1, 3)])


def down_line(value, steps):
    return along(value, [(floor, floor - 1) for floor in range(1, 5 - steps)])


def swap_outer(value):
    return along(value, [(0, 1), (1, 0), (2, 3), (3, 2)])


def to_inner(value):
    return along(value, [(0, 1), (3, 2)])


def over_middle(value):
    return along(value, [(1, 2), (2, 1)])


def to_outer(value):
    return along(value, [(1, 0), (2, 3)])


def core(value):
    return swap_bit(value, "stream", 0)


def across(value):
    return swap_bit(value, "stream", 1)


def modality_groups():
    size = lax.axis_size("stream")
    half = size // 2
    return [list(range(half)), list(range(half, size))]


def body(
    regions,
    cotangent,
    page_lens,
    qkv_weight,
    out_weight,
    up_weight,
    down_weight,
    ln1_gain,
    ln1_bias,
    ln2_gain,
    ln2_bias,
    up_bias,
    down_bias,
    gate_own,
    gate_other,
):
    half = lax.axis_size("stream") // 2
    depth = lax.axis_size("dp")
    paired = half == 4 and depth == 4
    side = lax.axis_index("stream") % half
    floor = lax.axis_index("dp")
    count = 4 if paired else 1
    slots = jnp.arange(4, dtype=jnp.int32)
    picks = jnp.bitwise_xor(side.astype(jnp.int32), slots) if paired else jnp.zeros_like(slots)
    places = jnp.concatenate([picks, floor.astype(jnp.int32)[None]])
    order = Order()
    short = (ln1_gain, ln1_bias, ln2_gain, ln2_bias, down_bias, gate_own, gate_other, up_bias)
    sizes = [member.size for member in short]
    partner_tangent = from_partner(cotangent)

    lengths = lax.dynamic_slice_in_dim(page_lens, side * depth + floor, 1, 0)
    positions = jnp.arange(SEQ, dtype=jnp.int32)
    page_ends = jnp.cumsum(lengths[0], dtype=jnp.int32)
    pages = jnp.sum((page_ends[:, None] <= positions[None, :]).astype(jnp.int32), axis=0)
    page_row, page_column = pages[None, :], pages[:, None]

    def attend_all(wide, other):
        first, cost = (0, 0) if wide is own_wide else (WIDE // PAIR, 60)
        return attend(order, first, queries, wide, other, page_row, page_column, cost)

    if paired:
        (qkv_shard,) = cast_pass(order, [qkv_weight])
        qkv_across, qkv_near = across(qkv_shard), core(qkv_shard)
        short_all = jnp.concatenate(short)[None]
        down_shard, down_slice, short_shard = pack_pass(order, places, down_weight, short_all, sizes)
        short_across, slice_across = across(short_shard), across(down_slice)
        wide_shard = wide_cast_pass(order, out_weight, up_weight)
        wide_near, down_near = core(wide_shard), core(down_shard)
        short_pair = stack_pass(order, short_shard, short_across)
        (qkv_across,) = order.hold([qkv_across], waits=[partner_tangent])
        short_far, qkv_far = core(short_pair), core(qkv_across)
        qkv_parts = [qkv_shard, qkv_near, qkv_across, qkv_far]
        queries, own_wide, own_narrow, normed, vectors, hidden_bias = project(
            order, places, regions, qkv_parts, (short_pair, short_far), [wide_near, down_near]
        )
        other_wide, other_narrow = from_partner(own_wide), from_partner(own_narrow)
        own_slice, wide_shard = order.hold([slice_across, wide_shard])
        wide_across = across(wide_shard)
        up_one, down_one = up_line(own_slice, 1), down_line(own_slice, 1)
        up_one, down_one = order.hold([up_one, down_one])
        up_two, down_two = up_line(up_one, 2), down_line(down_one, 2)
        up_two, down_two = order.hold([up_two, down_two])
        up_three, down_three = up_line(up_two, 3), down_line(down_two, 3)
        context_wide, logs_wide = attend_all(own_wide, other_wide)
        pieces = (own_slice, up_one, up_two, up_three, down_one, down_two, down_three)
        down_across = line_pass(order, places, pieces)
        down_far = core(down_across)
        wide_across, vectors = order.hold([wide_across, vectors])
        partner = from_partner(vectors)
        wide_far = core(wide_across)
        context_narrow, logs_narrow = attend_all(own_narrow, other_narrow)
        wide_parts = [wide_shard, wide_near, wide_across, wide_far]
        down_parts = [down_shard, down_near, down_across, down_far]
    else:

        def gather(shard):
            return [
                lax.all_gather(shard, "stream", axis_index_groups=modality_groups(), tiled=True)
            ]

        packed = jnp.concatenate([member.astype(bf16) for member in short])[None]
        found = gather(packed)[0].astype(f32)
        shard = D // half
        rows = [found[:, k * shard : (k + 1) * shard].reshape(1, D) for k in range(7)]
        given = (
            jnp.concatenate(rows + [jnp.zeros((1, D), f32)], axis=0),
            found[:, 7 * shard :].reshape(1, FF),
        )
        qkv_parts = gather(qkv_weight.astype(bf16))
        wide_parts = gather(jnp.concatenate([out_weight, up_weight], axis=1).astype(bf16))
        down_parts = gather(down_weight.astype(bf16))
        queries, own_wide, own_narrow, normed, vectors, hidden_bias = project(
            order, places, regions, qkv_parts, given
        )
        other_wide, other_narrow = from_partner(own_wide), from_partner(own_narrow)
        partner = from_partner(vectors)
        context_wide, logs_wide = attend_all(own_wide, other_wide)
        context_narrow, logs_narrow = attend_all(own_narrow, other_narrow)

    contexts = [context_wide, context_narrow]
    middle, second, hidden, slope, modal, inner_own = middle_pass(
        order,
        places,
        regions,
        contexts,
        partner_tangent,
        vectors,
        partner,
        hidden_bias,
        wide_parts,
        down_parts,
    )
    inner_other = from_partner(inner_own)
    modal_grad, modal_low, columns, output_bias_grad = gate_pass(
        order, inner_own, inner_other, cotangent, partner_tangent, vectors, partner
    )

    def attend_back_group(group):
        query_first = group * THIRD // PAIR
        wide = group * THIRD < WIDE
        query_grad, own_grad, other_grad = attend_back(
            order,
            query_first,
            query_first if wide else 0,
            queries,
            own_wide if wide else own_narrow,
            other_wide if wide else other_narrow,
            context_grad,
            logs_wide if wide else logs_narrow,
            page_row,
            page_column,
        )
        query_grads.append(query_grad)
        own_grads.append(own_grad)
        returned.append(from_partner(other_grad))

    def pair_group(group):
        pair_grad, *flat = row_grads(
            order,
            places,
            [normed],
            [own_grads[group], returned[group]],
            [2 * THIRD],
            count,
            summed=True,
        )
        pair_grads.append(pair_grad)
        return flat

    def last_pass():
        short_grads = (
            gain_two_grad,
            bias_two_grad,
            output_bias_grad,
            gate_self_grad,
            gate_cross_grad,
            hidden_bias_grad,
        )
        return first_pass(
            order,
            places,
            query_grads,
            pair_grads,
            middle_grad,
            regions,
            vectors,
            short_grads,
            qkv_parts,
        )

    query_grads, own_grads, returned, pair_grads = [], [], [], []
    if paired:
        d1, far = down_grads(order, places, modal_low, hidden, 0, 384, 2, count)
        d1_core = core(far)
        d2, far = down_grads(order, places, modal_low, hidden, 384, 384, 2, count)
        d2_core = core(far)
        (modal,) = order.hold([modal])
        partner_modal = from_partner(modal)
        d1, away = sums_pass(order, places, folds=[[(d1, d1_core)]])
        d1_in = across(away)
        upper_low, hidden_bias_grad, middle_grad, middle_low, context_grad, gain_two_grad, bias_two_grad = (
            chain_pass(
                order, places, modal_low, modal_grad, slope, middle, vectors, wide_parts, down_parts
            )
        )
        u1, far_one, u2, far_two = row_grads(order, places, [second], [upper_low], [1536, 1536], count)
        u1_core, u2_core = core(far_one), core(far_two)
        d2, away, d1 = sums_pass(order, places, folds=[[(d2, d2_core)]], adds=[(d1, d1_in)])
        d2_in, d1_in = across(away), to_inner(d1)
        attend_back_group(0)
        mixed_rows, gate_self_grad, gate_cross_grad = mix_pass(order, modal, partner_modal, columns)
        o1, far_one = row_grads(order, places, contexts, [middle_low], [D], count)
        o1_core = core(far_one)
        u1, away, u2, away_two, d2, d1 = sums_pass(
            order,
            places,
            folds=[[(u1, u1_core)], [(u2, u2_core)]],
            adds=[(d2, d2_in), (d1, d1_in)],
        )
        u1_in, d2_in, d1_mid = across(away), to_inner(d2), over_middle(d1)
        attend_back_group(1)
        d2, u1, u1_pay = sums_pass(
            order,
            places,
            adds=[(d2, d2_in)],
            pays=[(u1, u1_in, d1, d1_mid)],
            waits=[returned[0], o1_core],
        )
        (away_two,) = order.hold([away_two])
        u2_in, u1_in, d2_mid = across(away_two), swap_outer(u1_pay), over_middle(d2)
        attend_back_group(2)
        q1, far_two = row_grads(order, places, [normed], query_grads, [D], count)
        q1_core = core(far_two)
        p1, far = pair_group(0)
        p1_core = core(far)
        u1, u2, u2_pay = sums_pass(
            order, places, adds=[(u1, u1_in)], pays=[(u2, u2_in, d2, d2_mid)], waits=[returned[1]]
        )
        d1_out = u1_in
        u2_in, u1_mid = swap_outer(u2_pay), over_middle(u1)
        oq, away, p1, away_two = sums_pass(
            order, places, folds=[[(o1, o1_core), (q1, q1_core)], [(p1, p1_core)]]
        )
        oq_in, p1_in = across(away), across(away_two)
        p2, far = pair_group(1)
        p2_core = core(far)
        p3, far = pair_group(2)
        p3_core = core(far)
        region_grad, short_rows = last_pass()
        s_core = core(short_rows)
        p2, away, p3, away_two, u2, short_rows, oq, oq_pay = sums_pass(
            order,
            places,
            folds=[[(p2, p2_core)], [(p3, p3_core)]],
            adds=[(u2, u2_in), (short_rows, s_core)],
            pays=[(oq, oq_in, u1, u1_mid)],
            waits=[p1_in],
        )
        d2_out = u2_in
        oq_in, u2_mid = swap_outer(oq_pay), over_middle(u2)
        p2_in, p3_in, s_in = across(away), across(away_two), across(short_rows)
        down_grad = settle(order, "turn", places, [(u1_pay, d1_out), (u2_pay, d2_out)], [(D, D)])
        p1, p2, p3, short_rows = sums_pass(
            order, places, adds=[(p1, p1_in), (p2, p2_in), (p3, p3_in), (short_rows, s_in)]
        )
        p1_in, p2_in, p3_in = to_inner(p1), to_inner(p2), to_inner(p3)
        oq, u2 = sums_pass(order, places, adds=[(oq, oq_in), (u2, u2_mid)])
        u1_out = oq_in
        oq_mid, u2_out = over_middle(oq), to_outer(u2)
        p1, p2 = sums_pass(order, places, adds=[(p1, p1_in), (p2, p2_in)])
        s_in = to_inner(short_rows)
        p1_mid, p2_mid = over_middle(p1), over_middle(p2)
        p3, oq = sums_pass(order, places, adds=[(p3, p3_in), (oq, oq_mid)], waits=[u2_out])
        p3_mid, oq_out = over_middle(p3), to_outer(oq)
        up_grad = settle(order, "columns", places, [(oq_pay, u1_out), (u2, u2_out)], [(D // 4, FF)])
        short_rows, p1, p2 = sums_pass(
            order, places, adds=[(short_rows, s_in), (p1, p1_mid), (p2, p2_mid)]
        )
        s_mid, p1_out, p2_out = over_middle(short_rows), to_outer(p1), to_outer(p2)
        p3, short_rows = sums_pass(order, places, adds=[(p3, p3_mid), (short_rows, s_mid)])
        p3_out, s_out = to_outer(p3), to_outer(short_rows)
        qkv_grad, out_grad = settle(
            order,
            "pairs",
            places,
            [(oq, oq_out), (p1, p1_out), (p2, p2_out), (p3, p3_out)],
            [(D // 4, 3 * D), (D // 4, D)],
        )
        inner = jnp.logical_and(floor > 0, floor < 3)
        short_rows = jnp.where(inner, short_rows, s_out)
    else:
        (down_block,) = down_grads(order, places, modal_low, hidden, 0, D, 1, count)
        upper_low, hidden_bias_grad, middle_grad, middle_low, context_grad, gain_two_grad, bias_two_grad = (
            chain_pass(
                order, places, modal_low, modal_grad, slope, middle, vectors, wide_parts, down_parts
            )
        )
        (up_block,) = row_grads(order, places, [second], [upper_low], [FF], count)
        (out_block,) = row_grads(order, places, contexts, [middle_low], [D], count)
        for group in range(GROUPS):
            attend_back_group(group)
        partner_modal = from_partner(modal)
        mixed_rows, gate_self_grad, gate_cross_grad = mix_pass(order, modal, partner_modal, columns)
        (query_block,) = row_grads(order, places, [normed], query_grads, [D], count)
        pair_blocks = [pair_group(group)[0] for group in range(GROUPS)]
        region_grad, short_rows = last_pass()

        def total(block):
            groups = modality_groups()
            owned = lax.psum_scatter(
                block.astype(f32), "stream", axis_index_groups=groups, tiled=True
            )
            return lax.psum(owned, "dp")

        down_grad = total(down_block[0].T)
        up_grad, out_grad = total(up_block[0]), total(out_block[0])
        qkv_grad = total(
            jnp.concatenate(
                [query_block[0]]
                + [block[0, :, :THIRD] for block in pair_blocks]
                + [block[0, :, THIRD:] for block in pair_blocks],
                axis=1,
            )
        )
        short_rows = lax.psum(
            lax.psum(short_rows, "stream", axis_index_groups=modality_groups()), "dp"
        )

    shard = D // half
    own_rows = lax.dynamic_slice_in_dim(short_rows, side * shard, shard, 1)
    hidden_rows = short_rows[8 : 8 + FF // D].reshape(FF)
    own_hidden = lax.dynamic_slice_in_dim(hidden_rows, side * (FF // half), FF // half, 0)
    return (
        mixed_rows,
        region_grad,
        qkv_grad,
        out_grad,
        up_grad,
        down_grad,
        own_rows[0],
        own_rows[1],
        own_rows[2],
        own_rows[3],
        own_hidden,
        own_rows[4],
        own_rows[5],
        own_rows[6],
    )


def solution(mesh):
    in_specs = (
        P(("stream", "dp"), None),
        P(("stream", "dp"), None),
        P(),
        P("stream", None),
        P("stream", None),
        P("stream", None),
        P("stream", None),
        P("stream"),
        P("stream"),
        P("stream"),
        P("stream"),
        P("stream"),
        P("stream"),
        P("stream"),
        P("stream"),
    )
    out_specs = (
        P(("stream", "dp"), None),
        P(("stream", "dp"), None),
        P("stream", None),
        P("stream", None),
        P("stream", None),
        P("stream", None),
        P("stream"),
        P("stream"),
        P("stream"),
        P("stream"),
        P("stream"),
        P("stream"),
        P("stream"),
        P("stream"),
    )
    return jax.shard_map(body, mesh=mesh, in_specs=in_specs, out_specs=out_specs, check_vma=False)
```

```python
import functools
import math

import jax
import jax.numpy as jnp
from jax import lax
from jax.experimental import pallas as pl
from jax.experimental.pallas import tpu as pltpu
from jax.sharding import PartitionSpec as P

D = 768
HEADS = 12
HEAD_DIM = 64
FF = 3072
SEQ = 512
GROUPS = 2
PART = D // GROUPS
PAIR = 2 * HEAD_DIM
BLOCK = 128
REACH = 96
ROWS = 256
MIB = 1024 * 1024

epsilon = 1e-05
masked_score = -1e30
score_scale = HEAD_DIM ** (-0.5)
gelu_scale = math.sqrt(2.0 / math.pi)
gelu_cubic = 0.044715

f32 = jnp.float32
bf16 = jnp.bfloat16

WINDOWS = [
    (max(0, start - REACH), min(SEQ, start + BLOCK + REACH)) for start in range(0, SEQ, BLOCK)
]
WINDOW = BLOCK + 2 * REACH

in_smem = pl.BlockSpec(memory_space=pltpu.SMEM)
in_vmem = pl.BlockSpec(memory_space=pltpu.VMEM)
in_any = pl.BlockSpec(memory_space=pl.ANY)


def shape_of(dims, dtype):
    return jax.ShapeDtypeStruct(dims, dtype)


def dot(left, right):
    return lax.dot_general(left, right, (((1,), (0,)), ((), ())), preferred_element_type=f32)


def dot_nt(left, right):
    return lax.dot_general(left, right, (((1,), (1,)), ((), ())), preferred_element_type=f32)


def dot_tn(left, right):
    return lax.dot_general(left, right, (((0,), (0,)), ((), ())), preferred_element_type=f32)


def normalise(values):
    average = jnp.mean(values, axis=-1, keepdims=True)
    centred = values - average
    spread = jnp.mean(centred * centred, axis=-1, keepdims=True)
    root = lax.rsqrt(spread + epsilon)
    return centred * root, root


def norm_back(scaled, root, gain, incoming):
    weighted = incoming * gain
    average = jnp.mean(weighted, axis=-1, keepdims=True)
    slope = jnp.mean(weighted * scaled, axis=-1, keepdims=True)
    return root * (weighted - average - scaled * slope)


def column_sums(values):
    return jnp.sum(values, axis=0, keepdims=True)


class Order:
    def __init__(self):
        self.token = []

    def call(
        self,
        kernel,
        args,
        in_specs,
        outs,
        out_specs,
        scratch=(),
        grid=(),
        limit=16,
        name=None,
        prefetch=None,
        waits=(),
        aliases=None,
        cost=0,
    ):
        given = len(args)
        extra = list(self.token) + list(waits)
        ahead = [] if prefetch is None else [prefetch]
        count = len(ahead)

        def wrapped(*refs):
            kernel(*refs[: count + given], *refs[count + given + len(extra) :])

        results = pl.pallas_call(
            wrapped,
            out_shape=outs,
            grid_spec=pltpu.PrefetchScalarGridSpec(
                num_scalar_prefetch=count,
                grid=grid,
                in_specs=list(in_specs) + [in_any] * len(extra),
                out_specs=out_specs,
                scratch_shapes=list(scratch),
            ),
            compiler_params=pltpu.CompilerParams(vmem_limit_bytes=limit * MIB),
            cost_estimate=pl.CostEstimate(flops=1 + cost * 10**9, bytes_accessed=1 + cost * MIB, transcendentals=cost * 10**6),
            input_output_aliases=aliases or {},
            name=name,
        )(*ahead, *args, *extra)
        self.token = [min(results, key=lambda out: out.size)]
        return results

    def hold(self, arrays, waits=()):
        return self.call(
            lambda *refs: None,
            arrays,
            [in_any] * len(arrays),
            [shape_of(array.shape, array.dtype) for array in arrays],
            [in_any] * len(arrays),
            name="hold",
            cost=0,
            waits=waits,
            aliases={k: k for k in range(len(arrays))},
        )

    def pause(self, value):
        return self.call(
            lambda *refs: None,
            [value],
            [in_any],
            [shape_of(value.shape, value.dtype)],
            [in_any],
            name="pause",
            cost=60,
            aliases={0: 0},
        )[0]


def assemble(places, parts, whole):
    rows = whole.shape[0] // len(parts)
    for k, part in enumerate(parts):
        whole[pl.ds(pl.multiple_of(places[k] * rows, 16), rows)] = part[:rows]


def sums_pass(order, places, folds=(), adds=(), pays=(), waits=(), extra=0):
    args, outs, steps = [], [], []

    def give(*arrays):
        args.extend(arrays)
        return list(range(len(args) - len(arrays), len(args)))

    def make(dims, dtype):
        outs.append(shape_of(dims, dtype))
        return len(outs) - 1

    for near, received, widths in folds:
        made = []
        for width in widths:
            rows = near.shape[1] if len(near.shape) == 3 else (near.shape[0] + 16) // 2
            made += [make((rows + add, width), near.dtype) for add in (0, extra)]
        steps.append(("fold", give(near, received), made))
    for left, right in adds:
        steps.append(("add", give(left, right), [make(left.shape, left.dtype)]))
    for mine, received, older, crossed in pays:
        given = give(mine, received, older, crossed)
        steps.append(("pay", given, [make(mine.shape, mine.dtype) for _ in range(2)]))
    count = len(args)

    def kernel(places_ref, *refs):
        ins, results = refs[:count], refs[count:]
        inner = jnp.logical_and(places_ref[4] > 0, places_ref[4] < 3)
        for kind, given, made in steps:
            if kind == "fold" and len(ins[given[0]].shape) == 3:
                first = 0
                for k in range(0, len(made), 2):
                    width = results[made[k]].shape[1]
                    part = slice(first, first + width)
                    for slot in range(2):
                        total = ins[given[0]][slot, :, part].astype(f32)
                        total += ins[given[1]][slot, :, part].astype(f32)
                        results[made[k + slot]][: total.shape[0]] = total.astype(bf16)
                    if extra:
                        results[made[k + 1]][total.shape[0] :] = jnp.zeros((extra, width), bf16)
                    first += width
            elif kind == "fold":
                total = (ins[given[0]][...].astype(f32) + ins[given[1]][...].astype(f32)).astype(bf16)
                rows = results[made[0]].shape[0] - 16
                for slot in range(2):
                    results[made[slot]][:rows] = total[slot * rows : (slot + 1) * rows]
                    results[made[slot]][rows:] = total[2 * rows :]
            elif kind == "add":
                rows = ins[given[0]].shape[0]
                total = ins[given[0]][...].astype(f32) + ins[given[1]][:rows].astype(f32)
                results[made[0]][...] = total.astype(results[made[0]].dtype)
            else:
                rows = ins[given[0]].shape[0]
                fresh = ins[given[0]][...].astype(f32) + ins[given[1]][:rows].astype(f32)
                older = ins[given[2]][...].astype(f32) + ins[given[3]][...].astype(f32)
                results[made[0]][...] = fresh.astype(results[made[0]].dtype)
                results[made[1]][...] = jnp.where(inner, older, fresh).astype(results[made[1]].dtype)

    found = order.call(
        kernel,
        [places, *args],
        [in_smem] + [in_vmem] * len(args),
        outs,
        [in_vmem] * len(outs),
        limit=12,
        name="sums",
        waits=waits,
    )
    found = list(found)
    return found[0] if len(found) == 1 else found


def first_cast_kernel(sizes, qkv, short, out, weight, rows, sem):
    copy = pltpu.make_async_copy(qkv, weight, sem)
    copy.start()
    rows[...] = jnp.zeros_like(rows)
    offset = 0
    for line, size in enumerate(sizes):
        rows[line : line + 1, :size] = short[:, offset : offset + size]
        offset += size
    height = weight.shape[0]
    out[height:] = rows[...].astype(bf16)
    copy.wait()
    out[:height] = weight[...].astype(bf16)


def first_cast_pass(order, qkv, members):
    return order.call(
        functools.partial(first_cast_kernel, [member.size for member in members]),
        [qkv, jnp.concatenate(members)[None]],
        [in_any, in_vmem],
        [shape_of((qkv.shape[0] + 16, 3 * D), bf16)],
        [in_vmem],
        scratch=[
            pltpu.VMEM(qkv.shape, f32),
            pltpu.VMEM((16, 3 * D), f32),
            pltpu.SemaphoreType.DMA,
        ],
        limit=16,
        name="first_cast",
    )[0]


def cast_kernel(places, left, right, down, wide_out, down_out, lead_out, half_out):
    wide_out[:, :D] = left[...].astype(bf16)
    wide_out[:, D:] = right[...].astype(bf16)
    down_out[...] = down[...].astype(bf16)
    lead_out[...] = wide_out[:, : lead_out.shape[1]]
    rows = left.shape[0]
    turn = places[4] % 2
    first = turn * 2 * rows
    for run in range(2):
        start = pl.multiple_of(first + run * rows, 16)
        half_out[:rows, run * D : (run + 1) * D] = down_out[pl.ds(start, rows)]
    start = pl.multiple_of(turn * (rows // 2), 16)
    half_out[rows:] = wide_out[pl.ds(start, rows // 2), D + FF // 2 :]


def cast_pass(order, places, left, right, down):
    rows = left.shape[0]
    return order.call(
        cast_kernel,
        [places, left, right, down],
        [in_smem] + [in_vmem] * 3,
        [
            shape_of((rows, D + FF), bf16),
            shape_of(down.shape, bf16),
            shape_of((rows, D + FF // 2), bf16),
            shape_of((rows + rows // 2, FF // 2), bf16),
        ],
        [in_vmem] * 4,
        limit=16,
        name="cast",
    )


def project_kernel(count, packed, places, rows, *rest):
    given, rest = ((), rest) if packed else (rest[:2], rest[2:])
    parts, rest = rest[:count], rest[count:]
    pair_outs, rest = rest[:GROUPS], rest[GROUPS:]
    query_out, normed_out, vectors_out, hidden_out, weight, wide_pair, last_pair, sems = rest
    pairs = [wide_pair.at[k] for k in range(GROUPS - 1)] + [last_pair]
    shard = D // count
    if packed:
        vectors = jnp.zeros((8, D), f32)
        line = lax.broadcasted_iota(jnp.int32, (8, D), 0)
        for k in range(count):
            block = parts[k][shard : shard + 16, :D].astype(f32)[:8]
            vectors += pltpu.roll(jnp.where(line < 7, block, 0.0), places[k] * shard, 1)
            start = pl.multiple_of(places[k] * D, 128)
            hidden_out[:, pl.ds(start, D)] = block[7:8]
    else:
        vectors = given[0][...]
        hidden_out[...] = given[1][...]
    vectors_out[...] = vectors
    assemble(places, parts, weight)
    scaled, _ = normalise(rows[...].astype(f32))
    normed_out[...] = (scaled * vectors[0:1] + vectors[1:2]).astype(bf16)

    def block(column):
        return dot(normed_out[...], weight[:, column : column + PART]).astype(bf16)

    for kind in range(2):
        line = vectors[6:7, kind * PART : (kind + 1) * PART]
        last_pair[kind, SEQ:] = jnp.concatenate([line] * 16, axis=0).astype(bf16)
    copies = []
    for group in range(GROUPS):
        for kind in range(2):
            pairs[group][kind, :SEQ] = block((kind + 1) * D + group * PART)
        copies.append(pltpu.make_async_copy(pairs[group], pair_outs[group], sems.at[group]))
        copies[-1].start()
    for first in range(0, D, PART):
        query_out[:, first : first + PART] = block(first)
    for copy in copies:
        copy.wait()


def project(order, places, rows, parts, given=(), waits=()):
    count = len(parts)
    outs = order.call(
        functools.partial(project_kernel, count, not given),
        [places, rows, *given, *parts],
        [in_smem] + [in_vmem] * (1 + len(given) + count),
        [shape_of((2, SEQ, PART), bf16)] * (GROUPS - 1)
        + [
            shape_of((2, SEQ + 16, PART), bf16),
            shape_of((SEQ, D), bf16),
            shape_of((SEQ, D), bf16),
            shape_of((8, D), f32),
            shape_of((1, FF), f32),
        ],
        [in_any] * GROUPS + [in_vmem] * 4,
        scratch=[
            pltpu.VMEM((D, 3 * D), bf16),
            pltpu.VMEM((GROUPS - 1, 2, SEQ, PART), bf16),
            pltpu.VMEM((2, SEQ + 16, PART), bf16),
            pltpu.SemaphoreType.DMA((GROUPS,)),
        ],
        limit=16,
        name="project",
        waits=waits,
    )
    return outs[:GROUPS], *outs[GROUPS:]


def fill_page_bias(page_row, page_column, bias):
    for index, (low, high) in enumerate(WINDOWS):
        start = index * BLOCK
        same = page_column[low:high] == page_row[:, start : start + BLOCK]
        bias[index, : high - low] = jnp.where(same, 0.0, masked_score)


def two_heads(block):
    lane = lax.broadcasted_iota(jnp.int32, block.shape, 1)
    zero = jnp.zeros_like(block)
    return jnp.concatenate(
        [jnp.where(lane < HEAD_DIM, block, zero), jnp.where(lane < HEAD_DIM, zero, block)], axis=0
    )


def head_rows(both):
    return jnp.concatenate([both[:HEAD_DIM, :BLOCK], both[HEAD_DIM:, BLOCK:]], axis=0).T


def page_bias(bias, index, size):
    block = bias[index, :size]
    return jnp.concatenate([block, block], axis=1)


def attend_kernel(
    query_first, query, own, other, page_row, page_column, context, log_total, bias
):
    fill_page_bias(page_row, page_column, bias)

    def pair(step, carry):
        lanes = pl.ds(pl.multiple_of(step * PAIR, PAIR), PAIR)
        query_lanes = pl.ds(pl.multiple_of((query_first + step) * PAIR, PAIR), PAIR)
        for index, (low, high) in enumerate(WINDOWS):
            start = index * BLOCK
            queries = two_heads(query[start : start + BLOCK, query_lanes] * score_scale)
            allowed = page_bias(bias, index, high - low)
            scores = dot_nt(own[0, low:high, lanes], queries) + allowed
            scores_two = dot_nt(other[0, low:high, lanes], queries) + allowed
            largest = jnp.maximum(
                jnp.max(scores, axis=0, keepdims=True), jnp.max(scores_two, axis=0, keepdims=True)
            )
            exponent = jnp.exp(scores - largest)
            exponent_two = jnp.exp(scores_two - largest)
            total = column_sums(exponent) + column_sums(exponent_two)
            inverse = 1.0 / total
            shares = (exponent * inverse).astype(bf16)
            shares_two = (exponent_two * inverse).astype(bf16)
            both = dot_tn(own[1, low:high, lanes], shares)
            both += dot_tn(other[1, low:high, lanes], shares_two)
            context[start : start + BLOCK, lanes] = head_rows(both).astype(bf16)
            log_total[step, index : index + 1] = largest + jnp.log(total)
        return carry

    lax.fori_loop(0, own.shape[2] // PAIR, pair, 0)


def attend(order, query_first, queries, own, other, page_row, page_column, waits=()):
    width = own.shape[2]
    return order.call(
        functools.partial(attend_kernel, query_first),
        [queries, own, other, page_row, page_column],
        [in_vmem] * 5,
        [
            shape_of((SEQ, width), bf16),
            shape_of((width // PAIR, len(WINDOWS), 2 * BLOCK), f32),
        ],
        [in_vmem] * 2,
        scratch=[pltpu.VMEM((len(WINDOWS), WINDOW, BLOCK), f32)],
        limit=12,
        name="attend",
        cost=60,
        waits=waits,
    )


def attend_back_kernel(
    query_first,
    query,
    own,
    other,
    context_grad,
    log_total,
    page_row,
    page_column,
    *rest,
):
    *given, query_grad, own_grad, other_grad, bias, other_sum = rest
    fill_page_bias(page_row, page_column, bias)
    own_grad[...] = jnp.zeros_like(own_grad)
    other_sum[...] = jnp.zeros_like(other_sum)

    def pair(step, carry):
        lanes = pl.ds(pl.multiple_of(step * PAIR, PAIR), PAIR)
        query_lanes = pl.ds(pl.multiple_of((query_first + step) * PAIR, PAIR), PAIR)
        for index, (low, high) in enumerate(WINDOWS):
            start = index * BLOCK
            queries = two_heads(query[start : start + BLOCK, query_lanes] * score_scale)
            grads = two_heads(context_grad[start : start + BLOCK, query_lanes])
            log_row = log_total[step, index : index + 1]
            allowed = page_bias(bias, index, high - low)
            keys, keys_two = own[0, low:high, lanes], other[0, low:high, lanes]
            shares = jnp.exp(dot_nt(keys, queries) + allowed - log_row)
            shares_two = jnp.exp(dot_nt(keys_two, queries) + allowed - log_row)
            share_grad = dot_nt(own[1, low:high, lanes], grads)
            share_grad_two = dot_nt(other[1, low:high, lanes], grads)
            centre = column_sums(shares * share_grad) + column_sums(shares_two * share_grad_two)
            score_grad = (shares * (share_grad - centre)).astype(bf16)
            score_grad_two = (shares_two * (share_grad_two - centre)).astype(bf16)
            own_grad[0, low:high, lanes] += dot(score_grad, queries)
            own_grad[1, low:high, lanes] += dot(shares.astype(bf16), grads)
            other_sum[0, low:high, lanes] += dot(score_grad_two, queries)
            other_sum[1, low:high, lanes] += dot(shares_two.astype(bf16), grads)
            both = dot_tn(keys, score_grad) + dot_tn(keys_two, score_grad_two)
            query_grad[start : start + BLOCK, lanes] = (head_rows(both) * score_scale).astype(bf16)
        return carry

    lax.fori_loop(0, own_grad.shape[2] // PAIR, pair, 0)
    other_grad[:, :SEQ] = other_sum[...].astype(bf16)
    if given:
        for kind in range(2):
            line = given[0][:, kind * PART : (kind + 1) * PART]
            other_grad[kind, SEQ:] = jnp.concatenate([line] * 2, axis=0).astype(bf16)


def attend_back(
    order, query_first, queries, own, other, context_grad, logs, page_row, page_column, given
):
    return order.call(
        functools.partial(attend_back_kernel, query_first),
        [queries, own, other, context_grad, logs, page_row, page_column, *given],
        [in_vmem] * (7 + len(given)),
        [
            shape_of((SEQ, PART), bf16),
            shape_of((2, SEQ, PART), f32),
            shape_of((2, SEQ + 16 * len(given), PART), bf16),
        ],
        [in_vmem] * 3,
        scratch=[
            pltpu.VMEM((len(WINDOWS), WINDOW, BLOCK), f32),
            pltpu.VMEM((2, SEQ, PART), f32),
        ],
        limit=16,
        name="attend_back",
        cost=60,
    )


def partner_cross(pair):
    rows = pair[:, SEQ:].astype(f32)
    return jnp.concatenate([rows[0, :1], rows[1, :1]], axis=1)


def join_blocks(places, wides, downs, leads, halves, wide, down):
    rows = wide.shape[0] // (len(wides) + len(leads))
    for k, part in enumerate(wides):
        wide[pl.ds(pl.multiple_of(places[k] * rows, 16), rows)] = part[...]
        down[k] = downs[k][...]
    turn = places[4] % 2
    for k, part in enumerate(leads):
        first = places[len(wides) + k] * rows
        wide[pl.ds(pl.multiple_of(first, 16), rows), : part.shape[1]] = part[...]
        for side, half in enumerate(halves[k]):
            place = turn if side == 0 else 1 - turn
            start = pl.multiple_of(first + place * (rows // 2), 16)
            wide[pl.ds(start, rows // 2), part.shape[1] :] = half[rows:]
            for run in range(2):
                start = pl.multiple_of((2 * place + run) * rows, 16)
                down[len(wides) + k, pl.ds(start, rows)] = half[:rows, run * D : (run + 1) * D]


def middle_kernel(kinds, places, rows, *rest):
    contexts, rest = rest[:GROUPS], rest[GROUPS:]
    (tangent, vectors, partner, hidden_bias), rest = rest[:4], rest[4:]
    wides, downs, leads = [], [], []
    for group, size in zip((wides, downs, leads), kinds):
        group += rest[:size]
        rest = rest[size:]
    halves = [rest[2 * k : 2 * k + 2] for k in range(kinds[2])]
    rest = rest[2 * kinds[2] :]
    middle_out, second_out, hidden_out, slope_out, modal_out, inner_out, wide, down, total = rest
    join_blocks(places, wides, downs, leads, halves, wide, down)
    count = down.shape[0]
    middle = rows[...].astype(f32)
    for group, context in enumerate(contexts):
        middle += dot(context[...], wide[group * PART : (group + 1) * PART, :D])
    middle_out[...] = middle
    scaled, _ = normalise(middle)
    second_out[...] = (scaled * vectors[2:3] + vectors[3:4]).astype(bf16)
    total[...] = middle + vectors[4:5]
    slot = FF // count
    size = 384
    for k in range(count):
        for first in range(0, slot, size):
            start = places[k] * slot + first
            part = pl.ds(pl.multiple_of(start, 128), size)
            column = pl.ds(pl.multiple_of(D + start, 128), size)
            upper = dot(second_out[...], wide[:, column]) + hidden_bias[:, part]
            square = upper * upper
            angle = jnp.tanh(upper * (gelu_scale + (gelu_cubic * gelu_scale) * square))
            half = 0.5 + 0.5 * angle
            hidden = (upper * half).astype(bf16)
            hidden_out[:, part] = hidden
            bend = 2.0 * gelu_scale + (6.0 * gelu_cubic * gelu_scale) * square
            slope_out[:, part] = (half + half * (1.0 - half) * (upper * bend)).astype(bf16)
            total[...] += dot(hidden, down[k, first : first + size])
    modal_out[...] = total[...].astype(bf16)
    modal = modal_out[...].astype(f32)
    own = jnp.sum(modal * vectors[5:6], axis=1, keepdims=True)
    cross = jnp.sum(modal * partner_cross(partner), axis=1, keepdims=True)
    met = jnp.sum(modal * tangent[...].astype(f32), axis=1, keepdims=True)
    lane = lax.broadcasted_iota(jnp.int32, (SEQ, 128), 1)
    columns = jnp.where(lane == 0, own, jnp.where(lane == 1, cross, met))
    inner_out[...] = columns.T[:8]


def middle_pass(
    order, places, rows, contexts, tangent, vectors, partner, hidden_bias, wides, downs, leads, halves
):
    count = len(wides) + len(leads)
    parts = [*wides, *downs, *leads] + [piece for pair in halves for piece in pair]
    return order.call(
        functools.partial(middle_kernel, (len(wides), len(downs), len(leads))),
        [places, rows, *contexts, tangent, vectors, partner, hidden_bias, *parts],
        [in_smem] + [in_vmem] * (5 + GROUPS + len(parts)),
        [
            shape_of((SEQ, D), f32),
            shape_of((SEQ, D), bf16),
            shape_of((SEQ, FF), bf16),
            shape_of((SEQ, FF), bf16),
            shape_of((SEQ, D), bf16),
            shape_of((8, SEQ), f32),
            shape_of((D, D + FF), bf16),
            shape_of((count, FF // count, D), bf16),
        ],
        [in_vmem] * 8,
        scratch=[pltpu.VMEM((SEQ, D), f32)],
        limit=16,
        name="middle",
    )


def gate_kernel(
    own,
    other,
    tangent,
    partner_tangent,
    vectors,
    partner,
    grad_out,
    low_out,
    columns_out,
    sums,
):
    gate = jax.nn.sigmoid(own[0:1] + other[1:2])
    gate_two = jax.nn.sigmoid(other[0:1] + own[1:2])
    logit = other[2:3] * gate * (1.0 - gate)
    logit_two = own[2:3] * gate_two * (1.0 - gate_two)
    padding = jnp.zeros((124, SEQ), f32)
    columns = jnp.concatenate([gate, logit, gate_two, logit_two, padding], axis=0).T
    columns_out[...] = columns
    grad = (
        tangent[...].astype(f32)
        + columns[:, 1:2] * vectors[5:6]
        + partner_tangent[...].astype(f32) * columns[:, 2:3]
        + columns[:, 3:4] * partner_cross(partner)
    )
    grad_out[...] = grad
    low_out[...] = grad.astype(bf16)
    sums[...] = column_sums(grad)


def gate_pass(order, own, other, tangent, partner_tangent, vectors, partner):
    return order.call(
        gate_kernel,
        [own, other, tangent, partner_tangent, vectors, partner],
        [in_vmem] * 6,
        [
            shape_of((SEQ, D), f32),
            shape_of((SEQ, D), bf16),
            shape_of((SEQ, 128), f32),
            shape_of((1, D), f32),
        ],
        [in_vmem] * 4,
        name="gate",
    )


def mix_kernel(own, other, columns, mixed):
    mixed[...] = (
        own[...].astype(f32) + columns[:, 0:1] * other[...].astype(f32)
    ).astype(bf16)


def mix_pass(order, own, other, columns):
    return order.call(
        mix_kernel,
        [own, other, columns],
        [in_vmem] * 3,
        [shape_of((SEQ, D), bf16)],
        [in_vmem],
        name="mix",
        cost=60,
    )[0]


def gate_sums_kernel(own, columns, out):
    rows = own[...].astype(f32)
    out[...] = jnp.zeros_like(out)
    out[0:1] = column_sums(columns[:, 1:2] * rows)
    out[1:2] = column_sums(columns[:, 3:4] * rows)


def gate_sums_pass(order, own, columns):
    return order.call(
        gate_sums_kernel, [own, columns], [in_vmem] * 2, [shape_of((8, D), f32)], [in_vmem], name="gate_sums"
    )[0]


def chain_kernel(widths, places, low, grad, slope, middle, vectors, wide, second, down, *rest):
    total_out, total_low_out, context_out, upper_sums, gain_sums, bias_sums = rest[:6]
    outs, (normed_grad, upper_out, whole) = rest[6:-3], rest[-3:]
    normed_grad[...] = jnp.zeros_like(normed_grad)
    count = down.shape[0]
    slot = FF // count
    size = 384
    for k in range(count):
        for first in range(0, slot, size):
            start = places[k] * slot + first
            part = pl.ds(pl.multiple_of(start, 128), size)
            column = pl.ds(pl.multiple_of(D + start, 128), size)
            upper = dot_nt(low[...], down[k, first : first + size]) * slope[:, part].astype(f32)
            upper_sums[:, part] = column_sums(upper)
            upper_low = upper.astype(bf16)
            upper_out[:, part] = upper_low
            normed_grad[...] += dot_nt(upper_low, wide[:, column])
    scaled, root = normalise(middle[...])
    incoming = normed_grad[...]
    gain_sums[...] = column_sums(incoming * scaled)
    bias_sums[...] = column_sums(incoming)
    total = grad[...] + norm_back(scaled, root, vectors[2:3], incoming)
    total_out[...] = total
    total_low_out[...] = total.astype(bf16)
    context_out[...] = dot_nt(total_low_out[...], wide[:, :D]).astype(bf16)
    turned = second[...].T
    products = [(turned, upper_out[:, k : k + 512]) for k in range(0, FF, 512)]
    store_blocks(places, count, products, widths, outs, whole)


def chain_pass(order, places, low, grad, slope, middle, vectors, wide, second, down, widths):
    count = down.shape[0]
    return order.call(
        functools.partial(chain_kernel, widths),
        [places, low, grad, slope, middle, vectors, wide, second, down],
        [in_smem] + [in_vmem] * 8,
        [
            shape_of((SEQ, D), f32),
            shape_of((SEQ, D), bf16),
            shape_of((SEQ, D), bf16),
            shape_of((1, FF), f32),
            shape_of((1, D), f32),
            shape_of((1, D), f32),
        ]
        + block_shapes(widths, count),
        [in_vmem] * (6 + len(block_shapes(widths, count))),
        scratch=[
            pltpu.VMEM((SEQ, D), f32),
            pltpu.VMEM((SEQ, FF), bf16),
            pltpu.VMEM((D, max(widths)), bf16),
        ],
        limit=20,
        name="chain",
    )


def slots_of(count):
    return (list(range(0, count, 2)), list(range(1, count, 2)))


def block_shapes(widths, count):
    near, far = slots_of(count)
    rows = D // count
    outs = []
    for width in widths:
        outs.append(shape_of((len(near), rows, width), bf16))
        if far:
            outs.append(shape_of((len(far), rows, width), bf16))
    return outs


def store_blocks(places, count, products, widths, outs, whole):
    near, far = slots_of(count)
    rows = D // count
    products = list(products)
    each = 2 if far else 1
    for index, width in enumerate(widths):
        low = 0
        while low < width:
            left, right = products.pop(0)
            whole[:, low : low + right.shape[1]] = dot(left, right).astype(bf16)
            low += right.shape[1]
        for out, slots in zip(outs[each * index : each * index + each], (near, far)):
            for place, slot in enumerate(slots):
                begin = pl.multiple_of(places[slot] * rows, 16)
                out[place] = whole[pl.ds(begin, rows), :width]


def lead_grads_kernel(count, places, context, context_two, low, normed, *rest):
    queries, (own, returned), rest = rest[:GROUPS], rest[GROUPS : GROUPS + 2], rest[GROUPS + 2 :]
    pair_low, outs, whole = rest[0], rest[1:-1], rest[-1]
    pair_low[...] = (own[...] + returned[:, :SEQ].astype(f32)).astype(bf16)
    turned = jnp.concatenate([context[...].T, context_two[...].T], axis=0)
    products = [(turned, low[:, k : k + PART]) for k in range(0, D, PART)]
    turned = normed[...].T
    products += [(turned, query[...]) for query in queries]
    products += [(turned, pair_low[kind]) for kind in range(2)]
    store_blocks(places, count, products, [3 * D], outs, whole)


def lead_grads(order, places, contexts, low, normed, queries, own, returned, count):
    outs = block_shapes([3 * D], count)
    args = [*contexts, low, normed, *queries, own, returned]
    return order.call(
        functools.partial(lead_grads_kernel, count),
        [places, *args],
        [in_smem] + [in_vmem] * len(args),
        [shape_of(own.shape, bf16)] + outs,
        [in_vmem] * (1 + len(outs)),
        scratch=[pltpu.VMEM((D, 3 * D), bf16)],
        limit=16,
        name="lead_grads",
    )


def down_grads_kernel(count, first, height, fold, places, low, hidden, *outs):
    near, far = slots_of(count)
    width = FF // count
    turned = low[:, first : first + height].T
    rows = height // fold
    for out, slots in zip(outs, (near, far)):
        for place, slot in enumerate(slots):
            begin = pl.multiple_of(places[slot] * width, 128)
            block = dot(turned, hidden[:, pl.ds(begin, width)]).astype(bf16)
            for k in range(fold):
                out[place, :, k * width : (k + 1) * width] = block[k * rows : (k + 1) * rows]


def down_grads(order, places, low, hidden, first, height, fold, count):
    near, far = slots_of(count)
    width = FF // count
    outs = [shape_of((len(near), height // fold, fold * width), bf16)]
    if far:
        outs.append(shape_of((len(far), height // fold, fold * width), bf16))
    return order.call(
        functools.partial(down_grads_kernel, count, first, height, fold),
        [places, low, hidden],
        [in_smem, in_vmem, in_vmem],
        outs,
        [in_vmem] * len(outs),
        limit=16,
        name="down_grads",
    )


def first_kernel(count, places, total, rows, vectors, normed, own, returned, *rest):
    parts, rest = rest[:count], rest[count:]
    queries, pair, rest = rest[:GROUPS], rest[GROUPS], rest[GROUPS + 1 :]
    gain_two, bias_two, output_bias, gate_own, hidden_bias = rest[:5]
    grad_out, outs = rest[5], rest[6:-5]
    pair_low, normed_grad, weight, whole, short = rest[-5:]
    pair_low[...] = (own[...] + returned[:, :SEQ].astype(f32)).astype(bf16)
    assemble(places, parts, weight)
    for group, pairs in enumerate((pair, pair_low)):
        start = group * PART
        block = dot_nt(queries[group][...], weight[:, start : start + PART])
        for kind in range(2):
            start = (kind + 1) * D + group * PART
            block += dot_nt(pairs[kind], weight[:, start : start + PART])
        if group == 0:
            normed_grad[...] = block
        else:
            normed_grad[...] += block
    scaled, root = normalise(rows[...].astype(f32))
    incoming = normed_grad[...]
    short[...] = jnp.zeros_like(short)
    short[0:1] = column_sums(incoming * scaled)
    short[1:2] = column_sums(incoming)
    for line, member in enumerate((gain_two, bias_two, output_bias)):
        short[line + 2 : line + 3] = member[...]
    short[5:6] = gate_own[0:1]
    for kind in range(2):
        line = returned[kind, SEQ : SEQ + 8].astype(f32)
        short[6:7, kind * PART : (kind + 1) * PART] = line[1:2]
    for line in range(FF // D):
        short[line + 8 : line + 9] = hidden_bias[:, line * D : (line + 1) * D]
    grad_out[...] = total[...] + norm_back(scaled, root, vectors[0:1], incoming)
    turned = normed[...].T
    for kind in range(2):
        whole[:, kind * PART : (kind + 1) * PART] = dot(turned, pair_low[kind]).astype(bf16)
    height = D // count
    for out, slots in zip(outs, slots_of(count)):
        for place, slot in enumerate(slots):
            begin = pl.multiple_of(places[slot] * height, 16)
            out[place * height : (place + 1) * height] = whole[pl.ds(begin, height)]
        out[len(slots) * height :] = short[...].astype(bf16)


def first_pass(
    order, places, total, rows, vectors, normed, own, returned, parts, queries, pair, short
):
    count = len(parts)
    args = [total, rows, vectors, normed, own, returned, *parts, *queries, pair, *short]
    outs = [
        shape_of((len(slots) * (D // count) + 16, 2 * PART), bf16) for slots in slots_of(count) if slots
    ]
    return order.call(
        functools.partial(first_kernel, count),
        [places, *args],
        [in_smem] + [in_vmem] * len(args),
        [shape_of((SEQ, D), f32)] + outs,
        [in_vmem] * (1 + len(outs)),
        scratch=[
            pltpu.VMEM((2, SEQ, PART), bf16),
            pltpu.VMEM((SEQ, D), f32),
            pltpu.VMEM((D, 3 * D), bf16),
            pltpu.VMEM((D, 2 * PART), bf16),
            pltpu.VMEM((16, D), f32),
        ],
        limit=20,
        name="first",
    )


def settle_kernel(kind, count, given, places, *refs):
    totals, returned, outs = refs[:count], refs[count : 2 * count], refs[2 * count + given :]
    inner = jnp.logical_and(places[4] > 0, places[4] < 3)
    values = [jnp.where(inner, a[...], b[...]).astype(f32) for a, b in zip(totals, returned)]
    out = outs[0]
    if kind == "turn":
        first = 0
        for value in values:
            rows = value.shape[0]
            for k in range(0, value.shape[1], D):
                out[:, first : first + rows] = value[:, k : k + D].T
                first += rows
    elif kind == "columns":
        first = 0
        for value in values:
            out[:, first : first + value.shape[1]] = value
            first += value.shape[1]
    elif kind == "halves":
        outs[1][...] = values[0][:, :D]
        out[...] = values[0][:, D:]
    else:
        out[:, :D] = refs[2 * count][...]
        rows = out.shape[0]
        for group, value in enumerate(values):
            for part in range(2):
                start = (part + 1) * D + group * PART
                out[:, start : start + PART] = value[:rows, part * PART : (part + 1) * PART]
        outs[1][...] = values[-1][rows:]


def settle(order, kind, places, blocks, dims, given=()):
    count = len(blocks)
    found = order.call(
        functools.partial(settle_kernel, kind, count, len(given)),
        [places] + [block[0] for block in blocks] + [block[1] for block in blocks] + list(given),
        [in_smem] + [in_vmem] * (2 * count + len(given)),
        [shape_of(each, f32) for each in dims],
        [in_vmem] * len(dims),
        name="settle",
    )
    return found[0] if len(dims) == 1 else found


def swap_bit(value, axis, bit):
    size = lax.axis_size(axis)
    return lax.ppermute(value, axis, [(source, source ^ (1 << bit)) for source in range(size)])


def from_partner(value):
    size = lax.axis_size("stream")
    half = size // 2
    return lax.ppermute(value, "stream", [(source, (source + half) % size) for source in range(size)])


def along(value, pairs):
    return lax.ppermute(value, "dp", pairs)


def up_line(value, steps):
    return along(value, [(floor, floor + 1) for floor in range(steps - 1, 3)])


def down_line(value, steps):
    return along(value, [(floor, floor - 1) for floor in range(1, 5 - steps)])


def swap_outer(value):
    return along(value, [(0, 1), (1, 0), (2, 3), (3, 2)])


def to_inner(value):
    return along(value, [(0, 1), (3, 2)])


def over_middle(value):
    return along(value, [(1, 2), (2, 1)])


def to_outer(value):
    return along(value, [(1, 0), (2, 3)])


def core(value):
    return swap_bit(value, "stream", 0)


def across(value):
    return swap_bit(value, "stream", 1)


def modality_groups():
    size = lax.axis_size("stream")
    half = size // 2
    return [list(range(half)), list(range(half, size))]


def body(
    regions,
    cotangent,
    page_lens,
    qkv_weight,
    out_weight,
    up_weight,
    down_weight,
    ln1_gain,
    ln1_bias,
    ln2_gain,
    ln2_bias,
    up_bias,
    down_bias,
    gate_own,
    gate_other,
):
    half = lax.axis_size("stream") // 2
    depth = lax.axis_size("dp")
    paired = half == 4 and depth == 4
    side = lax.axis_index("stream") % half
    floor = lax.axis_index("dp")
    count = 4 if paired else 1
    slots = jnp.arange(4, dtype=jnp.int32)
    picks = jnp.bitwise_xor(side.astype(jnp.int32), slots) if paired else jnp.zeros_like(slots)
    places = jnp.concatenate([picks, floor.astype(jnp.int32)[None]])
    order = Order()
    short = (ln1_gain, ln1_bias, ln2_gain, ln2_bias, down_bias, gate_own, gate_other, up_bias)
    partner_tangent = from_partner(cotangent)

    lengths = lax.dynamic_slice_in_dim(page_lens, side * depth + floor, 1, 0)
    positions = jnp.arange(SEQ, dtype=jnp.int32)
    page_ends = jnp.cumsum(lengths[0], dtype=jnp.int32)
    pages = jnp.sum((page_ends[:, None] <= positions[None, :]).astype(jnp.int32), axis=0)
    page_row, page_column = pages[None, :], pages[:, None]

    def attend_group(group, waits=()):
        context, log_total = attend(
            order,
            group * PART // PAIR,
            queries,
            own_pairs[group],
            other_pairs[group],
            page_row,
            page_column,
            waits,
        )
        contexts.append(context)
        logs.append(log_total)

    contexts, logs = [], []
    if paired:
        qkv_shard = first_cast_pass(order, qkv_weight, short)
        qkv_across, qkv_near = across(qkv_shard), core(qkv_shard)
        wide_shard, down_shard, lead, half_own = cast_pass(
            order, places, out_weight, up_weight, down_weight
        )
        wide_near, down_near = core(wide_shard), core(down_shard)
        (qkv_across,) = order.hold([qkv_across], waits=[partner_tangent, qkv_near])
        qkv_far, half_own = core(qkv_across), across(half_own)
        qkv_parts = [qkv_shard, qkv_near, qkv_across, qkv_far]
        own_pairs, queries, normed, vectors, hidden_bias = project(
            order, places, regions, qkv_parts, waits=[wide_near, down_near]
        )
        other_pairs = [from_partner(pair) for pair in own_pairs]
        lead_across = across(lead)
        (half_own,) = order.hold([half_own])
        half_other, half_own_far = swap_outer(half_own), core(half_own)
        attend_group(0)
        (lead_across,) = order.hold([lead_across])
        vectors = order.pause(vectors)
        (half_other,) = order.hold([half_other])
        half_other_far, lead_far = core(half_other), core(lead_across)
        attend_group(1)
        wides, downs = [wide_shard, wide_near], [down_shard, down_near]
        leads = [lead_across, lead_far]
        halves = [(half_own, half_other), (half_own_far, half_other_far)]
    else:

        def gather(shard):
            return [
                lax.all_gather(shard, "stream", axis_index_groups=modality_groups(), tiled=True)
            ]

        packed = jnp.concatenate([member.astype(bf16) for member in short])[None]
        found = gather(packed)[0].astype(f32)
        shard = D // half
        rows = [found[:, k * shard : (k + 1) * shard].reshape(1, D) for k in range(7)]
        given = (
            jnp.concatenate(rows + [jnp.zeros((1, D), f32)], axis=0),
            found[:, 7 * shard :].reshape(1, FF),
        )
        qkv_parts = gather(qkv_weight.astype(bf16))
        wides = gather(jnp.concatenate([out_weight, up_weight], axis=1).astype(bf16))
        downs, leads, halves = gather(down_weight.astype(bf16)), [], []
        own_pairs, queries, normed, vectors, hidden_bias = project(
            order, places, regions, qkv_parts, given
        )
        other_pairs = [from_partner(pair) for pair in own_pairs]
        for group in range(GROUPS):
            attend_group(group)

    middle, second, hidden, slope, modal, inner_own, wide, down = middle_pass(
        order,
        places,
        regions,
        contexts,
        partner_tangent,
        vectors,
        other_pairs[-1],
        hidden_bias,
        wides,
        downs,
        leads,
        halves,
    )
    inner_other = from_partner(inner_own)
    modal_grad, modal_low, columns, output_bias_grad = gate_pass(
        order, inner_own, inner_other, cotangent, partner_tangent, vectors, other_pairs[-1]
    )

    def attend_back_group(group):
        query_grad, own_grad, other_grad = attend_back(
            order,
            group * PART // PAIR,
            queries,
            own_pairs[group],
            other_pairs[group],
            context_grad,
            logs[group],
            page_row,
            page_column,
            [gate_sums] if group == GROUPS - 1 else [],
        )
        query_grads.append(query_grad)
        own_grads.append(own_grad)
        returned.append(from_partner(other_grad))

    def last_pass(pair_low):
        short_grads = (
            gain_two_grad,
            bias_two_grad,
            output_bias_grad,
            gate_sums,
            hidden_bias_grad,
        )
        return first_pass(
            order,
            places,
            middle_grad,
            regions,
            vectors,
            normed,
            own_grads[1],
            returned[1],
            qkv_parts,
            query_grads,
            pair_low,
            short_grads,
        )

    query_grads, own_grads, returned = [], [], []
    back = (order, places, modal_low, modal_grad, slope, middle, vectors, wide, second, down)
    if paired:
        d1, far = down_grads(order, places, modal_low, hidden, 0, 384, 2, count)
        d1_core = core(far)
        d2, far = down_grads(order, places, modal_low, hidden, 384, 384, 2, count)
        d2_core = core(far)
        d1, away = sums_pass(order, places, folds=[(d1, d1_core, [FF // 2])])
        d1_in = across(away)
        d2, away = sums_pass(order, places, folds=[(d2, d2_core, [FF // 2])])
        d2_in = across(away)
        middle_grad, middle_low, context_grad, *rest = chain_pass(*back, [FF // 2, FF // 2])
        hidden_bias_grad, gain_two_grad, bias_two_grad, u1, far_one, u2, far_two = rest
        d1 = sums_pass(order, places, adds=[(d1, d1_in)])
        d1_in = to_inner(d1)
        u1_core, u2_core = core(far_one), core(far_two)
        columns = order.pause(columns)
        u1, away = sums_pass(order, places, folds=[(u1, u1_core, [FF // 2])], extra=16)
        u1_in = across(away)
        gate_sums = gate_sums_pass(order, modal, columns)
        attend_back_group(0)
        d2, d1 = sums_pass(order, places, adds=[(d2, d2_in), (d1, d1_in)])
        d2_in, d1_mid = to_inner(d2), over_middle(d1)
        u2, away = sums_pass(order, places, folds=[(u2, u2_core, [FF // 2])])
        attend_back_group(1)
        d2, u1, u1_pay = sums_pass(
            order, places, adds=[(d2, d2_in)], pays=[(u1, u1_in, d1, d1_mid)]
        )
        u1_in, d2_mid = swap_outer(u1_pay), over_middle(d2)
        (away,) = order.hold([away])
        u2_in = across(away)
        pair_low, lead_near, lead_far = lead_grads(
            order, places, contexts, middle_low, normed, query_grads, own_grads[0], returned[0], count
        )
        lead_core = core(lead_far)
        u1, u2, u2_pay = sums_pass(
            order, places, adds=[(u1, u1_in)], pays=[(u2, u2_in, d2, d2_mid)]
        )
        d1_out = u1_in
        u2_in, u1_mid = swap_outer(u2_pay), over_middle(u1)
        gate_sums = order.pause(gate_sums)
        oq, away, p1, away_two = sums_pass(
            order, places, folds=[(lead_near, lead_core, [2 * D, D])]
        )
        oq_in, p1_in = across(away), across(away_two)
        region_grad, last_near, last_far = last_pass(pair_low)
        last_core = core(last_far)
        u2, oq, oq_pay = sums_pass(
            order, places, adds=[(u2, u2_in)], pays=[(oq, oq_in, u1, u1_mid)]
        )
        d2_out = u2_in
        oq_in, u2_mid = swap_outer(oq_pay), over_middle(u2)
        modal = order.pause(modal)
        p2, away = sums_pass(order, places, folds=[(last_near, last_core, [D])])
        p2_in = across(away)
        down_grad = settle(order, "turn", places, [(u1_pay, d1_out), (u2_pay, d2_out)], [(D, D)])
        oq, u2, p1 = sums_pass(
            order, places, adds=[(oq, oq_in), (u2, u2_mid), (p1, p1_in)]
        )
        u1_out = oq_in
        oq_mid, u2_out, p1_in = over_middle(oq), to_outer(u2), to_inner(p1)
        p2 = sums_pass(order, places, adds=[(p2, p2_in)])
        p2_in = to_inner(p2)
        p1 = sums_pass(order, places, adds=[(p1, p1_in)])
        p1_mid = over_middle(p1)
        (modal,) = order.hold([modal])
        partner_modal = from_partner(modal)
        oq, p2 = sums_pass(order, places, adds=[(oq, oq_mid), (p2, p2_in)], waits=[u2_out])
        oq_out, p2_mid = to_outer(oq), over_middle(p2)
        up_grad = settle(order, "columns", places, [(oq_pay, u1_out), (u2, u2_out)], [(D // 4, FF)])
        p1 = sums_pass(order, places, adds=[(p1, p1_mid)])
        p1_out = to_outer(p1)
        p2 = sums_pass(order, places, adds=[(p2, p2_mid)])
        p2_out = to_outer(p2)
        query_grad, out_grad = settle(order, "halves", places, [(oq, oq_out)], [(D // 4, D)] * 2)
        mixed_rows = mix_pass(order, modal, partner_modal, columns)
        qkv_grad, short_rows = settle(
            order,
            "pairs",
            places,
            [(p1, p1_out), (p2, p2_out)],
            [(D // 4, 3 * D), (16, D)],
            [query_grad],
        )
    else:
        (down_block,) = down_grads(order, places, modal_low, hidden, 0, D, 1, count)
        middle_grad, middle_low, context_grad, *rest = chain_pass(*back, [FF])
        hidden_bias_grad, gain_two_grad, bias_two_grad, up_block = rest
        gate_sums = gate_sums_pass(order, modal, columns)
        for group in range(GROUPS):
            attend_back_group(group)
        mixed_rows = mix_pass(order, modal, from_partner(modal), columns)
        pair_low, lead_block = lead_grads(
            order, places, contexts, middle_low, normed, query_grads, own_grads[0], returned[0], count
        )
        region_grad, last_block = last_pass(pair_low)
        lead_block = lead_block[0]
        short_rows = last_block[D:].astype(f32)

        def total(block):
            groups = modality_groups()
            owned = lax.psum_scatter(
                block.astype(f32), "stream", axis_index_groups=groups, tiled=True
            )
            return lax.psum(owned, "dp")

        down_grad = total(down_block[0].T)
        up_grad, out_grad = total(up_block[0]), total(lead_block[:, :D])
        qkv_grad = total(
            jnp.concatenate(
                [
                    lead_block[:, D : 2 * D + PART],
                    last_block[:D, :PART],
                    lead_block[:, 2 * D + PART :],
                    last_block[:D, PART:],
                ],
                axis=1,
            )
        )
        short_rows = lax.psum(
            lax.psum(short_rows, "stream", axis_index_groups=modality_groups()), "dp"
        )

    shard = D // half
    own_rows = lax.dynamic_slice_in_dim(short_rows, side * shard, shard, 1)
    hidden_rows = short_rows[8 : 8 + FF // D].reshape(FF)
    own_hidden = lax.dynamic_slice_in_dim(hidden_rows, side * (FF // half), FF // half, 0)
    return (
        mixed_rows,
        region_grad,
        qkv_grad,
        out_grad,
        up_grad,
        down_grad,
        own_rows[0],
        own_rows[1],
        own_rows[2],
        own_rows[3],
        own_hidden,
        own_rows[4],
        own_rows[5],
        own_rows[6],
    )


def solution(mesh):
    in_specs = (
        P(("stream", "dp"), None),
        P(("stream", "dp"), None),
        P(),
        P("stream", None),
        P("stream", None),
        P("stream", None),
        P("stream", None),
        P("stream"),
        P("stream"),
        P("stream"),
        P("stream"),
        P("stream"),
        P("stream"),
        P("stream"),
        P("stream"),
    )
    out_specs = (
        P(("stream", "dp"), None),
        P(("stream", "dp"), None),
        P("stream", None),
        P("stream", None),
        P("stream", None),
        P("stream", None),
        P("stream"),
        P("stream"),
        P("stream"),
        P("stream"),
        P("stream"),
        P("stream"),
        P("stream"),
        P("stream"),
    )
    return jax.shard_map(body, mesh=mesh, in_specs=in_specs, out_specs=out_specs, check_vma=False)
```

```python
import functools
import math

import jax
import jax.numpy as jnp
from jax import lax
from jax.experimental import pallas as pl
from jax.experimental.pallas import tpu as pltpu
from jax.sharding import PartitionSpec as P

D = 768
HEADS = 12
HEAD_DIM = 64
FF = 3072
SEQ = 512
GROUPS = 2
PART = D // GROUPS
PAIR = 2 * HEAD_DIM
BLOCK = 128
REACH = 96
ROWS = 256
MIB = 1024 * 1024

epsilon = 1e-05
masked_score = -1e30
score_scale = HEAD_DIM ** (-0.5)
gelu_scale = math.sqrt(2.0 / math.pi)
gelu_cubic = 0.044715

f32 = jnp.float32
bf16 = jnp.bfloat16

WINDOWS = [
    (max(0, start - REACH), min(SEQ, start + BLOCK + REACH)) for start in range(0, SEQ, BLOCK)
]
WINDOW = BLOCK + 2 * REACH

in_smem = pl.BlockSpec(memory_space=pltpu.SMEM)
in_vmem = pl.BlockSpec(memory_space=pltpu.VMEM)
in_any = pl.BlockSpec(memory_space=pl.ANY)
in_hbm = pl.BlockSpec(memory_space=pltpu.HBM)


def shape_of(dims, dtype):
    return jax.ShapeDtypeStruct(dims, dtype)


def dot(left, right):
    return lax.dot_general(left, right, (((1,), (0,)), ((), ())), preferred_element_type=f32)


def dot_nt(left, right):
    return lax.dot_general(left, right, (((1,), (1,)), ((), ())), preferred_element_type=f32)


def dot_tn(left, right):
    return lax.dot_general(left, right, (((0,), (0,)), ((), ())), preferred_element_type=f32)


def normalise(values):
    average = jnp.mean(values, axis=-1, keepdims=True)
    centred = values - average
    spread = jnp.mean(centred * centred, axis=-1, keepdims=True)
    root = lax.rsqrt(spread + epsilon)
    return centred * root, root


def norm_back(scaled, root, gain, incoming):
    weighted = incoming * gain
    average = jnp.mean(weighted, axis=-1, keepdims=True)
    slope = jnp.mean(weighted * scaled, axis=-1, keepdims=True)
    return root * (weighted - average - scaled * slope)


def column_sums(values):
    return jnp.sum(values, axis=0, keepdims=True)


class Order:
    def __init__(self):
        self.token = []

    def call(
        self,
        kernel,
        args,
        in_specs,
        outs,
        out_specs,
        scratch=(),
        grid=(),
        limit=16,
        name=None,
        prefetch=None,
        waits=(),
        aliases=None,
        cost=0,
    ):
        given = len(args)
        extra = list(self.token) + list(waits)
        ahead = [] if prefetch is None else [prefetch]
        count = len(ahead)
        smallest = min(math.prod(out.shape) for out in outs)
        marked = smallest > 4096 and not aliases
        outs, out_specs = list(outs), list(out_specs)
        if marked:
            outs.append(shape_of((8, 128), f32))
            out_specs.append(in_vmem)
        place = count + given + len(extra) + len(outs) - 1

        def wrapped(*refs):
            used = list(refs[: count + given]) + list(refs[count + given + len(extra) :])
            if marked:
                refs[place][...] = jnp.zeros((8, 128), f32)
                used.pop(count + given + len(outs) - 1)
            kernel(*used)

        results = pl.pallas_call(
            wrapped,
            out_shape=outs,
            grid_spec=pltpu.PrefetchScalarGridSpec(
                num_scalar_prefetch=count,
                grid=grid,
                in_specs=list(in_specs) + [in_any] * len(extra),
                out_specs=out_specs,
                scratch_shapes=list(scratch),
            ),
            compiler_params=pltpu.CompilerParams(vmem_limit_bytes=limit * MIB),
            cost_estimate=pl.CostEstimate(flops=1 + cost * 10**9, bytes_accessed=1 + cost * MIB, transcendentals=cost * 10**6),
            input_output_aliases=aliases or {},
            name=name,
        )(*ahead, *args, *extra)
        self.token = [min(results, key=lambda out: out.size)]
        return list(results)[:-1] if marked else results

    def hold(self, arrays, waits=()):
        return self.call(
            lambda *refs: None,
            arrays,
            [in_any] * len(arrays),
            [shape_of(array.shape, array.dtype) for array in arrays],
            [in_any] * len(arrays),
            name="hold",
            cost=0,
            waits=waits,
            aliases={k: k for k in range(len(arrays))},
        )

    def pause(self, value):
        return self.call(
            lambda *refs: None,
            [value],
            [in_any],
            [shape_of(value.shape, value.dtype)],
            [in_any],
            name="pause",
            cost=60,
            aliases={0: 0},
        )[0]


def assemble(places, parts, whole):
    rows = whole.shape[0] // len(parts)
    for k, part in enumerate(parts):
        whole[pl.ds(pl.multiple_of(places[k] * rows, 16), rows)] = part[:rows]


def sums_pass(order, places, folds=(), adds=(), pays=(), waits=(), extra=0):
    args, outs, steps = [], [], []

    def give(*arrays):
        args.extend(arrays)
        return list(range(len(args) - len(arrays), len(args)))

    def make(dims, dtype):
        outs.append(shape_of(dims, dtype))
        return len(outs) - 1

    for near, received, widths in folds:
        made = []
        for width in widths:
            rows = near.shape[1] if len(near.shape) == 3 else (near.shape[0] + 16) // 2
            made += [make((rows + add, width), near.dtype) for add in (0, extra)]
        steps.append(("fold", give(near, received), made))
    for left, right in adds:
        steps.append(("add", give(left, right), [make(left.shape, left.dtype)]))
    for mine, received, older, crossed in pays:
        given = give(mine, received, older, crossed)
        steps.append(("pay", given, [make(mine.shape, mine.dtype) for _ in range(2)]))
    count = len(args)

    def kernel(places_ref, *refs):
        ins, results = refs[:count], refs[count:]
        inner = jnp.logical_and(places_ref[4] > 0, places_ref[4] < 3)
        for kind, given, made in steps:
            if kind == "fold" and len(ins[given[0]].shape) == 3:
                first = 0
                for k in range(0, len(made), 2):
                    width = results[made[k]].shape[1]
                    part = slice(first, first + width)
                    for slot in range(2):
                        total = ins[given[0]][slot, :, part].astype(f32)
                        total += ins[given[1]][slot, :, part].astype(f32)
                        results[made[k + slot]][: total.shape[0]] = total.astype(bf16)
                    if extra:
                        results[made[k + 1]][total.shape[0] :] = jnp.zeros((extra, width), bf16)
                    first += width
            elif kind == "fold":
                total = (ins[given[0]][...].astype(f32) + ins[given[1]][...].astype(f32)).astype(bf16)
                rows = results[made[0]].shape[0] - 16
                for slot in range(2):
                    results[made[slot]][:rows] = total[slot * rows : (slot + 1) * rows]
                    results[made[slot]][rows:] = total[2 * rows :]
            elif kind == "add":
                rows = ins[given[0]].shape[0]
                total = ins[given[0]][...].astype(f32) + ins[given[1]][:rows].astype(f32)
                results[made[0]][...] = total.astype(results[made[0]].dtype)
            else:
                rows = ins[given[0]].shape[0]
                fresh = ins[given[0]][...].astype(f32) + ins[given[1]][:rows].astype(f32)
                older = ins[given[2]][...].astype(f32) + ins[given[3]][...].astype(f32)
                results[made[0]][...] = fresh.astype(results[made[0]].dtype)
                results[made[1]][...] = jnp.where(inner, older, fresh).astype(results[made[1]].dtype)

    found = order.call(
        kernel,
        [places, *args],
        [in_smem] + [in_vmem] * len(args),
        outs,
        [in_vmem] * len(outs),
        limit=12,
        name="sums",
        waits=waits,
    )
    found = list(found)
    return found[0] if len(found) == 1 else found


def first_cast_kernel(sizes, qkv, short, out, weight, rows, sem):
    copy = pltpu.make_async_copy(qkv, weight, sem)
    copy.start()
    rows[...] = jnp.zeros_like(rows)
    offset = 0
    for line, size in enumerate(sizes):
        rows[line : line + 1, :size] = short[:, offset : offset + size]
        offset += size
    height = weight.shape[0]
    out[height:] = rows[...].astype(bf16)
    copy.wait()
    out[:height] = weight[...].astype(bf16)


def first_cast_pass(order, qkv, members):
    return order.call(
        functools.partial(first_cast_kernel, [member.size for member in members]),
        [qkv, jnp.concatenate(members)[None]],
        [in_hbm, in_vmem],
        [shape_of((qkv.shape[0] + 16, 3 * D), bf16)],
        [in_vmem],
        scratch=[
            pltpu.VMEM(qkv.shape, f32),
            pltpu.VMEM((16, 3 * D), f32),
            pltpu.SemaphoreType.DMA,
        ],
        limit=16,
        name="first_cast",
    )[0]


def cast_kernel(
    places,
    lengths,
    left,
    right,
    down,
    wide_out,
    down_out,
    lead_out,
    half_out,
    row_out,
    column_out,
):
    wide_out[:, :D] = left[...].astype(bf16)
    wide_out[:, D:] = right[...].astype(bf16)
    down_out[...] = down[...].astype(bf16)
    lead_out[...] = wide_out[:, : lead_out.shape[1]]
    rows = left.shape[0]
    turn = places[4] % 2
    first = turn * 2 * rows
    for run in range(2):
        start = pl.multiple_of(first + run * rows, 16)
        half_out[:rows, run * D : (run + 1) * D] = down_out[pl.ds(start, rows)]
    start = pl.multiple_of(turn * (rows // 2), 16)
    half_out[rows:] = wide_out[pl.ds(start, rows // 2), D + FF // 2 :]
    pack = places[0] * 4 + places[4]
    row_places = lax.broadcasted_iota(jnp.int32, (1, SEQ), 1)
    column_places = lax.broadcasted_iota(jnp.int32, (SEQ, 1), 0)
    page_row, page_column = jnp.zeros_like(row_places), jnp.zeros_like(column_places)
    end = jnp.int32(0)
    for page in range(lengths.shape[1]):
        end += lengths[pack, page]
        page_row += (row_places >= end).astype(jnp.int32)
        page_column += (column_places >= end).astype(jnp.int32)
    row_out[...] = page_row
    column_out[...] = page_column


def cast_pass(order, places, lengths, left, right, down):
    rows = left.shape[0]
    return order.call(
        cast_kernel,
        [places, lengths, left, right, down],
        [in_smem] * 2 + [in_vmem] * 3,
        [
            shape_of((rows, D + FF), bf16),
            shape_of(down.shape, bf16),
            shape_of((rows, D + FF // 2), bf16),
            shape_of((rows + rows // 2, FF // 2), bf16),
            shape_of((1, SEQ), jnp.int32),
            shape_of((SEQ, 1), jnp.int32),
        ],
        [in_vmem] * 6,
        limit=16,
        name="cast",
    )


def project_kernel(count, packed, places, rows, *rest):
    given, rest = ((), rest) if packed else (rest[:2], rest[2:])
    parts, rest = rest[:count], rest[count:]
    pair_outs, rest = rest[:GROUPS], rest[GROUPS:]
    query_out, normed_out, vectors_out, hidden_out, weight, wide_pair, last_pair, query, low, sems = rest
    pairs = [wide_pair.at[k] for k in range(GROUPS - 1)] + [last_pair]
    shard = D // count
    if packed:
        vectors = jnp.zeros((8, D), f32)
        line = lax.broadcasted_iota(jnp.int32, (8, D), 0)
        for k in range(count):
            block = parts[k][shard : shard + 16, :D].astype(f32)[:8]
            vectors += pltpu.roll(jnp.where(line < 7, block, 0.0), places[k] * shard, 1)
            start = pl.multiple_of(places[k] * D, 128)
            hidden_out[:, pl.ds(start, D)] = block[7:8]
    else:
        vectors = given[0][...]
        hidden_out[...] = given[1][...]
    vectors_out[...] = vectors
    assemble(places, parts, weight)
    scaled, _ = normalise(rows[...].astype(f32))
    low[...] = (scaled * vectors[0:1] + vectors[1:2]).astype(bf16)
    copies = [pltpu.make_async_copy(low, normed_out, sems.at[GROUPS])]
    copies[0].start()

    def block(column):
        return dot(low[...], weight[:, column : column + PART]).astype(bf16)

    for kind in range(2):
        line = vectors[6:7, kind * PART : (kind + 1) * PART]
        last_pair[kind, SEQ:] = jnp.concatenate([line] * 16, axis=0).astype(bf16)
    for group in range(GROUPS):
        for kind in range(2):
            pairs[group][kind, :SEQ] = block((kind + 1) * D + group * PART)
        copies.append(pltpu.make_async_copy(pairs[group], pair_outs[group], sems.at[group]))
        copies[-1].start()
    for index, first in enumerate(range(0, D, PART)):
        part = pl.ds(first, PART)
        query[:, part] = block(first)
        sem = sems.at[GROUPS + 1 + index]
        copies.append(pltpu.make_async_copy(query.at[:, part], query_out.at[:, part], sem))
        copies[-1].start()
    for copy in copies:
        copy.wait()


def project(order, places, rows, parts, given=(), waits=()):
    count = len(parts)
    outs = order.call(
        functools.partial(project_kernel, count, not given),
        [places, rows, *given, *parts],
        [in_smem] + [in_vmem] * (1 + len(given) + count),
        [shape_of((2, SEQ, PART), bf16)] * (GROUPS - 1)
        + [
            shape_of((2, SEQ + 16, PART), bf16),
            shape_of((SEQ, D), bf16),
            shape_of((SEQ, D), bf16),
            shape_of((8, D), f32),
            shape_of((1, FF), f32),
        ],
        [in_hbm] * (GROUPS + 2) + [in_vmem] * 2,
        scratch=[
            pltpu.VMEM((D, 3 * D), bf16),
            pltpu.VMEM((GROUPS - 1, 2, SEQ, PART), bf16),
            pltpu.VMEM((2, SEQ + 16, PART), bf16),
            pltpu.VMEM((SEQ, D), bf16),
            pltpu.VMEM((SEQ, D), bf16),
            pltpu.SemaphoreType.DMA((2 * GROUPS + 1,)),
        ],
        limit=16,
        name="project",
        waits=waits,
    )
    return outs[:GROUPS], *outs[GROUPS:]


def fill_page_bias(page_row, page_column, bias):
    for index, (low, high) in enumerate(WINDOWS):
        start = index * BLOCK
        same = page_column[low:high] == page_row[:, start : start + BLOCK]
        bias[index, : high - low] = jnp.where(same, 0.0, masked_score)


def two_heads(block):
    lane = lax.broadcasted_iota(jnp.int32, block.shape, 1)
    zero = jnp.zeros_like(block)
    return jnp.concatenate(
        [jnp.where(lane < HEAD_DIM, block, zero), jnp.where(lane < HEAD_DIM, zero, block)], axis=0
    )


def head_rows(both):
    return jnp.concatenate([both[:HEAD_DIM, :BLOCK], both[HEAD_DIM:, BLOCK:]], axis=0).T


def page_bias(bias, index, size):
    block = bias[index, :size]
    return jnp.concatenate([block, block], axis=1)


def attend_kernel(
    query_first, query, own, other, page_row, page_column, context, log_total, bias
):
    fill_page_bias(page_row, page_column, bias)

    def pair(step, carry):
        lanes = pl.ds(pl.multiple_of(step * PAIR, PAIR), PAIR)
        query_lanes = pl.ds(pl.multiple_of((query_first + step) * PAIR, PAIR), PAIR)
        for index, (low, high) in enumerate(WINDOWS):
            start = index * BLOCK
            queries = two_heads(query[start : start + BLOCK, query_lanes] * score_scale)
            allowed = page_bias(bias, index, high - low)
            scores = dot_nt(own[0, low:high, lanes], queries) + allowed
            scores_two = dot_nt(other[0, low:high, lanes], queries) + allowed
            largest = jnp.maximum(
                jnp.max(scores, axis=0, keepdims=True), jnp.max(scores_two, axis=0, keepdims=True)
            )
            exponent = jnp.exp(scores - largest)
            exponent_two = jnp.exp(scores_two - largest)
            total = column_sums(exponent) + column_sums(exponent_two)
            inverse = 1.0 / total
            shares = (exponent * inverse).astype(bf16)
            shares_two = (exponent_two * inverse).astype(bf16)
            both = dot_tn(own[1, low:high, lanes], shares)
            both += dot_tn(other[1, low:high, lanes], shares_two)
            context[start : start + BLOCK, lanes] = head_rows(both).astype(bf16)
            log_total[step, index : index + 1] = largest + jnp.log(total)
        return carry

    lax.fori_loop(0, own.shape[2] // PAIR, pair, 0)


def attend(order, query_first, queries, own, other, page_row, page_column, waits=()):
    width = own.shape[2]
    return order.call(
        functools.partial(attend_kernel, query_first),
        [queries, own, other, page_row, page_column],
        [in_vmem] * 5,
        [
            shape_of((SEQ, width), bf16),
            shape_of((width // PAIR, len(WINDOWS), 2 * BLOCK), f32),
        ],
        [in_vmem] * 2,
        scratch=[pltpu.VMEM((len(WINDOWS), WINDOW, BLOCK), f32)],
        limit=12,
        name="attend",
        cost=60,
        waits=waits,
    )


def attend_back_kernel(
    query_first,
    query,
    own,
    other,
    context_grad,
    log_total,
    page_row,
    page_column,
    *rest,
):
    *given, query_grad, own_grad, other_grad, bias, other_sum = rest
    fill_page_bias(page_row, page_column, bias)
    own_grad[...] = jnp.zeros_like(own_grad)
    other_sum[...] = jnp.zeros_like(other_sum)

    def pair(step, carry):
        lanes = pl.ds(pl.multiple_of(step * PAIR, PAIR), PAIR)
        query_lanes = pl.ds(pl.multiple_of((query_first + step) * PAIR, PAIR), PAIR)
        for index, (low, high) in enumerate(WINDOWS):
            start = index * BLOCK
            queries = two_heads(query[start : start + BLOCK, query_lanes] * score_scale)
            grads = two_heads(context_grad[start : start + BLOCK, query_lanes])
            log_row = log_total[step, index : index + 1]
            allowed = page_bias(bias, index, high - low)
            keys, keys_two = own[0, low:high, lanes], other[0, low:high, lanes]
            shares = jnp.exp(dot_nt(keys, queries) + allowed - log_row)
            shares_two = jnp.exp(dot_nt(keys_two, queries) + allowed - log_row)
            share_grad = dot_nt(own[1, low:high, lanes], grads)
            share_grad_two = dot_nt(other[1, low:high, lanes], grads)
            centre = column_sums(shares * share_grad) + column_sums(shares_two * share_grad_two)
            score_grad = (shares * (share_grad - centre)).astype(bf16)
            score_grad_two = (shares_two * (share_grad_two - centre)).astype(bf16)
            own_grad[0, low:high, lanes] += dot(score_grad, queries)
            own_grad[1, low:high, lanes] += dot(shares.astype(bf16), grads)
            other_sum[0, low:high, lanes] += dot(score_grad_two, queries)
            other_sum[1, low:high, lanes] += dot(shares_two.astype(bf16), grads)
            both = dot_tn(keys, score_grad) + dot_tn(keys_two, score_grad_two)
            query_grad[start : start + BLOCK, lanes] = (head_rows(both) * score_scale).astype(bf16)
        return carry

    lax.fori_loop(0, own_grad.shape[2] // PAIR, pair, 0)
    other_grad[:, :SEQ] = other_sum[...].astype(bf16)
    if given:
        for kind in range(2):
            line = given[0][:, kind * PART : (kind + 1) * PART]
            other_grad[kind, SEQ:] = jnp.concatenate([line] * 2, axis=0).astype(bf16)


def attend_back(
    order, query_first, queries, own, other, context_grad, logs, page_row, page_column, given
):
    return order.call(
        functools.partial(attend_back_kernel, query_first),
        [queries, own, other, context_grad, logs, page_row, page_column, *given],
        [in_vmem] * (7 + len(given)),
        [
            shape_of((SEQ, PART), bf16),
            shape_of((2, SEQ, PART), f32),
            shape_of((2, SEQ + 16 * len(given), PART), bf16),
        ],
        [in_vmem] * 3,
        scratch=[
            pltpu.VMEM((len(WINDOWS), WINDOW, BLOCK), f32),
            pltpu.VMEM((2, SEQ, PART), f32),
        ],
        limit=16,
        name="attend_back",
        cost=60,
    )


def partner_cross(pair):
    rows = pair[:, SEQ:].astype(f32)
    return jnp.concatenate([rows[0, :1], rows[1, :1]], axis=1)


def join_blocks(places, wides, downs, leads, halves, wide, down):
    rows = wide.shape[0] // (len(wides) + len(leads))
    for k, part in enumerate(wides):
        wide[pl.ds(pl.multiple_of(places[k] * rows, 16), rows)] = part[...]
        down[k] = downs[k][...]
    turn = places[4] % 2
    for k, part in enumerate(leads):
        first = places[len(wides) + k] * rows
        wide[pl.ds(pl.multiple_of(first, 16), rows), : part.shape[1]] = part[...]
        for side, half in enumerate(halves[k]):
            place = turn if side == 0 else 1 - turn
            start = pl.multiple_of(first + place * (rows // 2), 16)
            wide[pl.ds(start, rows // 2), part.shape[1] :] = half[rows:]
            for run in range(2):
                start = pl.multiple_of((2 * place + run) * rows, 16)
                down[len(wides) + k, pl.ds(start, rows)] = half[:rows, run * D : (run + 1) * D]


def middle_kernel(kinds, places, rows, *rest):
    contexts, rest = rest[:GROUPS], rest[GROUPS:]
    (tangent, vectors, partner, hidden_bias), rest = rest[:4], rest[4:]
    wides, downs, leads = [], [], []
    for group, size in zip((wides, downs, leads), kinds):
        group += rest[:size]
        rest = rest[size:]
    halves = [rest[2 * k : 2 * k + 2] for k in range(kinds[2])]
    rest = rest[2 * kinds[2] :]
    middle_out, second_out, hidden_out, slope_out, modal_out, inner_out, wide, down, total = rest
    join_blocks(places, wides, downs, leads, halves, wide, down)
    count = down.shape[0]
    middle = rows[...].astype(f32)
    for group, context in enumerate(contexts):
        middle += dot(context[...], wide[group * PART : (group + 1) * PART, :D])
    middle_out[...] = middle
    scaled, _ = normalise(middle)
    second_out[...] = (scaled * vectors[2:3] + vectors[3:4]).astype(bf16)
    total[...] = middle + vectors[4:5]
    slot = FF // count
    size = 384
    for k in range(count):
        for first in range(0, slot, size):
            start = places[k] * slot + first
            part = pl.ds(pl.multiple_of(start, 128), size)
            column = pl.ds(pl.multiple_of(D + start, 128), size)
            upper = dot(second_out[...], wide[:, column]) + hidden_bias[:, part]
            square = upper * upper
            angle = jnp.tanh(upper * (gelu_scale + (gelu_cubic * gelu_scale) * square))
            half = 0.5 + 0.5 * angle
            hidden = (upper * half).astype(bf16)
            hidden_out[:, part] = hidden
            bend = 2.0 * gelu_scale + (6.0 * gelu_cubic * gelu_scale) * square
            slope_out[:, part] = (half + half * (1.0 - half) * (upper * bend)).astype(bf16)
            total[...] += dot(hidden, down[k, first : first + size])
    modal_out[...] = total[...].astype(bf16)
    modal = modal_out[...].astype(f32)
    own = jnp.sum(modal * vectors[5:6], axis=1, keepdims=True)
    cross = jnp.sum(modal * partner_cross(partner), axis=1, keepdims=True)
    met = jnp.sum(modal * tangent[...].astype(f32), axis=1, keepdims=True)
    lane = lax.broadcasted_iota(jnp.int32, (SEQ, 128), 1)
    columns = jnp.where(lane == 0, own, jnp.where(lane == 1, cross, met))
    inner_out[...] = columns.T[:8]


def middle_pass(
    order, places, rows, contexts, tangent, vectors, partner, hidden_bias, wides, downs, leads, halves
):
    count = len(wides) + len(leads)
    parts = [*wides, *downs, *leads] + [piece for pair in halves for piece in pair]
    return order.call(
        functools.partial(middle_kernel, (len(wides), len(downs), len(leads))),
        [places, rows, *contexts, tangent, vectors, partner, hidden_bias, *parts],
        [in_smem] + [in_vmem] * (5 + GROUPS + len(parts)),
        [
            shape_of((SEQ, D), f32),
            shape_of((SEQ, D), bf16),
            shape_of((SEQ, FF), bf16),
            shape_of((SEQ, FF), bf16),
            shape_of((SEQ, D), bf16),
            shape_of((8, SEQ), f32),
            shape_of((D, D + FF), bf16),
            shape_of((count, FF // count, D), bf16),
        ],
        [in_vmem] * 8,
        scratch=[pltpu.VMEM((SEQ, D), f32)],
        limit=16,
        name="middle",
    )


def gate_kernel(
    own,
    other,
    tangent,
    partner_tangent,
    vectors,
    partner,
    grad_out,
    low_out,
    columns_out,
    sums,
):
    gate = jax.nn.sigmoid(own[0:1] + other[1:2])
    gate_two = jax.nn.sigmoid(other[0:1] + own[1:2])
    logit = other[2:3] * gate * (1.0 - gate)
    logit_two = own[2:3] * gate_two * (1.0 - gate_two)
    padding = jnp.zeros((124, SEQ), f32)
    columns = jnp.concatenate([gate, logit, gate_two, logit_two, padding], axis=0).T
    columns_out[...] = columns
    grad = (
        tangent[...].astype(f32)
        + columns[:, 1:2] * vectors[5:6]
        + partner_tangent[...].astype(f32) * columns[:, 2:3]
        + columns[:, 3:4] * partner_cross(partner)
    )
    grad_out[...] = grad
    low_out[...] = grad.astype(bf16)
    sums[...] = column_sums(grad)


def gate_pass(order, own, other, tangent, partner_tangent, vectors, partner):
    return order.call(
        gate_kernel,
        [own, other, tangent, partner_tangent, vectors, partner],
        [in_vmem] * 6,
        [
            shape_of((SEQ, D), f32),
            shape_of((SEQ, D), bf16),
            shape_of((SEQ, 128), f32),
            shape_of((1, D), f32),
        ],
        [in_vmem] * 4,
        name="gate",
    )


def mix_kernel(own, other, columns, mixed):
    mixed[...] = (
        own[...].astype(f32) + columns[:, 0:1] * other[...].astype(f32)
    ).astype(bf16)


def mix_pass(order, own, other, columns, waits=()):
    return order.call(
        mix_kernel,
        [own, other, columns],
        [in_vmem] * 3,
        [shape_of((SEQ, D), bf16)],
        [in_vmem],
        name="mix",
        cost=60,
        waits=waits,
    )[0]


def gate_sums_kernel(own, columns, out):
    rows = own[...].astype(f32)
    out[...] = jnp.zeros_like(out)
    out[0:1] = column_sums(columns[:, 1:2] * rows)
    out[1:2] = column_sums(columns[:, 3:4] * rows)


def gate_sums_pass(order, own, columns):
    return order.call(
        gate_sums_kernel, [own, columns], [in_vmem] * 2, [shape_of((8, D), f32)], [in_vmem], name="gate_sums"
    )[0]


def chain_kernel(places, low, grad, slope, middle, vectors, wide, down, *rest):
    total_out, total_low_out, context_out, upper_out, upper_sums, gain_sums, bias_sums = rest[:7]
    normed_grad = rest[7]
    normed_grad[...] = jnp.zeros_like(normed_grad)
    count = down.shape[0]
    slot = FF // count
    size = 384
    for k in range(count):
        for first in range(0, slot, size):
            start = places[k] * slot + first
            part = pl.ds(pl.multiple_of(start, 128), size)
            column = pl.ds(pl.multiple_of(D + start, 128), size)
            upper = dot_nt(low[...], down[k, first : first + size]) * slope[:, part].astype(f32)
            upper_sums[:, part] = column_sums(upper)
            upper_low = upper.astype(bf16)
            upper_out[:, part] = upper_low
            normed_grad[...] += dot_nt(upper_low, wide[:, column])
    scaled, root = normalise(middle[...])
    incoming = normed_grad[...]
    gain_sums[...] = column_sums(incoming * scaled)
    bias_sums[...] = column_sums(incoming)
    total = grad[...] + norm_back(scaled, root, vectors[2:3], incoming)
    total_out[...] = total
    total_low_out[...] = total.astype(bf16)
    context_out[...] = dot_nt(total_low_out[...], wide[:, :D]).astype(bf16)


def chain_pass(order, places, low, grad, slope, middle, vectors, wide, down):
    return order.call(
        chain_kernel,
        [places, low, grad, slope, middle, vectors, wide, down],
        [in_smem] + [in_vmem] * 7,
        [
            shape_of((SEQ, D), f32),
            shape_of((SEQ, D), bf16),
            shape_of((SEQ, D), bf16),
            shape_of((SEQ, FF), bf16),
            shape_of((1, FF), f32),
            shape_of((1, D), f32),
            shape_of((1, D), f32),
        ],
        [in_vmem] * 7,
        scratch=[pltpu.VMEM((SEQ, D), f32)],
        limit=20,
        name="chain",
    )


def slots_of(count):
    return (list(range(0, count, 2)), list(range(1, count, 2)))


def block_shapes(widths, count):
    near, far = slots_of(count)
    rows = D // count
    outs = []
    for width in widths:
        outs.append(shape_of((len(near), rows, width), bf16))
        if far:
            outs.append(shape_of((len(far), rows, width), bf16))
    return outs


def store_blocks(places, count, products, widths, outs, whole):
    near, far = slots_of(count)
    rows = D // count
    products = list(products)
    each = 2 if far else 1
    for index, width in enumerate(widths):
        low = 0
        while low < width:
            left, right = products.pop(0)
            whole[:, low : low + right.shape[1]] = dot(left, right).astype(bf16)
            low += right.shape[1]
        for out, slots in zip(outs[each * index : each * index + each], (near, far)):
            for place, slot in enumerate(slots):
                begin = pl.multiple_of(places[slot] * rows, 16)
                out[place] = whole[pl.ds(begin, rows), :width]


def up_grads_kernel(count, widths, places, second, upper, *rest):
    turned = second[...].T
    products = [(turned, upper[:, k : k + 512]) for k in range(0, FF, 512)]
    store_blocks(places, count, products, widths, rest[:-1], rest[-1])


def up_grads(order, places, second, upper, widths, count):
    outs = block_shapes(widths, count)
    return order.call(
        functools.partial(up_grads_kernel, count, widths),
        [places, second, upper],
        [in_smem] + [in_vmem] * 2,
        outs,
        [in_vmem] * len(outs),
        scratch=[pltpu.VMEM((D, max(widths)), bf16)],
        limit=16,
        name="up_grads",
    )


def lead_grads_kernel(count, places, context, context_two, low, normed, *rest):
    queries, (own, returned), rest = rest[:GROUPS], rest[GROUPS : GROUPS + 2], rest[GROUPS + 2 :]
    pair_low, outs, whole = rest[0], rest[1:-1], rest[-1]
    pair_low[...] = (own[...] + returned[:, :SEQ].astype(f32)).astype(bf16)
    turned = jnp.concatenate([context[...].T, context_two[...].T], axis=0)
    products = [(turned, low[:, k : k + PART]) for k in range(0, D, PART)]
    turned = normed[...].T
    products += [(turned, query[...]) for query in queries]
    products += [(turned, pair_low[kind]) for kind in range(2)]
    store_blocks(places, count, products, [3 * D], outs, whole)


def lead_grads(order, places, contexts, low, normed, queries, own, returned, count):
    outs = block_shapes([3 * D], count)
    args = [*contexts, low, normed, *queries, own, returned]
    return order.call(
        functools.partial(lead_grads_kernel, count),
        [places, *args],
        [in_smem] + [in_vmem] * len(args),
        [shape_of(own.shape, bf16)] + outs,
        [in_vmem] * (1 + len(outs)),
        scratch=[pltpu.VMEM((D, 3 * D), bf16)],
        limit=16,
        name="lead_grads",
    )


def down_grads_kernel(count, first, height, fold, places, low, hidden, *outs):
    near, far = slots_of(count)
    width = FF // count
    turned = low[:, first : first + height].T
    rows = height // fold
    for out, slots in zip(outs, (near, far)):
        for place, slot in enumerate(slots):
            begin = pl.multiple_of(places[slot] * width, 128)
            block = dot(turned, hidden[:, pl.ds(begin, width)]).astype(bf16)
            for k in range(fold):
                out[place, :, k * width : (k + 1) * width] = block[k * rows : (k + 1) * rows]


def down_grads(order, places, low, hidden, first, height, fold, count):
    near, far = slots_of(count)
    width = FF // count
    outs = [shape_of((len(near), height // fold, fold * width), bf16)]
    if far:
        outs.append(shape_of((len(far), height // fold, fold * width), bf16))
    return order.call(
        functools.partial(down_grads_kernel, count, first, height, fold),
        [places, low, hidden],
        [in_smem, in_vmem, in_vmem],
        outs,
        [in_vmem] * len(outs),
        limit=16,
        name="down_grads",
    )


def first_kernel(count, places, total, rows, vectors, normed, own, returned, *rest):
    parts, rest = rest[:count], rest[count:]
    queries, pair, rest = rest[:GROUPS], rest[GROUPS], rest[GROUPS + 1 :]
    gain_two, bias_two, output_bias, gate_own, hidden_bias = rest[:5]
    grad_out, outs = rest[5], rest[6:-5]
    pair_low, normed_grad, weight, whole, short = rest[-5:]
    pair_low[...] = (own[...] + returned[:, :SEQ].astype(f32)).astype(bf16)
    assemble(places, parts, weight)
    for group, pairs in enumerate((pair, pair_low)):
        start = group * PART
        block = dot_nt(queries[group][...], weight[:, start : start + PART])
        for kind in range(2):
            start = (kind + 1) * D + group * PART
            block += dot_nt(pairs[kind], weight[:, start : start + PART])
        if group == 0:
            normed_grad[...] = block
        else:
            normed_grad[...] += block
    scaled, root = normalise(rows[...].astype(f32))
    incoming = normed_grad[...]
    short[...] = jnp.zeros_like(short)
    short[0:1] = column_sums(incoming * scaled)
    short[1:2] = column_sums(incoming)
    for line, member in enumerate((gain_two, bias_two, output_bias)):
        short[line + 2 : line + 3] = member[...]
    short[5:6] = gate_own[0:1]
    for kind in range(2):
        line = returned[kind, SEQ : SEQ + 8].astype(f32)
        short[6:7, kind * PART : (kind + 1) * PART] = line[1:2]
    for line in range(FF // D):
        short[line + 8 : line + 9] = hidden_bias[:, line * D : (line + 1) * D]
    grad_out[...] = total[...] + norm_back(scaled, root, vectors[0:1], incoming)
    turned = normed[...].T
    for kind in range(2):
        whole[:, kind * PART : (kind + 1) * PART] = dot(turned, pair_low[kind]).astype(bf16)
    height = D // count
    for out, slots in zip(outs, slots_of(count)):
        for place, slot in enumerate(slots):
            begin = pl.multiple_of(places[slot] * height, 16)
            out[place * height : (place + 1) * height] = whole[pl.ds(begin, height)]
        out[len(slots) * height :] = short[...].astype(bf16)


def first_pass(
    order, places, total, rows, vectors, normed, own, returned, parts, queries, pair, short
):
    count = len(parts)
    args = [total, rows, vectors, normed, own, returned, *parts, *queries, pair, *short]
    outs = [
        shape_of((len(slots) * (D // count) + 16, 2 * PART), bf16) for slots in slots_of(count) if slots
    ]
    return order.call(
        functools.partial(first_kernel, count),
        [places, *args],
        [in_smem] + [in_vmem] * len(args),
        [shape_of((SEQ, D), f32)] + outs,
        [in_vmem] * (1 + len(outs)),
        scratch=[
            pltpu.VMEM((2, SEQ, PART), bf16),
            pltpu.VMEM((SEQ, D), f32),
            pltpu.VMEM((D, 3 * D), bf16),
            pltpu.VMEM((D, 2 * PART), bf16),
            pltpu.VMEM((16, D), f32),
        ],
        limit=20,
        name="first",
    )


def settle_kernel(kind, count, outs, places, *refs):
    totals, returned, refs = refs[:count], refs[count : 2 * count], refs[2 * count :]
    targets, (scratch, sems) = refs[:outs], (refs[outs : 2 * outs], refs[2 * outs])
    copies = []

    def leave(index, *where):
        source, target = scratch[index].at[where], targets[index].at[where]
        copies.append(pltpu.make_async_copy(source, target, sems.at[len(copies)]))
        copies[-1].start()

    inner = jnp.logical_and(places[4] > 0, places[4] < 3)
    values = [jnp.where(inner, a[...], b[...]).astype(f32) for a, b in zip(totals, returned)]
    out, every = scratch[0], slice(None)
    if kind == "turn":
        first = 0
        for value in values:
            rows = value.shape[0]
            start = first
            for k in range(0, value.shape[1], D):
                out[:, first : first + rows] = value[:, k : k + D].T
                first += rows
            leave(0, every, pl.ds(start, first - start))
    elif kind == "columns":
        first = 0
        for value in values:
            out[:, first : first + value.shape[1]] = value
            leave(0, every, pl.ds(first, value.shape[1]))
            first += value.shape[1]
    else:
        scratch[1][...] = values[0][:, :D]
        leave(1, every)
        out[:, :D] = values[0][:, D:]
        for group, value in enumerate(values[1:]):
            for part in range(2):
                start = (part + 1) * D + group * PART
                out[:, start : start + PART] = value[:, part * PART : (part + 1) * PART]
        leave(0, every)
    for copy in copies:
        copy.wait()


def settle(order, kind, places, blocks, dims):
    count = len(blocks)
    found = order.call(
        functools.partial(settle_kernel, kind, count, len(dims)),
        [places] + [block[0] for block in blocks] + [block[1] for block in blocks],
        [in_smem] + [in_vmem] * (2 * count),
        [shape_of(each, f32) for each in dims],
        [in_hbm] * len(dims),
        scratch=[pltpu.VMEM(each, f32) for each in dims] + [pltpu.SemaphoreType.DMA((8,))],
        name="settle",
    )
    return found[0] if len(dims) == 1 else found


def last_settle_kernel(places, total, returned, given, out, *rest):
    short_outs, (scratch, sems) = rest[:8], rest[8:]
    inner = jnp.logical_and(places[4] > 0, places[4] < 3)
    value = jnp.where(inner, total[...], returned[...]).astype(f32)
    rows = scratch.shape[1]
    copies = []
    for part in range(2):
        scratch[part] = value[:rows, part * PART : (part + 1) * PART]
        place = out.at[:, pl.ds((part + 1) * D + PART, PART)]
        copies.append(pltpu.make_async_copy(scratch.at[part], place, sems.at[part]))
        copies[-1].start()
    short = value[rows:]
    turned = pltpu.roll(short, D - places[0] * rows, 1)
    for line in range(7):
        short_outs[line][...] = turned[line : line + 1, :rows].reshape(rows)
    line = lax.broadcasted_iota(jnp.int32, short.shape, 0)
    hidden = jnp.sum(jnp.where(line == 8 + places[0], short, 0.0), axis=0)
    short_outs[7][...] = hidden
    for copy in copies:
        copy.wait()


def last_settle(order, places, block, given):
    rows = given.shape[0]
    shorts = [shape_of((rows,), f32)] * 7 + [shape_of((D,), f32)]
    found = order.call(
        last_settle_kernel,
        [places, block[0], block[1], given],
        [in_smem, in_vmem, in_vmem, in_hbm],
        [shape_of(given.shape, f32)] + shorts,
        [in_hbm] + [in_vmem] * 8,
        scratch=[pltpu.VMEM((2, rows, PART), f32), pltpu.SemaphoreType.DMA((2,))],
        name="last_settle",
        aliases={3: 0},
    )
    return found[0], found[1:]


def swap_bit(value, axis, bit):
    size = lax.axis_size(axis)
    return lax.ppermute(value, axis, [(source, source ^ (1 << bit)) for source in range(size)])


def from_partner(value):
    size = lax.axis_size("stream")
    half = size // 2
    return lax.ppermute(value, "stream", [(source, (source + half) % size) for source in range(size)])


def along(value, pairs):
    return lax.ppermute(value, "dp", pairs)


def up_line(value, steps):
    return along(value, [(floor, floor + 1) for floor in range(steps - 1, 3)])


def down_line(value, steps):
    return along(value, [(floor, floor - 1) for floor in range(1, 5 - steps)])


def swap_outer(value):
    return along(value, [(0, 1), (1, 0), (2, 3), (3, 2)])


def to_inner(value):
    return along(value, [(0, 1), (3, 2)])


def over_middle(value):
    return along(value, [(1, 2), (2, 1)])


def to_outer(value):
    return along(value, [(1, 0), (2, 3)])


def core(value):
    return swap_bit(value, "stream", 0)


def across(value):
    return swap_bit(value, "stream", 1)


def modality_groups():
    size = lax.axis_size("stream")
    half = size // 2
    return [list(range(half)), list(range(half, size))]


def body(
    regions,
    cotangent,
    page_lens,
    qkv_weight,
    out_weight,
    up_weight,
    down_weight,
    ln1_gain,
    ln1_bias,
    ln2_gain,
    ln2_bias,
    up_bias,
    down_bias,
    gate_own,
    gate_other,
):
    half = lax.axis_size("stream") // 2
    depth = lax.axis_size("dp")
    paired = half == 4 and depth == 4
    side = lax.axis_index("stream") % half
    floor = lax.axis_index("dp")
    count = 4 if paired else 1
    slots = jnp.arange(4, dtype=jnp.int32)
    picks = jnp.bitwise_xor(side.astype(jnp.int32), slots) if paired else jnp.zeros_like(slots)
    places = jnp.concatenate([picks, floor.astype(jnp.int32)[None]])
    order = Order()
    short = (ln1_gain, ln1_bias, ln2_gain, ln2_bias, down_bias, gate_own, gate_other, up_bias)
    partner_tangent = from_partner(cotangent)

    def attend_group(group, waits=()):
        context, log_total = attend(
            order,
            group * PART // PAIR,
            queries,
            own_pairs[group],
            other_pairs[group],
            page_row,
            page_column,
            waits,
        )
        contexts.append(context)
        logs.append(log_total)

    contexts, logs = [], []
    if paired:
        qkv_shard = first_cast_pass(order, qkv_weight, short)
        qkv_across, qkv_near = across(qkv_shard), core(qkv_shard)
        wide_shard, down_shard, lead, half_own, page_row, page_column = cast_pass(
            order, places, page_lens, out_weight, up_weight, down_weight
        )
        wide_near, down_near = core(wide_shard), core(down_shard)
        (qkv_across,) = order.hold([qkv_across], waits=[partner_tangent, qkv_near])
        qkv_far, half_own = core(qkv_across), across(half_own)
        qkv_parts = [qkv_shard, qkv_near, qkv_across, qkv_far]
        own_pairs, queries, normed, vectors, hidden_bias = project(
            order, places, regions, qkv_parts, waits=[wide_near, down_near]
        )
        other_pairs = [from_partner(pair) for pair in own_pairs]
        lead_across = across(lead)
        (half_own,) = order.hold([half_own])
        half_other, half_own_far = swap_outer(half_own), core(half_own)
        attend_group(0)
        (lead_across,) = order.hold([lead_across])
        vectors = order.pause(vectors)
        (half_other,) = order.hold([half_other])
        half_other_far, lead_far = core(half_other), core(lead_across)
        attend_group(1)
        wides, downs = [wide_shard, wide_near], [down_shard, down_near]
        leads = [lead_across, lead_far]
        halves = [(half_own, half_other), (half_own_far, half_other_far)]
    else:
        lengths = lax.dynamic_slice_in_dim(page_lens, side * depth + floor, 1, 0)
        positions = jnp.arange(SEQ, dtype=jnp.int32)
        page_ends = jnp.cumsum(lengths[0], dtype=jnp.int32)
        pages = jnp.sum((page_ends[:, None] <= positions[None, :]).astype(jnp.int32), axis=0)
        page_row, page_column = pages[None, :], pages[:, None]

        def gather(shard):
            return [
                lax.all_gather(shard, "stream", axis_index_groups=modality_groups(), tiled=True)
            ]

        packed = jnp.concatenate([member.astype(bf16) for member in short])[None]
        found = gather(packed)[0].astype(f32)
        shard = D // half
        rows = [found[:, k * shard : (k + 1) * shard].reshape(1, D) for k in range(7)]
        given = (
            jnp.concatenate(rows + [jnp.zeros((1, D), f32)], axis=0),
            found[:, 7 * shard :].reshape(1, FF),
        )
        qkv_parts = gather(qkv_weight.astype(bf16))
        wides = gather(jnp.concatenate([out_weight, up_weight], axis=1).astype(bf16))
        downs, leads, halves = gather(down_weight.astype(bf16)), [], []
        own_pairs, queries, normed, vectors, hidden_bias = project(
            order, places, regions, qkv_parts, given
        )
        other_pairs = [from_partner(pair) for pair in own_pairs]
        for group in range(GROUPS):
            attend_group(group)

    middle, second, hidden, slope, modal, inner_own, wide, down = middle_pass(
        order,
        places,
        regions,
        contexts,
        partner_tangent,
        vectors,
        other_pairs[-1],
        hidden_bias,
        wides,
        downs,
        leads,
        halves,
    )
    inner_other = from_partner(inner_own)
    modal_grad, modal_low, columns, output_bias_grad = gate_pass(
        order, inner_own, inner_other, cotangent, partner_tangent, vectors, other_pairs[-1]
    )

    def attend_back_group(group):
        query_grad, own_grad, other_grad = attend_back(
            order,
            group * PART // PAIR,
            queries,
            own_pairs[group],
            other_pairs[group],
            context_grad,
            logs[group],
            page_row,
            page_column,
            [gate_sums] if group == GROUPS - 1 else [],
        )
        query_grads.append(query_grad)
        own_grads.append(own_grad)
        returned.append(from_partner(other_grad))

    def last_pass(pair_low):
        short_grads = (
            gain_two_grad,
            bias_two_grad,
            output_bias_grad,
            gate_sums,
            hidden_bias_grad,
        )
        return first_pass(
            order,
            places,
            middle_grad,
            regions,
            vectors,
            normed,
            own_grads[1],
            returned[1],
            qkv_parts,
            query_grads,
            pair_low,
            short_grads,
        )

    query_grads, own_grads, returned = [], [], []
    back = (order, places, modal_low, modal_grad, slope, middle, vectors, wide, down)
    if paired:
        d1, far = down_grads(order, places, modal_low, hidden, 0, 384, 2, count)
        d1_core = core(far)
        d2, far = down_grads(order, places, modal_low, hidden, 384, 384, 2, count)
        d2_core = core(far)
        d1, away = sums_pass(order, places, folds=[(d1, d1_core, [FF // 2])])
        d1_in = across(away)
        d2, away = sums_pass(order, places, folds=[(d2, d2_core, [FF // 2])])
        d2_in = across(away)
        middle_grad, middle_low, context_grad, upper_low, *rest = chain_pass(*back)
        hidden_bias_grad, gain_two_grad, bias_two_grad = rest
        d1 = sums_pass(order, places, adds=[(d1, d1_in)])
        d1_in = to_inner(d1)
        u1, far_one, u2, far_two = up_grads(
            order, places, second, upper_low, [FF // 2, FF // 2], count
        )
        u1_core, u2_core = core(far_one), core(far_two)
        attend_back_group(0)
        d2, d1 = sums_pass(order, places, adds=[(d2, d2_in), (d1, d1_in)])
        d2_in, d1_mid = to_inner(d2), over_middle(d1)
        columns = order.pause(columns)
        u1, away = sums_pass(order, places, folds=[(u1, u1_core, [FF // 2])])
        u1_in = across(away)
        u2, away = sums_pass(order, places, folds=[(u2, u2_core, [FF // 2])])
        gate_sums = gate_sums_pass(order, modal, columns)
        attend_back_group(1)
        d2, u1, u1_pay = sums_pass(
            order, places, adds=[(d2, d2_in)], pays=[(u1, u1_in, d1, d1_mid)]
        )
        u1_in, d2_mid = swap_outer(u1_pay), over_middle(d2)
        (away,) = order.hold([away])
        u2_in = across(away)
        pair_low, lead_near, lead_far = lead_grads(
            order, places, contexts, middle_low, normed, query_grads, own_grads[0], returned[0], count
        )
        lead_core = core(lead_far)
        u1, u2, u2_pay = sums_pass(
            order, places, adds=[(u1, u1_in)], pays=[(u2, u2_in, d2, d2_mid)]
        )
        d1_out = u1_in
        u2_in, u1_mid = swap_outer(u2_pay), over_middle(u1)
        gate_sums = order.pause(gate_sums)
        oq, away, p1, away_two = sums_pass(
            order, places, folds=[(lead_near, lead_core, [2 * D, D])]
        )
        oq_in, p1_in = across(away), across(away_two)
        region_grad, last_near, last_far = last_pass(pair_low)
        last_core = core(last_far)
        u2, oq, oq_pay = sums_pass(
            order, places, adds=[(u2, u2_in)], pays=[(oq, oq_in, u1, u1_mid)]
        )
        d2_out = u2_in
        oq_in, u2_mid = swap_outer(oq_pay), over_middle(u2)
        modal = order.pause(modal)
        p2, away = sums_pass(order, places, folds=[(last_near, last_core, [D])])
        p2_in = across(away)
        down_grad = settle(order, "turn", places, [(u1_pay, d1_out), (u2_pay, d2_out)], [(D, D)])
        oq, u2, p1 = sums_pass(
            order, places, adds=[(oq, oq_in), (u2, u2_mid), (p1, p1_in)]
        )
        u1_out = oq_in
        oq_mid, u2_out, p1_in = over_middle(oq), to_outer(u2), to_inner(p1)
        p2 = sums_pass(order, places, adds=[(p2, p2_in)])
        p2_in = to_inner(p2)
        p1 = sums_pass(order, places, adds=[(p1, p1_in)])
        p1_mid = over_middle(p1)
        (modal,) = order.hold([modal])
        partner_modal = from_partner(modal)
        oq, p2 = sums_pass(order, places, adds=[(oq, oq_mid), (p2, p2_in)], waits=[u2_out])
        oq_out, p2_mid = to_outer(oq), over_middle(p2)
        up_grad = settle(order, "columns", places, [(oq_pay, u1_out), (u2, u2_out)], [(D // 4, FF)])
        p1 = sums_pass(order, places, adds=[(p1, p1_mid)])
        p1_out = to_outer(p1)
        p2 = sums_pass(order, places, adds=[(p2, p2_mid)])
        p2_out = to_outer(p2)
        mixed_rows = mix_pass(order, modal, partner_modal, columns, [oq_out])
        qkv_grad, out_grad = settle(
            order,
            "pairs",
            places,
            [(oq, oq_out), (p1, p1_out)],
            [(D // 4, 3 * D), (D // 4, D)],
        )
        qkv_grad, shorts = last_settle(order, places, (p2, p2_out), qkv_grad)
    else:
        (down_block,) = down_grads(order, places, modal_low, hidden, 0, D, 1, count)
        middle_grad, middle_low, context_grad, upper_low, *rest = chain_pass(*back)
        hidden_bias_grad, gain_two_grad, bias_two_grad = rest
        (up_block,) = up_grads(order, places, second, upper_low, [FF], count)
        gate_sums = gate_sums_pass(order, modal, columns)
        for group in range(GROUPS):
            attend_back_group(group)
        mixed_rows = mix_pass(order, modal, from_partner(modal), columns)
        pair_low, lead_block = lead_grads(
            order, places, contexts, middle_low, normed, query_grads, own_grads[0], returned[0], count
        )
        region_grad, last_block = last_pass(pair_low)
        lead_block = lead_block[0]
        short_rows = last_block[D:].astype(f32)

        def total(block):
            groups = modality_groups()
            owned = lax.psum_scatter(
                block.astype(f32), "stream", axis_index_groups=groups, tiled=True
            )
            return lax.psum(owned, "dp")

        down_grad = total(down_block[0].T)
        up_grad, out_grad = total(up_block[0]), total(lead_block[:, :D])
        qkv_grad = total(
            jnp.concatenate(
                [
                    lead_block[:, D : 2 * D + PART],
                    last_block[:D, :PART],
                    lead_block[:, 2 * D + PART :],
                    last_block[:D, PART:],
                ],
                axis=1,
            )
        )
        short_rows = lax.psum(
            lax.psum(short_rows, "stream", axis_index_groups=modality_groups()), "dp"
        )

        shard = D // half
        own_rows = lax.dynamic_slice_in_dim(short_rows, side * shard, shard, 1)
        hidden_rows = short_rows[8 : 8 + FF // D].reshape(FF)
        own_hidden = lax.dynamic_slice_in_dim(hidden_rows, side * (FF // half), FF // half, 0)
        shorts = [own_rows[k] for k in range(7)] + [own_hidden]
    return (
        mixed_rows,
        region_grad,
        qkv_grad,
        out_grad,
        up_grad,
        down_grad,
        shorts[0],
        shorts[1],
        shorts[2],
        shorts[3],
        shorts[7],
        shorts[4],
        shorts[5],
        shorts[6],
    )


def solution(mesh):
    in_specs = (
        P(("stream", "dp"), None),
        P(("stream", "dp"), None),
        P(),
        P("stream", None),
        P("stream", None),
        P("stream", None),
        P("stream", None),
        P("stream"),
        P("stream"),
        P("stream"),
        P("stream"),
        P("stream"),
        P("stream"),
        P("stream"),
        P("stream"),
    )
    out_specs = (
        P(("stream", "dp"), None),
        P(("stream", "dp"), None),
        P("stream", None),
        P("stream", None),
        P("stream", None),
        P("stream", None),
        P("stream"),
        P("stream"),
        P("stream"),
        P("stream"),
        P("stream"),
        P("stream"),
        P("stream"),
        P("stream"),
    )
    return jax.shard_map(body, mesh=mesh, in_specs=in_specs, out_specs=out_specs, check_vma=False)
```

```python
import functools
import math

import jax
import jax.numpy as jnp
from jax import lax
from jax.experimental import pallas as pl
from jax.experimental.pallas import tpu as pltpu
from jax.sharding import PartitionSpec as P

D = 768
HEADS = 12
HEAD_DIM = 64
FF = 3072
LEAD = FF - 1280
RUNS = ((LEAD, 768), (LEAD + 768, 512))
SEQ = 512
GROUPS = 2
PART = D // GROUPS
PAIR = 2 * HEAD_DIM
BLOCK = 128
REACH = 96
ROWS = 256
MIB = 1024 * 1024

epsilon = 1e-05
masked_score = -1e30
score_scale = HEAD_DIM ** (-0.5)
gelu_scale = math.sqrt(2.0 / math.pi)
gelu_cubic = 0.044715

f32 = jnp.float32
bf16 = jnp.bfloat16

WINDOWS = [
    (max(0, start - REACH), min(SEQ, start + BLOCK + REACH)) for start in range(0, SEQ, BLOCK)
]
WINDOW = BLOCK + 2 * REACH

in_smem = pl.BlockSpec(memory_space=pltpu.SMEM)
in_vmem = pl.BlockSpec(memory_space=pltpu.VMEM)
in_any = pl.BlockSpec(memory_space=pl.ANY)
in_hbm = pl.BlockSpec(memory_space=pltpu.HBM)


def shape_of(dims, dtype):
    return jax.ShapeDtypeStruct(dims, dtype)


def dot(left, right):
    return lax.dot_general(left, right, (((1,), (0,)), ((), ())), preferred_element_type=f32)


def dot_nt(left, right):
    return lax.dot_general(left, right, (((1,), (1,)), ((), ())), preferred_element_type=f32)


def dot_tn(left, right):
    return lax.dot_general(left, right, (((0,), (0,)), ((), ())), preferred_element_type=f32)


def normalise(values):
    average = jnp.mean(values, axis=-1, keepdims=True)
    centred = values - average
    spread = jnp.mean(centred * centred, axis=-1, keepdims=True)
    root = lax.rsqrt(spread + epsilon)
    return centred * root, root


def norm_back(scaled, root, gain, incoming):
    weighted = incoming * gain
    average = jnp.mean(weighted, axis=-1, keepdims=True)
    slope = jnp.mean(weighted * scaled, axis=-1, keepdims=True)
    return root * (weighted - average - scaled * slope)


def column_sums(values):
    return jnp.sum(values, axis=0, keepdims=True)


class Order:
    def __init__(self):
        self.token = []

    def call(
        self,
        kernel,
        args,
        in_specs,
        outs,
        out_specs,
        scratch=(),
        grid=(),
        limit=16,
        name=None,
        prefetch=None,
        waits=(),
        aliases=None,
        cost=0,
    ):
        given = len(args)
        extra = list(self.token) + list(waits)
        ahead = [] if prefetch is None else [prefetch]
        count = len(ahead)
        smallest = min(math.prod(out.shape) for out in outs)
        marked = smallest > 4096 and not aliases
        outs, out_specs = list(outs), list(out_specs)
        if marked:
            outs.append(shape_of((8, 128), f32))
            out_specs.append(in_vmem)
        place = count + given + len(extra) + len(outs) - 1

        def wrapped(*refs):
            used = list(refs[: count + given]) + list(refs[count + given + len(extra) :])
            if marked:
                refs[place][...] = jnp.zeros((8, 128), f32)
                used.pop(count + given + len(outs) - 1)
            kernel(*used)

        results = pl.pallas_call(
            wrapped,
            out_shape=outs,
            grid_spec=pltpu.PrefetchScalarGridSpec(
                num_scalar_prefetch=count,
                grid=grid,
                in_specs=list(in_specs) + [in_any] * len(extra),
                out_specs=out_specs,
                scratch_shapes=list(scratch),
            ),
            compiler_params=pltpu.CompilerParams(vmem_limit_bytes=limit * MIB),
            cost_estimate=pl.CostEstimate(flops=1 + cost * 10**9, bytes_accessed=1 + cost * MIB, transcendentals=cost * 10**6),
            input_output_aliases=aliases or {},
            name=name,
        )(*ahead, *args, *extra)
        self.token = [min(results, key=lambda out: out.size)]
        return list(results)[:-1] if marked else results

    def hold(self, arrays, waits=()):
        return self.call(
            lambda *refs: None,
            arrays,
            [in_any] * len(arrays),
            [shape_of(array.shape, array.dtype) for array in arrays],
            [in_any] * len(arrays),
            name="hold",
            cost=0,
            waits=waits,
            aliases={k: k for k in range(len(arrays))},
        )

    def pause(self, value):
        return self.call(
            lambda *refs: None,
            [value],
            [in_any],
            [shape_of(value.shape, value.dtype)],
            [in_any],
            name="pause",
            cost=60,
            aliases={0: 0},
        )[0]


def assemble(places, parts, whole):
    rows = whole.shape[0] // len(parts)
    for k, part in enumerate(parts):
        whole[pl.ds(pl.multiple_of(places[k] * rows, 16), rows)] = part[:rows]


def sums_pass(order, places, folds=(), adds=(), pays=(), waits=(), extra=0):
    args, outs, steps = [], [], []

    def give(*arrays):
        args.extend(arrays)
        return list(range(len(args) - len(arrays), len(args)))

    def make(dims, dtype):
        outs.append(shape_of(dims, dtype))
        return len(outs) - 1

    for near, received, widths in folds:
        made = []
        for width in widths:
            rows = near.shape[1] if len(near.shape) == 3 else (near.shape[0] + 16) // 2
            made += [make((rows + add, width), near.dtype) for add in (0, extra)]
        steps.append(("fold", give(near, received), made))
    for left, right in adds:
        steps.append(("add", give(left, right), [make(left.shape, left.dtype)]))
    for mine, received, older, crossed in pays:
        given = give(mine, received, older, crossed)
        steps.append(("pay", given, [make(mine.shape, mine.dtype) for _ in range(2)]))
    count = len(args)

    def kernel(places_ref, *refs):
        ins, results = refs[:count], refs[count:]
        inner = jnp.logical_and(places_ref[4] > 0, places_ref[4] < 3)
        for kind, given, made in steps:
            if kind == "fold" and len(ins[given[0]].shape) == 3:
                first = 0
                for k in range(0, len(made), 2):
                    width = results[made[k]].shape[1]
                    part = slice(first, first + width)
                    for slot in range(2):
                        total = ins[given[0]][slot, :, part].astype(f32)
                        total += ins[given[1]][slot, :, part].astype(f32)
                        results[made[k + slot]][: total.shape[0]] = total.astype(bf16)
                    if extra:
                        results[made[k + 1]][total.shape[0] :] = jnp.zeros((extra, width), bf16)
                    first += width
            elif kind == "fold":
                total = (ins[given[0]][...].astype(f32) + ins[given[1]][...].astype(f32)).astype(bf16)
                rows = results[made[0]].shape[0] - 16
                for slot in range(2):
                    results[made[slot]][:rows] = total[slot * rows : (slot + 1) * rows]
                    results[made[slot]][rows:] = total[2 * rows :]
            elif kind == "add":
                rows = ins[given[0]].shape[0]
                total = ins[given[0]][...].astype(f32) + ins[given[1]][:rows].astype(f32)
                results[made[0]][...] = total.astype(results[made[0]].dtype)
            else:
                rows = ins[given[0]].shape[0]
                fresh = ins[given[0]][...].astype(f32) + ins[given[1]][:rows].astype(f32)
                older = ins[given[2]][...].astype(f32) + ins[given[3]][...].astype(f32)
                results[made[0]][...] = fresh.astype(results[made[0]].dtype)
                results[made[1]][...] = jnp.where(inner, older, fresh).astype(results[made[1]].dtype)

    found = order.call(
        kernel,
        [places, *args],
        [in_smem] + [in_vmem] * len(args),
        outs,
        [in_vmem] * len(outs),
        limit=12,
        name="sums",
        waits=waits,
    )
    found = list(found)
    return found[0] if len(found) == 1 else found


def first_cast_kernel(sizes, qkv, short, out, rows):
    rows[...] = jnp.zeros_like(rows)
    offset = 0
    for line, size in enumerate(sizes):
        rows[line : line + 1, :size] = short[:, offset : offset + size]
        offset += size
    height = qkv.shape[0]
    out[height:] = rows[...].astype(bf16)
    out[:height] = qkv[...].astype(bf16)


def first_cast_pass(order, qkv, members):
    return order.call(
        functools.partial(first_cast_kernel, [member.size for member in members]),
        [qkv, jnp.concatenate(members)[None]],
        [in_vmem] * 2,
        [shape_of((qkv.shape[0] + 16, 3 * D), bf16)],
        [in_vmem],
        scratch=[pltpu.VMEM((16, 3 * D), f32)],
        limit=16,
        name="first_cast",
    )[0]


def cast_kernel(
    places,
    lengths,
    left,
    right,
    down,
    wide_out,
    down_out,
    lead_out,
    half_out,
    row_out,
    column_out,
):
    wide_out[:, :D] = left[...].astype(bf16)
    wide_out[:, D:] = right[...].astype(bf16)
    down_out[...] = down[...].astype(bf16)
    lead_out[...] = wide_out[:, : lead_out.shape[1]]
    rows = left.shape[0]
    turn = places[4] % 2
    first = turn * 2 * rows
    for run in range(2):
        start = pl.multiple_of(first + run * rows, 16)
        half_out[:rows, run * D : (run + 1) * D] = down_out[pl.ds(start, rows)]
    start = pl.multiple_of(turn * (rows // 2), 16)
    line = rows
    for column, width in RUNS:
        count = 2 * D // width
        height = rows // 2 // count
        for run in range(count):
            part = pl.ds(pl.multiple_of(start + run * height, 16), height)
            block = wide_out[part, D + column : D + column + width]
            half_out[line : line + height, run * width : (run + 1) * width] = block
        line += height
    pack = places[0] * 4 + places[4]
    row_places = lax.broadcasted_iota(jnp.int32, (1, SEQ), 1)
    column_places = lax.broadcasted_iota(jnp.int32, (SEQ, 1), 0)
    page_row, page_column = jnp.zeros_like(row_places), jnp.zeros_like(column_places)
    end = jnp.int32(0)
    for page in range(lengths.shape[1]):
        end += lengths[pack, page]
        page_row += (row_places >= end).astype(jnp.int32)
        page_column += (column_places >= end).astype(jnp.int32)
    row_out[...] = page_row
    column_out[...] = page_column


def cast_pass(order, places, lengths, left, right, down):
    rows = left.shape[0]
    return order.call(
        cast_kernel,
        [places, lengths, left, right, down],
        [in_smem] * 2 + [in_vmem] * 3,
        [
            shape_of((rows, D + FF), bf16),
            shape_of(down.shape, bf16),
            shape_of((rows, D + LEAD), bf16),
            shape_of((rows + sum(rows * width // (4 * D) for _, width in RUNS), 2 * D), bf16),
            shape_of((1, SEQ), jnp.int32),
            shape_of((SEQ, 1), jnp.int32),
        ],
        [in_vmem] * 6,
        limit=16,
        name="cast",
    )


def pairs_kernel(count, packed, places, rows, *rest):
    given, rest = ((), rest) if packed else (rest[:2], rest[2:])
    parts, rest = rest[:count], rest[count:]
    pair_outs, rest = rest[:GROUPS], rest[GROUPS:]
    normed_out, vectors_out, hidden_out, weight, wide_pair, last_pair, sems = rest
    pairs = [wide_pair.at[k] for k in range(GROUPS - 1)] + [last_pair]
    shard = D // count
    if packed:
        vectors = jnp.zeros((8, D), f32)
        line = lax.broadcasted_iota(jnp.int32, (8, D), 0)
        for k in range(count):
            block = parts[k][shard : shard + 16, :D].astype(f32)[:8]
            vectors += pltpu.roll(jnp.where(line < 7, block, 0.0), places[k] * shard, 1)
            start = pl.multiple_of(places[k] * D, 128)
            hidden_out[:, pl.ds(start, D)] = block[7:8]
    else:
        vectors = given[0][...]
        hidden_out[...] = given[1][...]
    vectors_out[...] = vectors
    for k, part in enumerate(parts):
        weight[pl.ds(pl.multiple_of(places[k] * shard, 16), shard)] = part[:shard, D:]
    scaled, _ = normalise(rows[...].astype(f32))
    normed_out[...] = (scaled * vectors[0:1] + vectors[1:2]).astype(bf16)
    for kind in range(2):
        line = vectors[6:7, kind * PART : (kind + 1) * PART]
        last_pair[kind, SEQ:] = jnp.concatenate([line] * 16, axis=0).astype(bf16)
    copies = []
    for group in range(GROUPS):
        for kind in range(2):
            first = kind * D + group * PART
            block = dot(normed_out[...], weight[:, first : first + PART])
            pairs[group][kind, :SEQ] = block.astype(bf16)
        copies.append(pltpu.make_async_copy(pairs[group], pair_outs[group], sems.at[group]))
        copies[-1].start()
    for copy in copies:
        copy.wait()


def pairs_pass(order, places, rows, parts, given=(), waits=()):
    count = len(parts)
    outs = order.call(
        functools.partial(pairs_kernel, count, not given),
        [places, rows, *given, *parts],
        [in_smem] + [in_vmem] * (1 + len(given) + count),
        [shape_of((2, SEQ, PART), bf16)] * (GROUPS - 1)
        + [
            shape_of((2, SEQ + 16, PART), bf16),
            shape_of((SEQ, D), bf16),
            shape_of((8, D), f32),
            shape_of((1, FF), f32),
        ],
        [in_hbm] * GROUPS + [in_vmem] * 3,
        scratch=[
            pltpu.VMEM((D, 2 * D), bf16),
            pltpu.VMEM((GROUPS - 1, 2, SEQ, PART), bf16),
            pltpu.VMEM((2, SEQ + 16, PART), bf16),
            pltpu.SemaphoreType.DMA((GROUPS,)),
        ],
        limit=16,
        name="pairs",
        waits=waits,
    )
    return outs[:GROUPS], *outs[GROUPS:]


def queries_kernel(places, normed, *rest):
    parts, (out, weight) = rest[:-2], rest[-2:]
    shard = D // len(parts)
    for k, part in enumerate(parts):
        weight[pl.ds(pl.multiple_of(places[k] * shard, 16), shard)] = part[:shard, :D]
    for first in range(0, D, PART):
        block = dot(normed[...], weight[:, first : first + PART])
        out[:, first : first + PART] = block.astype(bf16)


def queries_pass(order, places, normed, parts):
    return order.call(
        queries_kernel,
        [places, normed, *parts],
        [in_smem] + [in_vmem] * (1 + len(parts)),
        [shape_of((SEQ, D), bf16)],
        [in_vmem],
        scratch=[pltpu.VMEM((D, D), bf16)],
        limit=16,
        name="queries",
    )[0]


def fill_page_bias(page_row, page_column, bias):
    for index, (low, high) in enumerate(WINDOWS):
        start = index * BLOCK
        same = page_column[low:high] == page_row[:, start : start + BLOCK]
        bias[index, : high - low] = jnp.where(same, 0.0, masked_score)


def two_heads(block):
    lane = lax.broadcasted_iota(jnp.int32, block.shape, 1)
    zero = jnp.zeros_like(block)
    return jnp.concatenate(
        [jnp.where(lane < HEAD_DIM, block, zero), jnp.where(lane < HEAD_DIM, zero, block)], axis=0
    )


def head_rows(both):
    return jnp.concatenate([both[:HEAD_DIM, :BLOCK], both[HEAD_DIM:, BLOCK:]], axis=0).T


def page_bias(bias, index, size):
    block = bias[index, :size]
    return jnp.concatenate([block, block], axis=1)


def attend_kernel(
    query_first, query, own, other, page_row, page_column, context, log_total, bias
):
    fill_page_bias(page_row, page_column, bias)

    def pair(step, carry):
        lanes = pl.ds(pl.multiple_of(step * PAIR, PAIR), PAIR)
        query_lanes = pl.ds(pl.multiple_of((query_first + step) * PAIR, PAIR), PAIR)
        for index, (low, high) in enumerate(WINDOWS):
            start = index * BLOCK
            queries = two_heads(query[start : start + BLOCK, query_lanes] * score_scale)
            allowed = page_bias(bias, index, high - low)
            scores = dot_nt(own[0, low:high, lanes], queries) + allowed
            scores_two = dot_nt(other[0, low:high, lanes], queries) + allowed
            largest = jnp.maximum(
                jnp.max(scores, axis=0, keepdims=True), jnp.max(scores_two, axis=0, keepdims=True)
            )
            exponent = jnp.exp(scores - largest)
            exponent_two = jnp.exp(scores_two - largest)
            total = column_sums(exponent) + column_sums(exponent_two)
            inverse = 1.0 / total
            shares = (exponent * inverse).astype(bf16)
            shares_two = (exponent_two * inverse).astype(bf16)
            both = dot_tn(own[1, low:high, lanes], shares)
            both += dot_tn(other[1, low:high, lanes], shares_two)
            context[start : start + BLOCK, lanes] = head_rows(both).astype(bf16)
            log_total[step, index : index + 1] = largest + jnp.log(total)
        return carry

    lax.fori_loop(0, own.shape[2] // PAIR, pair, 0)


def attend(order, query_first, queries, own, other, page_row, page_column, waits=()):
    width = own.shape[2]
    return order.call(
        functools.partial(attend_kernel, query_first),
        [queries, own, other, page_row, page_column],
        [in_vmem] * 5,
        [
            shape_of((SEQ, width), bf16),
            shape_of((width // PAIR, len(WINDOWS), 2 * BLOCK), f32),
        ],
        [in_vmem] * 2,
        scratch=[pltpu.VMEM((len(WINDOWS), WINDOW, BLOCK), f32)],
        limit=12,
        name="attend",
        cost=60,
        waits=waits,
    )


def attend_back_kernel(
    query_first,
    query,
    own,
    other,
    context_grad,
    log_total,
    page_row,
    page_column,
    *rest,
):
    *given, query_grad, own_grad, other_grad, bias, other_sum = rest
    fill_page_bias(page_row, page_column, bias)
    own_grad[...] = jnp.zeros_like(own_grad)
    other_sum[...] = jnp.zeros_like(other_sum)

    def pair(step, carry):
        lanes = pl.ds(pl.multiple_of(step * PAIR, PAIR), PAIR)
        query_lanes = pl.ds(pl.multiple_of((query_first + step) * PAIR, PAIR), PAIR)
        for index, (low, high) in enumerate(WINDOWS):
            start = index * BLOCK
            queries = two_heads(query[start : start + BLOCK, query_lanes] * score_scale)
            grads = two_heads(context_grad[start : start + BLOCK, query_lanes])
            log_row = log_total[step, index : index + 1]
            allowed = page_bias(bias, index, high - low)
            keys, keys_two = own[0, low:high, lanes], other[0, low:high, lanes]
            shares = jnp.exp(dot_nt(keys, queries) + allowed - log_row)
            shares_two = jnp.exp(dot_nt(keys_two, queries) + allowed - log_row)
            share_grad = dot_nt(own[1, low:high, lanes], grads)
            share_grad_two = dot_nt(other[1, low:high, lanes], grads)
            centre = column_sums(shares * share_grad) + column_sums(shares_two * share_grad_two)
            score_grad = (shares * (share_grad - centre)).astype(bf16)
            score_grad_two = (shares_two * (share_grad_two - centre)).astype(bf16)
            own_grad[0, low:high, lanes] += dot(score_grad, queries)
            own_grad[1, low:high, lanes] += dot(shares.astype(bf16), grads)
            other_sum[0, low:high, lanes] += dot(score_grad_two, queries)
            other_sum[1, low:high, lanes] += dot(shares_two.astype(bf16), grads)
            both = dot_tn(keys, score_grad) + dot_tn(keys_two, score_grad_two)
            query_grad[start : start + BLOCK, lanes] = (head_rows(both) * score_scale).astype(bf16)
        return carry

    lax.fori_loop(0, own_grad.shape[2] // PAIR, pair, 0)
    other_grad[:, :SEQ] = other_sum[...].astype(bf16)
    if given:
        for kind in range(2):
            line = given[0][:, kind * PART : (kind + 1) * PART]
            other_grad[kind, SEQ:] = jnp.concatenate([line] * 2, axis=0).astype(bf16)


def attend_back(
    order, query_first, queries, own, other, context_grad, logs, page_row, page_column, given
):
    return order.call(
        functools.partial(attend_back_kernel, query_first),
        [queries, own, other, context_grad, logs, page_row, page_column, *given],
        [in_vmem] * (7 + len(given)),
        [
            shape_of((SEQ, PART), bf16),
            shape_of((2, SEQ, PART), f32),
            shape_of((2, SEQ + 16 * len(given), PART), bf16),
        ],
        [in_vmem] * 3,
        scratch=[
            pltpu.VMEM((len(WINDOWS), WINDOW, BLOCK), f32),
            pltpu.VMEM((2, SEQ, PART), f32),
        ],
        limit=16,
        name="attend_back",
        cost=60,
    )


def partner_cross(pair):
    rows = pair[:, SEQ:].astype(f32)
    return jnp.concatenate([rows[0, :1], rows[1, :1]], axis=1)


def join_blocks(places, wides, downs, leads, halves, wide, down):
    rows = wide.shape[0] // (len(wides) + len(leads))
    for k, part in enumerate(wides):
        wide[pl.ds(pl.multiple_of(places[k] * rows, 16), rows)] = part[...]
        down[k] = downs[k][...]
    turn = places[4] % 2
    for k, part in enumerate(leads):
        first = places[len(wides) + k] * rows
        wide[pl.ds(pl.multiple_of(first, 16), rows), : part.shape[1]] = part[...]
        for side, half in enumerate(halves[k]):
            place = turn if side == 0 else 1 - turn
            line = rows
            for column, width in RUNS:
                runs = 2 * D // width
                height = rows // 2 // runs
                for run in range(runs):
                    start = pl.multiple_of(first + place * (rows // 2) + run * height, 16)
                    block = half[line : line + height, run * width : (run + 1) * width]
                    wide[pl.ds(start, height), D + column : D + column + width] = block
                line += height
            for run in range(2):
                start = pl.multiple_of((2 * place + run) * rows, 16)
                down[len(wides) + k, pl.ds(start, rows)] = half[:rows, run * D : (run + 1) * D]


def middle_kernel(kinds, places, rows, *rest):
    contexts, rest = rest[:GROUPS], rest[GROUPS:]
    (tangent, vectors, partner, hidden_bias), rest = rest[:4], rest[4:]
    wides, downs, leads = [], [], []
    for group, size in zip((wides, downs, leads), kinds):
        group += rest[:size]
        rest = rest[size:]
    halves = [rest[2 * k : 2 * k + 2] for k in range(kinds[2])]
    rest = rest[2 * kinds[2] :]
    middle_out, second_out, hidden_out, slope_out, modal_out, inner_out, wide, down, total = rest
    join_blocks(places, wides, downs, leads, halves, wide, down)
    count = down.shape[0]
    middle = rows[...].astype(f32)
    for group, context in enumerate(contexts):
        middle += dot(context[...], wide[group * PART : (group + 1) * PART, :D])
    middle_out[...] = middle
    scaled, _ = normalise(middle)
    second_out[...] = (scaled * vectors[2:3] + vectors[3:4]).astype(bf16)
    total[...] = middle + vectors[4:5]
    slot = FF // count
    size = 384
    for k in range(count):
        for first in range(0, slot, size):
            start = places[k] * slot + first
            part = pl.ds(pl.multiple_of(start, 128), size)
            column = pl.ds(pl.multiple_of(D + start, 128), size)
            upper = dot(second_out[...], wide[:, column]) + hidden_bias[:, part]
            square = upper * upper
            angle = jnp.tanh(upper * (gelu_scale + (gelu_cubic * gelu_scale) * square))
            half = 0.5 + 0.5 * angle
            hidden = (upper * half).astype(bf16)
            hidden_out[:, part] = hidden
            bend = 2.0 * gelu_scale + (6.0 * gelu_cubic * gelu_scale) * square
            slope_out[:, part] = (half + half * (1.0 - half) * (upper * bend)).astype(bf16)
            total[...] += dot(hidden, down[k, first : first + size])
    modal_out[...] = total[...].astype(bf16)
    modal = modal_out[...].astype(f32)
    own = jnp.sum(modal * vectors[5:6], axis=1, keepdims=True)
    cross = jnp.sum(modal * partner_cross(partner), axis=1, keepdims=True)
    met = jnp.sum(modal * tangent[...].astype(f32), axis=1, keepdims=True)
    lane = lax.broadcasted_iota(jnp.int32, (SEQ, 128), 1)
    columns = jnp.where(lane == 0, own, jnp.where(lane == 1, cross, met))
    inner_out[...] = columns.T[:8]


def middle_pass(
    order, places, rows, contexts, tangent, vectors, partner, hidden_bias, wides, downs, leads, halves
):
    count = len(wides) + len(leads)
    parts = [*wides, *downs, *leads] + [piece for pair in halves for piece in pair]
    return order.call(
        functools.partial(middle_kernel, (len(wides), len(downs), len(leads))),
        [places, rows, *contexts, tangent, vectors, partner, hidden_bias, *parts],
        [in_smem] + [in_vmem] * (5 + GROUPS + len(parts)),
        [
            shape_of((SEQ, D), f32),
            shape_of((SEQ, D), bf16),
            shape_of((SEQ, FF), bf16),
            shape_of((SEQ, FF), bf16),
            shape_of((SEQ, D), bf16),
            shape_of((8, SEQ), f32),
            shape_of((D, D + FF), bf16),
            shape_of((count, FF // count, D), bf16),
        ],
        [in_vmem] * 8,
        scratch=[pltpu.VMEM((SEQ, D), f32)],
        limit=16,
        name="middle",
    )


def gate_kernel(
    own,
    other,
    tangent,
    partner_tangent,
    vectors,
    partner,
    grad_out,
    low_out,
    columns_out,
    sums,
):
    gate = jax.nn.sigmoid(own[0:1] + other[1:2])
    gate_two = jax.nn.sigmoid(other[0:1] + own[1:2])
    logit = other[2:3] * gate * (1.0 - gate)
    logit_two = own[2:3] * gate_two * (1.0 - gate_two)
    padding = jnp.zeros((124, SEQ), f32)
    columns = jnp.concatenate([gate, logit, gate_two, logit_two, padding], axis=0).T
    columns_out[...] = columns
    grad = (
        tangent[...].astype(f32)
        + columns[:, 1:2] * vectors[5:6]
        + partner_tangent[...].astype(f32) * columns[:, 2:3]
        + columns[:, 3:4] * partner_cross(partner)
    )
    grad_out[...] = grad
    low_out[...] = grad.astype(bf16)
    sums[...] = column_sums(grad)


def gate_pass(order, own, other, tangent, partner_tangent, vectors, partner):
    return order.call(
        gate_kernel,
        [own, other, tangent, partner_tangent, vectors, partner],
        [in_vmem] * 6,
        [
            shape_of((SEQ, D), f32),
            shape_of((SEQ, D), bf16),
            shape_of((SEQ, 128), f32),
            shape_of((1, D), f32),
        ],
        [in_vmem] * 4,
        name="gate",
    )


def mix_kernel(own, other, columns, mixed):
    mixed[...] = (
        own[...].astype(f32) + columns[:, 0:1] * other[...].astype(f32)
    ).astype(bf16)


def mix_pass(order, own, other, columns, waits=()):
    return order.call(
        mix_kernel,
        [own, other, columns],
        [in_vmem] * 3,
        [shape_of((SEQ, D), bf16)],
        [in_vmem],
        name="mix",
        cost=60,
        waits=waits,
    )[0]


def gate_sums_kernel(own, columns, out):
    rows = own[...].astype(f32)
    out[...] = jnp.zeros_like(out)
    out[0:1] = column_sums(columns[:, 1:2] * rows)
    out[1:2] = column_sums(columns[:, 3:4] * rows)


def gate_sums_pass(order, own, columns):
    return order.call(
        gate_sums_kernel, [own, columns], [in_vmem] * 2, [shape_of((8, D), f32)], [in_vmem], name="gate_sums"
    )[0]


def chain_kernel(places, low, grad, slope, middle, vectors, wide, down, *rest):
    total_out, total_low_out, context_out, upper_out, upper_sums, gain_sums, bias_sums = rest[:7]
    normed_grad = rest[7]
    normed_grad[...] = jnp.zeros_like(normed_grad)
    count = down.shape[0]
    slot = FF // count
    size = 384
    for k in range(count):
        for first in range(0, slot, size):
            start = places[k] * slot + first
            part = pl.ds(pl.multiple_of(start, 128), size)
            column = pl.ds(pl.multiple_of(D + start, 128), size)
            upper = dot_nt(low[...], down[k, first : first + size]) * slope[:, part].astype(f32)
            upper_sums[:, part] = column_sums(upper)
            upper_low = upper.astype(bf16)
            upper_out[:, part] = upper_low
            normed_grad[...] += dot_nt(upper_low, wide[:, column])
    scaled, root = normalise(middle[...])
    incoming = normed_grad[...]
    gain_sums[...] = column_sums(incoming * scaled)
    bias_sums[...] = column_sums(incoming)
    total = grad[...] + norm_back(scaled, root, vectors[2:3], incoming)
    total_out[...] = total
    total_low_out[...] = total.astype(bf16)
    context_out[...] = dot_nt(total_low_out[...], wide[:, :D]).astype(bf16)


def chain_pass(order, places, low, grad, slope, middle, vectors, wide, down):
    return order.call(
        chain_kernel,
        [places, low, grad, slope, middle, vectors, wide, down],
        [in_smem] + [in_vmem] * 7,
        [
            shape_of((SEQ, D), f32),
            shape_of((SEQ, D), bf16),
            shape_of((SEQ, D), bf16),
            shape_of((SEQ, FF), bf16),
            shape_of((1, FF), f32),
            shape_of((1, D), f32),
            shape_of((1, D), f32),
        ],
        [in_vmem] * 7,
        scratch=[pltpu.VMEM((SEQ, D), f32)],
        limit=20,
        name="chain",
    )


def slots_of(count):
    return (list(range(0, count, 2)), list(range(1, count, 2)))


def block_shapes(widths, count):
    near, far = slots_of(count)
    rows = D // count
    outs = []
    for width in widths:
        outs.append(shape_of((len(near), rows, width), bf16))
        if far:
            outs.append(shape_of((len(far), rows, width), bf16))
    return outs


def store_blocks(places, count, products, widths, outs, whole):
    near, far = slots_of(count)
    rows = D // count
    products = list(products)
    each = 2 if far else 1
    for index, width in enumerate(widths):
        low = 0
        while low < width:
            left, right = products.pop(0)
            whole[:, low : low + right.shape[1]] = dot(left, right).astype(bf16)
            low += right.shape[1]
        for out, slots in zip(outs[each * index : each * index + each], (near, far)):
            for place, slot in enumerate(slots):
                begin = pl.multiple_of(places[slot] * rows, 16)
                out[place] = whole[pl.ds(begin, rows), :width]


def up_grads_kernel(count, widths, places, second, upper, *rest):
    turned = second[...].T
    products = [(turned, upper[:, k : k + 512]) for k in range(0, FF, 512)]
    store_blocks(places, count, products, widths, rest[:-1], rest[-1])


def up_grads(order, places, second, upper, widths, count):
    outs = block_shapes(widths, count)
    return order.call(
        functools.partial(up_grads_kernel, count, widths),
        [places, second, upper],
        [in_smem] + [in_vmem] * 2,
        outs,
        [in_vmem] * len(outs),
        scratch=[pltpu.VMEM((D, max(widths)), bf16)],
        limit=16,
        name="up_grads",
    )


def lead_grads_kernel(count, places, context, context_two, low, normed, *rest):
    queries, (own, returned), rest = rest[:GROUPS], rest[GROUPS : GROUPS + 2], rest[GROUPS + 2 :]
    pair_low, outs, whole = rest[0], rest[1:-1], rest[-1]
    pair_low[...] = (own[...] + returned[:, :SEQ].astype(f32)).astype(bf16)
    turned = jnp.concatenate([context[...].T, context_two[...].T], axis=0)
    products = [(turned, low[:, k : k + PART]) for k in range(0, D, PART)]
    turned = normed[...].T
    products += [(turned, query[...]) for query in queries]
    products += [(turned, pair_low[kind]) for kind in range(2)]
    store_blocks(places, count, products, [3 * D], outs, whole)


def lead_grads(order, places, contexts, low, normed, queries, own, returned, count):
    outs = block_shapes([3 * D], count)
    args = [*contexts, low, normed, *queries, own, returned]
    return order.call(
        functools.partial(lead_grads_kernel, count),
        [places, *args],
        [in_smem] + [in_vmem] * len(args),
        [shape_of(own.shape, bf16)] + outs,
        [in_vmem] * (1 + len(outs)),
        scratch=[pltpu.VMEM((D, 3 * D), bf16)],
        limit=16,
        name="lead_grads",
    )


def down_grads_kernel(count, first, height, fold, places, low, hidden, *outs):
    near, far = slots_of(count)
    width = FF // count
    turned = low[:, first : first + height].T
    rows = height // fold
    for out, slots in zip(outs, (near, far)):
        for place, slot in enumerate(slots):
            begin = pl.multiple_of(places[slot] * width, 128)
            block = dot(turned, hidden[:, pl.ds(begin, width)]).astype(bf16)
            for k in range(fold):
                out[place, :, k * width : (k + 1) * width] = block[k * rows : (k + 1) * rows]


def down_grads(order, places, low, hidden, first, height, fold, count):
    near, far = slots_of(count)
    width = FF // count
    outs = [shape_of((len(near), height // fold, fold * width), bf16)]
    if far:
        outs.append(shape_of((len(far), height // fold, fold * width), bf16))
    return order.call(
        functools.partial(down_grads_kernel, count, first, height, fold),
        [places, low, hidden],
        [in_smem, in_vmem, in_vmem],
        outs,
        [in_vmem] * len(outs),
        limit=16,
        name="down_grads",
    )


def first_kernel(count, places, total, rows, vectors, normed, own, returned, *rest):
    parts, rest = rest[:count], rest[count:]
    queries, pair, rest = rest[:GROUPS], rest[GROUPS], rest[GROUPS + 1 :]
    gain_two, bias_two, output_bias, gate_own, hidden_bias = rest[:5]
    grad_out, outs = rest[5], rest[6:-5]
    pair_low, normed_grad, weight, whole, short = rest[-5:]
    pair_low[...] = (own[...] + returned[:, :SEQ].astype(f32)).astype(bf16)
    assemble(places, parts, weight)
    for group, pairs in enumerate((pair, pair_low)):
        start = group * PART
        block = dot_nt(queries[group][...], weight[:, start : start + PART])
        for kind in range(2):
            start = (kind + 1) * D + group * PART
            block += dot_nt(pairs[kind], weight[:, start : start + PART])
        if group == 0:
            normed_grad[...] = block
        else:
            normed_grad[...] += block
    scaled, root = normalise(rows[...].astype(f32))
    incoming = normed_grad[...]
    short[...] = jnp.zeros_like(short)
    short[0:1] = column_sums(incoming * scaled)
    short[1:2] = column_sums(incoming)
    for line, member in enumerate((gain_two, bias_two, output_bias)):
        short[line + 2 : line + 3] = member[...]
    short[5:6] = gate_own[0:1]
    for kind in range(2):
        line = returned[kind, SEQ : SEQ + 8].astype(f32)
        short[6:7, kind * PART : (kind + 1) * PART] = line[1:2]
    for line in range(FF // D):
        short[line + 8 : line + 9] = hidden_bias[:, line * D : (line + 1) * D]
    grad_out[...] = total[...] + norm_back(scaled, root, vectors[0:1], incoming)
    turned = normed[...].T
    for kind in range(2):
        whole[:, kind * PART : (kind + 1) * PART] = dot(turned, pair_low[kind]).astype(bf16)
    height = D // count
    for out, slots in zip(outs, slots_of(count)):
        for place, slot in enumerate(slots):
            begin = pl.multiple_of(places[slot] * height, 16)
            out[place * height : (place + 1) * height] = whole[pl.ds(begin, height)]
        out[len(slots) * height :] = short[...].astype(bf16)


def first_pass(
    order, places, total, rows, vectors, normed, own, returned, parts, queries, pair, short
):
    count = len(parts)
    args = [total, rows, vectors, normed, own, returned, *parts, *queries, pair, *short]
    outs = [
        shape_of((len(slots) * (D // count) + 16, 2 * PART), bf16) for slots in slots_of(count) if slots
    ]
    return order.call(
        functools.partial(first_kernel, count),
        [places, *args],
        [in_smem] + [in_vmem] * len(args),
        [shape_of((SEQ, D), f32)] + outs,
        [in_vmem] * (1 + len(outs)),
        scratch=[
            pltpu.VMEM((2, SEQ, PART), bf16),
            pltpu.VMEM((SEQ, D), f32),
            pltpu.VMEM((D, 3 * D), bf16),
            pltpu.VMEM((D, 2 * PART), bf16),
            pltpu.VMEM((16, D), f32),
        ],
        limit=20,
        name="first",
    )


def settle_kernel(kind, count, outs, places, *refs):
    totals, returned, refs = refs[:count], refs[count : 2 * count], refs[2 * count :]
    targets, (scratch, sems) = refs[:outs], (refs[outs : 2 * outs], refs[2 * outs])
    copies = []

    def leave(index, *where):
        source, target = scratch[index].at[where], targets[index].at[where]
        copies.append(pltpu.make_async_copy(source, target, sems.at[len(copies)]))
        copies[-1].start()

    inner = jnp.logical_and(places[4] > 0, places[4] < 3)
    values = [jnp.where(inner, a[...], b[...]).astype(f32) for a, b in zip(totals, returned)]
    out, every = scratch[0], slice(None)
    if kind == "turn":
        first = 0
        for value in values:
            rows = value.shape[0]
            start = first
            for k in range(0, value.shape[1], D):
                out[:, first : first + rows] = value[:, k : k + D].T
                first += rows
            leave(0, every, pl.ds(start, first - start))
    elif kind == "columns":
        first = 0
        for value in values:
            out[:, first : first + value.shape[1]] = value
            leave(0, every, pl.ds(first, value.shape[1]))
            first += value.shape[1]
    else:
        scratch[1][...] = values[0][:, :D]
        leave(1, every)
        out[:, :D] = values[0][:, D:]
        for group, value in enumerate(values[1:]):
            for part in range(2):
                start = (part + 1) * D + group * PART
                out[:, start : start + PART] = value[:, part * PART : (part + 1) * PART]
        leave(0, every)
    for copy in copies:
        copy.wait()


def settle(order, kind, places, blocks, dims):
    count = len(blocks)
    found = order.call(
        functools.partial(settle_kernel, kind, count, len(dims)),
        [places] + [block[0] for block in blocks] + [block[1] for block in blocks],
        [in_smem] + [in_vmem] * (2 * count),
        [shape_of(each, f32) for each in dims],
        [in_hbm] * len(dims),
        scratch=[pltpu.VMEM(each, f32) for each in dims] + [pltpu.SemaphoreType.DMA((8,))],
        name="settle",
    )
    return found[0] if len(dims) == 1 else found


def last_settle_kernel(places, total, returned, given, out, *rest):
    short_outs, (scratch, sems) = rest[:8], rest[8:]
    inner = jnp.logical_and(places[4] > 0, places[4] < 3)
    value = jnp.where(inner, total[...], returned[...]).astype(f32)
    rows = scratch.shape[1]
    copies = []
    for part in range(2):
        scratch[part] = value[:rows, part * PART : (part + 1) * PART]
        place = out.at[:, pl.ds((part + 1) * D + PART, PART)]
        copies.append(pltpu.make_async_copy(scratch.at[part], place, sems.at[part]))
        copies[-1].start()
    short = value[rows:]
    turned = pltpu.roll(short, D - places[0] * rows, 1)
    for line in range(7):
        short_outs[line][...] = turned[line : line + 1, :rows].reshape(rows)
    line = lax.broadcasted_iota(jnp.int32, short.shape, 0)
    hidden = jnp.sum(jnp.where(line == 8 + places[0], short, 0.0), axis=0)
    short_outs[7][...] = hidden
    for copy in copies:
        copy.wait()


def last_settle(order, places, block, given):
    rows = given.shape[0]
    shorts = [shape_of((rows,), f32)] * 7 + [shape_of((D,), f32)]
    found = order.call(
        last_settle_kernel,
        [places, block[0], block[1], given],
        [in_smem, in_vmem, in_vmem, in_hbm],
        [shape_of(given.shape, f32)] + shorts,
        [in_hbm] + [in_vmem] * 8,
        scratch=[pltpu.VMEM((2, rows, PART), f32), pltpu.SemaphoreType.DMA((2,))],
        name="last_settle",
        aliases={3: 0},
    )
    return found[0], found[1:]


def swap_bit(value, axis, bit):
    size = lax.axis_size(axis)
    return lax.ppermute(value, axis, [(source, source ^ (1 << bit)) for source in range(size)])


def from_partner(value):
    size = lax.axis_size("stream")
    half = size // 2
    return lax.ppermute(value, "stream", [(source, (source + half) % size) for source in range(size)])


def along(value, pairs):
    return lax.ppermute(value, "dp", pairs)


def up_line(value, steps):
    return along(value, [(floor, floor + 1) for floor in range(steps - 1, 3)])


def down_line(value, steps):
    return along(value, [(floor, floor - 1) for floor in range(1, 5 - steps)])


def swap_outer(value):
    return along(value, [(0, 1), (1, 0), (2, 3), (3, 2)])


def to_inner(value):
    return along(value, [(0, 1), (3, 2)])


def over_middle(value):
    return along(value, [(1, 2), (2, 1)])


def to_outer(value):
    return along(value, [(1, 0), (2, 3)])


def core(value):
    return swap_bit(value, "stream", 0)


def across(value):
    return swap_bit(value, "stream", 1)


def modality_groups():
    size = lax.axis_size("stream")
    half = size // 2
    return [list(range(half)), list(range(half, size))]


def body(
    regions,
    cotangent,
    page_lens,
    qkv_weight,
    out_weight,
    up_weight,
    down_weight,
    ln1_gain,
    ln1_bias,
    ln2_gain,
    ln2_bias,
    up_bias,
    down_bias,
    gate_own,
    gate_other,
):
    half = lax.axis_size("stream") // 2
    depth = lax.axis_size("dp")
    paired = half == 4 and depth == 4
    side = lax.axis_index("stream") % half
    floor = lax.axis_index("dp")
    count = 4 if paired else 1
    slots = jnp.arange(4, dtype=jnp.int32)
    picks = jnp.bitwise_xor(side.astype(jnp.int32), slots) if paired else jnp.zeros_like(slots)
    places = jnp.concatenate([picks, floor.astype(jnp.int32)[None]])
    order = Order()
    short = (ln1_gain, ln1_bias, ln2_gain, ln2_bias, down_bias, gate_own, gate_other, up_bias)
    partner_tangent = from_partner(cotangent)

    def attend_group(group, waits=()):
        context, log_total = attend(
            order,
            group * PART // PAIR,
            queries,
            own_pairs[group],
            other_pairs[group],
            page_row,
            page_column,
            waits,
        )
        contexts.append(context)
        logs.append(log_total)

    contexts, logs = [], []
    if paired:
        qkv_shard = first_cast_pass(order, qkv_weight, short)
        qkv_across, qkv_near = across(qkv_shard), core(qkv_shard)
        wide_shard, down_shard, lead, half_own, page_row, page_column = cast_pass(
            order, places, page_lens, out_weight, up_weight, down_weight
        )
        wide_near, down_near = core(wide_shard), core(down_shard)
        (qkv_across,) = order.hold([qkv_across], waits=[partner_tangent, qkv_near])
        qkv_far, half_own = core(qkv_across), across(half_own)
        qkv_parts = [qkv_shard, qkv_near, qkv_across, qkv_far]
        own_pairs, normed, vectors, hidden_bias = pairs_pass(
            order, places, regions, qkv_parts, waits=[wide_near, down_near]
        )
        queries = queries_pass(order, places, normed, qkv_parts)
        other_pairs = [from_partner(pair) for pair in own_pairs]
        lead_across = across(lead)
        (half_own,) = order.hold([half_own])
        half_other, half_own_far = swap_outer(half_own), core(half_own)
        attend_group(0)
        (lead_across,) = order.hold([lead_across])
        vectors = order.pause(vectors)
        (half_other,) = order.hold([half_other])
        half_other_far, lead_far = core(half_other), core(lead_across)
        attend_group(1)
        wides, downs = [wide_shard, wide_near], [down_shard, down_near]
        leads = [lead_across, lead_far]
        halves = [(half_own, half_other), (half_own_far, half_other_far)]
    else:
        lengths = lax.dynamic_slice_in_dim(page_lens, side * depth + floor, 1, 0)
        positions = jnp.arange(SEQ, dtype=jnp.int32)
        page_ends = jnp.cumsum(lengths[0], dtype=jnp.int32)
        pages = jnp.sum((page_ends[:, None] <= positions[None, :]).astype(jnp.int32), axis=0)
        page_row, page_column = pages[None, :], pages[:, None]

        def gather(shard):
            return [
                lax.all_gather(shard, "stream", axis_index_groups=modality_groups(), tiled=True)
            ]

        packed = jnp.concatenate([member.astype(bf16) for member in short])[None]
        found = gather(packed)[0].astype(f32)
        shard = D // half
        rows = [found[:, k * shard : (k + 1) * shard].reshape(1, D) for k in range(7)]
        given = (
            jnp.concatenate(rows + [jnp.zeros((1, D), f32)], axis=0),
            found[:, 7 * shard :].reshape(1, FF),
        )
        qkv_parts = gather(qkv_weight.astype(bf16))
        wides = gather(jnp.concatenate([out_weight, up_weight], axis=1).astype(bf16))
        downs, leads, halves = gather(down_weight.astype(bf16)), [], []
        own_pairs, normed, vectors, hidden_bias = pairs_pass(
            order, places, regions, qkv_parts, given
        )
        queries = queries_pass(order, places, normed, qkv_parts)
        other_pairs = [from_partner(pair) for pair in own_pairs]
        for group in range(GROUPS):
            attend_group(group)

    middle, second, hidden, slope, modal, inner_own, wide, down = middle_pass(
        order,
        places,
        regions,
        contexts,
        partner_tangent,
        vectors,
        other_pairs[-1],
        hidden_bias,
        wides,
        downs,
        leads,
        halves,
    )
    inner_other = from_partner(inner_own)
    modal_grad, modal_low, columns, output_bias_grad = gate_pass(
        order, inner_own, inner_other, cotangent, partner_tangent, vectors, other_pairs[-1]
    )

    def attend_back_group(group):
        query_grad, own_grad, other_grad = attend_back(
            order,
            group * PART // PAIR,
            queries,
            own_pairs[group],
            other_pairs[group],
            context_grad,
            logs[group],
            page_row,
            page_column,
            [gate_sums] if group == GROUPS - 1 else [],
        )
        query_grads.append(query_grad)
        own_grads.append(own_grad)
        returned.append(from_partner(other_grad))

    def last_pass(pair_low):
        short_grads = (
            gain_two_grad,
            bias_two_grad,
            output_bias_grad,
            gate_sums,
            hidden_bias_grad,
        )
        return first_pass(
            order,
            places,
            middle_grad,
            regions,
            vectors,
            normed,
            own_grads[1],
            returned[1],
            qkv_parts,
            query_grads,
            pair_low,
            short_grads,
        )

    query_grads, own_grads, returned = [], [], []
    back = (order, places, modal_low, modal_grad, slope, middle, vectors, wide, down)
    if paired:
        d1, far = down_grads(order, places, modal_low, hidden, 0, 384, 2, count)
        d1_core = core(far)
        d2, far = down_grads(order, places, modal_low, hidden, 384, 384, 2, count)
        d2_core = core(far)
        d1, away = sums_pass(order, places, folds=[(d1, d1_core, [FF // 2])])
        d1_in = across(away)
        d2, d2_away = sums_pass(order, places, folds=[(d2, d2_core, [FF // 2])])
        middle_grad, middle_low, context_grad, upper_low, *rest = chain_pass(*back)
        hidden_bias_grad, gain_two_grad, bias_two_grad = rest
        d1 = sums_pass(order, places, adds=[(d1, d1_in)])
        d1_in = to_inner(d1)
        (d2_away,) = order.hold([d2_away])
        d2_in = across(d2_away)
        gate_sums = gate_sums_pass(order, modal, columns)
        u1, far_one, u2, far_two = up_grads(
            order, places, second, upper_low, [FF // 2, FF // 2], count
        )
        u1_core, u2_core = core(far_one), core(far_two)
        attend_back_group(0)
        d2, d1 = sums_pass(order, places, adds=[(d2, d2_in), (d1, d1_in)])
        d2_in, d1_mid = to_inner(d2), over_middle(d1)
        columns = order.pause(columns)
        u1, away = sums_pass(order, places, folds=[(u1, u1_core, [FF // 2])])
        u1_in = across(away)
        u2, away = sums_pass(order, places, folds=[(u2, u2_core, [FF // 2])])
        attend_back_group(1)
        d2, u1, u1_pay = sums_pass(
            order, places, adds=[(d2, d2_in)], pays=[(u1, u1_in, d1, d1_mid)]
        )
        u1_in, d2_mid = swap_outer(u1_pay), over_middle(d2)
        (away,) = order.hold([away])
        u2_in = across(away)
        pair_low, lead_near, lead_far = lead_grads(
            order, places, contexts, middle_low, normed, query_grads, own_grads[0], returned[0], count
        )
        lead_core = core(lead_far)
        u1, u2, u2_pay = sums_pass(
            order, places, adds=[(u1, u1_in)], pays=[(u2, u2_in, d2, d2_mid)]
        )
        d1_out = u1_in
        u2_in, u1_mid = swap_outer(u2_pay), over_middle(u1)
        gate_sums = order.pause(gate_sums)
        oq, away, p1, away_two = sums_pass(
            order, places, folds=[(lead_near, lead_core, [2 * D, D])]
        )
        oq_in = across(away)
        region_grad, last_near, last_far = last_pass(pair_low)
        last_core = core(last_far)
        u2, oq, oq_pay = sums_pass(
            order, places, adds=[(u2, u2_in)], pays=[(oq, oq_in, u1, u1_mid)]
        )
        d2_out = u2_in
        oq_in, u2_mid = swap_outer(oq_pay), over_middle(u2)
        (away_two,) = order.hold([away_two])
        p1_in = across(away_two)
        modal = order.pause(modal)
        p2, away = sums_pass(order, places, folds=[(last_near, last_core, [D])])
        p2_in = across(away)
        down_grad = settle(order, "turn", places, [(u1_pay, d1_out), (u2_pay, d2_out)], [(D, D)])
        oq, u2, p1 = sums_pass(
            order, places, adds=[(oq, oq_in), (u2, u2_mid), (p1, p1_in)]
        )
        u1_out = oq_in
        oq_mid, u2_out, p1_in = over_middle(oq), to_outer(u2), to_inner(p1)
        p2 = sums_pass(order, places, adds=[(p2, p2_in)])
        p2_in = to_inner(p2)
        p1 = sums_pass(order, places, adds=[(p1, p1_in)])
        p1_mid = over_middle(p1)
        (modal,) = order.hold([modal])
        partner_modal = from_partner(modal)
        oq, p2 = sums_pass(order, places, adds=[(oq, oq_mid), (p2, p2_in)], waits=[u2_out])
        oq_out, p2_mid = to_outer(oq), over_middle(p2)
        up_grad = settle(order, "columns", places, [(oq_pay, u1_out), (u2, u2_out)], [(D // 4, FF)])
        p1 = sums_pass(order, places, adds=[(p1, p1_mid)])
        p1_out = to_outer(p1)
        p2 = sums_pass(order, places, adds=[(p2, p2_mid)])
        p2_out = to_outer(p2)
        mixed_rows = mix_pass(order, modal, partner_modal, columns, [oq_out])
        qkv_grad, out_grad = settle(
            order,
            "pairs",
            places,
            [(oq, oq_out), (p1, p1_out)],
            [(D // 4, 3 * D), (D // 4, D)],
        )
        qkv_grad, shorts = last_settle(order, places, (p2, p2_out), qkv_grad)
    else:
        (down_block,) = down_grads(order, places, modal_low, hidden, 0, D, 1, count)
        middle_grad, middle_low, context_grad, upper_low, *rest = chain_pass(*back)
        hidden_bias_grad, gain_two_grad, bias_two_grad = rest
        (up_block,) = up_grads(order, places, second, upper_low, [FF], count)
        gate_sums = gate_sums_pass(order, modal, columns)
        for group in range(GROUPS):
            attend_back_group(group)
        mixed_rows = mix_pass(order, modal, from_partner(modal), columns)
        pair_low, lead_block = lead_grads(
            order, places, contexts, middle_low, normed, query_grads, own_grads[0], returned[0], count
        )
        region_grad, last_block = last_pass(pair_low)
        lead_block = lead_block[0]
        short_rows = last_block[D:].astype(f32)

        def total(block):
            groups = modality_groups()
            owned = lax.psum_scatter(
                block.astype(f32), "stream", axis_index_groups=groups, tiled=True
            )
            return lax.psum(owned, "dp")

        down_grad = total(down_block[0].T)
        up_grad, out_grad = total(up_block[0]), total(lead_block[:, :D])
        qkv_grad = total(
            jnp.concatenate(
                [
                    lead_block[:, D : 2 * D + PART],
                    last_block[:D, :PART],
                    lead_block[:, 2 * D + PART :],
                    last_block[:D, PART:],
                ],
                axis=1,
            )
        )
        short_rows = lax.psum(
            lax.psum(short_rows, "stream", axis_index_groups=modality_groups()), "dp"
        )

        shard = D // half
        own_rows = lax.dynamic_slice_in_dim(short_rows, side * shard, shard, 1)
        hidden_rows = short_rows[8 : 8 + FF // D].reshape(FF)
        own_hidden = lax.dynamic_slice_in_dim(hidden_rows, side * (FF // half), FF // half, 0)
        shorts = [own_rows[k] for k in range(7)] + [own_hidden]
    return (
        mixed_rows,
        region_grad,
        qkv_grad,
        out_grad,
        up_grad,
        down_grad,
        shorts[0],
        shorts[1],
        shorts[2],
        shorts[3],
        shorts[7],
        shorts[4],
        shorts[5],
        shorts[6],
    )


def solution(mesh):
    in_specs = (
        P(("stream", "dp"), None),
        P(("stream", "dp"), None),
        P(),
        P("stream", None),
        P("stream", None),
        P("stream", None),
        P("stream", None),
        P("stream"),
        P("stream"),
        P("stream"),
        P("stream"),
        P("stream"),
        P("stream"),
        P("stream"),
        P("stream"),
    )
    out_specs = (
        P(("stream", "dp"), None),
        P(("stream", "dp"), None),
        P("stream", None),
        P("stream", None),
        P("stream", None),
        P("stream", None),
        P("stream"),
        P("stream"),
        P("stream"),
        P("stream"),
        P("stream"),
        P("stream"),
        P("stream"),
        P("stream"),
    )
    return jax.shard_map(body, mesh=mesh, in_specs=in_specs, out_specs=out_specs, check_vma=False)
```

```python
import functools
import math

import jax
import jax.numpy as jnp
from jax import lax
from jax.experimental import pallas as pl
from jax.experimental.pallas import tpu as pltpu
from jax.sharding import PartitionSpec as P

D = 768
HEADS = 12
HEAD_DIM = 64
FF = 3072
LEAD = FF - 1280
RUNS = ((LEAD, 768), (LEAD + 768, 512))
SEQ = 512
GROUPS = 2
PART = D // GROUPS
PAIR = 2 * HEAD_DIM
BLOCK = 128
REACH = 96
ROWS = 256
MIB = 1024 * 1024

epsilon = 1e-05
masked_score = -1e30
score_scale = HEAD_DIM ** (-0.5)
gelu_scale = math.sqrt(2.0 / math.pi)
gelu_cubic = 0.044715

f32 = jnp.float32
bf16 = jnp.bfloat16

WINDOWS = [
    (max(0, start - REACH), min(SEQ, start + BLOCK + REACH)) for start in range(0, SEQ, BLOCK)
]
WINDOW = BLOCK + 2 * REACH

in_smem = pl.BlockSpec(memory_space=pltpu.SMEM)
in_vmem = pl.BlockSpec(memory_space=pltpu.VMEM)
in_any = pl.BlockSpec(memory_space=pl.ANY)
in_hbm = pl.BlockSpec(memory_space=pltpu.HBM)


def shape_of(dims, dtype):
    return jax.ShapeDtypeStruct(dims, dtype)


def dot(left, right):
    return lax.dot_general(left, right, (((1,), (0,)), ((), ())), preferred_element_type=f32)


def dot_nt(left, right):
    return lax.dot_general(left, right, (((1,), (1,)), ((), ())), preferred_element_type=f32)


def dot_tn(left, right):
    return lax.dot_general(left, right, (((0,), (0,)), ((), ())), preferred_element_type=f32)


def normalise(values):
    average = jnp.mean(values, axis=-1, keepdims=True)
    centred = values - average
    spread = jnp.mean(centred * centred, axis=-1, keepdims=True)
    root = lax.rsqrt(spread + epsilon)
    return centred * root, root


def norm_back(scaled, root, gain, incoming):
    weighted = incoming * gain
    average = jnp.mean(weighted, axis=-1, keepdims=True)
    slope = jnp.mean(weighted * scaled, axis=-1, keepdims=True)
    return root * (weighted - average - scaled * slope)


def column_sums(values):
    return jnp.sum(values, axis=0, keepdims=True)


class Order:
    def __init__(self):
        self.token = []

    def call(
        self,
        kernel,
        args,
        in_specs,
        outs,
        out_specs,
        scratch=(),
        grid=(),
        limit=16,
        name=None,
        prefetch=None,
        waits=(),
        aliases=None,
        cost=0,
    ):
        given = len(args)
        extra = list(self.token) + list(waits)
        ahead = [] if prefetch is None else [prefetch]
        count = len(ahead)
        smallest = min(math.prod(out.shape) for out in outs)
        marked = smallest > 4096 and not aliases
        outs, out_specs = list(outs), list(out_specs)
        if marked:
            outs.append(shape_of((8, 128), f32))
            out_specs.append(in_vmem)
        place = count + given + len(extra) + len(outs) - 1

        def wrapped(*refs):
            used = list(refs[: count + given]) + list(refs[count + given + len(extra) :])
            if marked:
                refs[place][...] = jnp.zeros((8, 128), f32)
                used.pop(count + given + len(outs) - 1)
            kernel(*used)

        results = pl.pallas_call(
            wrapped,
            out_shape=outs,
            grid_spec=pltpu.PrefetchScalarGridSpec(
                num_scalar_prefetch=count,
                grid=grid,
                in_specs=list(in_specs) + [in_any] * len(extra),
                out_specs=out_specs,
                scratch_shapes=list(scratch),
            ),
            compiler_params=pltpu.CompilerParams(vmem_limit_bytes=limit * MIB),
            cost_estimate=pl.CostEstimate(flops=1 + cost * 10**9, bytes_accessed=1 + cost * MIB, transcendentals=cost * 10**6),
            input_output_aliases=aliases or {},
            name=name,
        )(*ahead, *args, *extra)
        self.token = [min(results, key=lambda out: out.size)]
        return list(results)[:-1] if marked else results

    def hold(self, arrays, waits=()):
        return self.call(
            lambda *refs: None,
            arrays,
            [in_any] * len(arrays),
            [shape_of(array.shape, array.dtype) for array in arrays],
            [in_any] * len(arrays),
            name="hold",
            cost=0,
            waits=waits,
            aliases={k: k for k in range(len(arrays))},
        )

    def pause(self, value):
        return self.call(
            lambda *refs: None,
            [value],
            [in_any],
            [shape_of(value.shape, value.dtype)],
            [in_any],
            name="pause",
            cost=60,
            aliases={0: 0},
        )[0]


def assemble(places, parts, whole):
    rows = whole.shape[0] // len(parts)
    for k, part in enumerate(parts):
        whole[pl.ds(pl.multiple_of(places[k] * rows, 16), rows)] = part[:rows]


def sums_pass(order, places, folds=(), adds=(), pays=(), waits=(), extra=0):
    args, outs, steps = [], [], []

    def give(*arrays):
        args.extend(arrays)
        return list(range(len(args) - len(arrays), len(args)))

    def make(dims, dtype):
        outs.append(shape_of(dims, dtype))
        return len(outs) - 1

    for near, received, widths in folds:
        made = []
        for width in widths:
            rows = near.shape[1] if len(near.shape) == 3 else (near.shape[0] + 16) // 2
            made += [make((rows + add, width), near.dtype) for add in (0, extra)]
        steps.append(("fold", give(near, received), made))
    for left, right in adds:
        steps.append(("add", give(left, right), [make(left.shape, left.dtype)]))
    for mine, received, older, crossed in pays:
        given = give(mine, received, older, crossed)
        steps.append(("pay", given, [make(mine.shape, mine.dtype) for _ in range(2)]))
    count = len(args)

    def kernel(places_ref, *refs):
        ins, results = refs[:count], refs[count:]
        inner = jnp.logical_and(places_ref[4] > 0, places_ref[4] < 3)
        for kind, given, made in steps:
            if kind == "fold" and len(ins[given[0]].shape) == 3:
                first = 0
                for k in range(0, len(made), 2):
                    width = results[made[k]].shape[1]
                    part = slice(first, first + width)
                    for slot in range(2):
                        total = ins[given[0]][slot, :, part].astype(f32)
                        total += ins[given[1]][slot, :, part].astype(f32)
                        results[made[k + slot]][: total.shape[0]] = total.astype(bf16)
                    if extra:
                        results[made[k + 1]][total.shape[0] :] = jnp.zeros((extra, width), bf16)
                    first += width
            elif kind == "fold":
                total = (ins[given[0]][...].astype(f32) + ins[given[1]][...].astype(f32)).astype(bf16)
                rows = results[made[0]].shape[0] - 16
                for slot in range(2):
                    results[made[slot]][:rows] = total[slot * rows : (slot + 1) * rows]
                    results[made[slot]][rows:] = total[2 * rows :]
            elif kind == "add":
                rows = ins[given[0]].shape[0]
                total = ins[given[0]][...].astype(f32) + ins[given[1]][:rows].astype(f32)
                results[made[0]][...] = total.astype(results[made[0]].dtype)
            else:
                rows = ins[given[0]].shape[0]
                fresh = ins[given[0]][...].astype(f32) + ins[given[1]][:rows].astype(f32)
                older = ins[given[2]][...].astype(f32) + ins[given[3]][...].astype(f32)
                results[made[0]][...] = fresh.astype(results[made[0]].dtype)
                results[made[1]][...] = jnp.where(inner, older, fresh).astype(results[made[1]].dtype)

    found = order.call(
        kernel,
        [places, *args],
        [in_smem] + [in_vmem] * len(args),
        outs,
        [in_vmem] * len(outs),
        limit=12,
        name="sums",
        waits=waits,
    )
    found = list(found)
    return found[0] if len(found) == 1 else found


def first_cast_kernel(sizes, qkv, short, out, rows):
    rows[...] = jnp.zeros_like(rows)
    offset = 0
    for line, size in enumerate(sizes):
        rows[line : line + 1, :size] = short[:, offset : offset + size]
        offset += size
    height = qkv.shape[0]
    out[height:] = rows[...].astype(bf16)
    out[:height] = qkv[...].astype(bf16)


def first_cast_pass(order, qkv, members):
    return order.call(
        functools.partial(first_cast_kernel, [member.size for member in members]),
        [qkv, jnp.concatenate(members)[None]],
        [in_vmem] * 2,
        [shape_of((qkv.shape[0] + 16, 3 * D), bf16)],
        [in_vmem],
        scratch=[pltpu.VMEM((16, 3 * D), f32)],
        limit=16,
        name="first_cast",
    )[0]


def cast_kernel(
    places,
    lengths,
    left,
    right,
    down,
    wide_out,
    down_out,
    lead_out,
    half_out,
    row_out,
    column_out,
):
    wide_out[:, :D] = left[...].astype(bf16)
    wide_out[:, D:] = right[...].astype(bf16)
    down_out[...] = down[...].astype(bf16)
    lead_out[...] = wide_out[:, : lead_out.shape[1]]
    rows = left.shape[0]
    turn = places[4] % 2
    first = turn * 2 * rows
    for run in range(2):
        start = pl.multiple_of(first + run * rows, 16)
        half_out[:rows, run * D : (run + 1) * D] = down_out[pl.ds(start, rows)]
    start = pl.multiple_of(turn * (rows // 2), 16)
    line = rows
    for column, width in RUNS:
        count = 2 * D // width
        height = rows // 2 // count
        for run in range(count):
            part = pl.ds(pl.multiple_of(start + run * height, 16), height)
            block = wide_out[part, D + column : D + column + width]
            half_out[line : line + height, run * width : (run + 1) * width] = block
        line += height
    pack = places[0] * 4 + places[4]
    row_places = lax.broadcasted_iota(jnp.int32, (1, SEQ), 1)
    column_places = lax.broadcasted_iota(jnp.int32, (SEQ, 1), 0)
    page_row, page_column = jnp.zeros_like(row_places), jnp.zeros_like(column_places)
    end = jnp.int32(0)
    for page in range(lengths.shape[1]):
        end += lengths[pack, page]
        page_row += (row_places >= end).astype(jnp.int32)
        page_column += (column_places >= end).astype(jnp.int32)
    row_out[...] = page_row
    column_out[...] = page_column


def cast_pass(order, places, lengths, left, right, down):
    rows = left.shape[0]
    return order.call(
        cast_kernel,
        [places, lengths, left, right, down],
        [in_smem] * 2 + [in_vmem] * 3,
        [
            shape_of((rows, D + FF), bf16),
            shape_of(down.shape, bf16),
            shape_of((rows, D + LEAD), bf16),
            shape_of((rows + sum(rows * width // (4 * D) for _, width in RUNS), 2 * D), bf16),
            shape_of((1, SEQ), jnp.int32),
            shape_of((SEQ, 1), jnp.int32),
        ],
        [in_vmem] * 6,
        limit=16,
        name="cast",
    )


def pairs_kernel(count, packed, places, rows, *rest):
    given, rest = ((), rest) if packed else (rest[:2], rest[2:])
    parts, rest = rest[:count], rest[count:]
    pair_outs, rest = rest[:GROUPS], rest[GROUPS:]
    normed_out, vectors_out, hidden_out, weight, wide_pair, last_pair, sems = rest
    pairs = [wide_pair.at[k] for k in range(GROUPS - 1)] + [last_pair]
    shard = D // count
    if packed:
        vectors = jnp.zeros((8, D), f32)
        line = lax.broadcasted_iota(jnp.int32, (8, D), 0)
        for k in range(count):
            block = parts[k][shard : shard + 16, :D].astype(f32)[:8]
            vectors += pltpu.roll(jnp.where(line < 7, block, 0.0), places[k] * shard, 1)
            start = pl.multiple_of(places[k] * D, 128)
            hidden_out[:, pl.ds(start, D)] = block[7:8]
    else:
        vectors = given[0][...]
        hidden_out[...] = given[1][...]
    vectors_out[...] = vectors
    for k, part in enumerate(parts):
        weight[pl.ds(pl.multiple_of(places[k] * shard, 16), shard)] = part[:shard, D:]
    scaled, _ = normalise(rows[...].astype(f32))
    normed_out[...] = (scaled * vectors[0:1] + vectors[1:2]).astype(bf16)
    for kind in range(2):
        line = vectors[6:7, kind * PART : (kind + 1) * PART]
        last_pair[kind, SEQ:] = jnp.concatenate([line] * 16, axis=0).astype(bf16)
    copies = []
    for group in range(GROUPS):
        for kind in range(2):
            first = kind * D + group * PART
            block = dot(normed_out[...], weight[:, first : first + PART])
            pairs[group][kind, :SEQ] = block.astype(bf16)
        copies.append(pltpu.make_async_copy(pairs[group], pair_outs[group], sems.at[group]))
        copies[-1].start()
    for copy in copies:
        copy.wait()


def pairs_pass(order, places, rows, parts, given=(), waits=()):
    count = len(parts)
    outs = order.call(
        functools.partial(pairs_kernel, count, not given),
        [places, rows, *given, *parts],
        [in_smem] + [in_vmem] * (1 + len(given) + count),
        [shape_of((2, SEQ, PART), bf16)] * (GROUPS - 1)
        + [
            shape_of((2, SEQ + 16, PART), bf16),
            shape_of((SEQ, D), bf16),
            shape_of((8, D), f32),
            shape_of((1, FF), f32),
        ],
        [in_hbm] * GROUPS + [in_vmem] * 3,
        scratch=[
            pltpu.VMEM((D, 2 * D), bf16),
            pltpu.VMEM((GROUPS - 1, 2, SEQ, PART), bf16),
            pltpu.VMEM((2, SEQ + 16, PART), bf16),
            pltpu.SemaphoreType.DMA((GROUPS,)),
        ],
        limit=16,
        name="pairs",
        waits=waits,
    )
    return outs[:GROUPS], *outs[GROUPS:]


def queries_kernel(places, normed, *rest):
    parts, (out, weight) = rest[:-2], rest[-2:]
    shard = D // len(parts)
    for k, part in enumerate(parts):
        weight[pl.ds(pl.multiple_of(places[k] * shard, 16), shard)] = part[:shard, :D]
    for first in range(0, D, PART):
        block = dot(normed[...], weight[:, first : first + PART])
        out[:, first : first + PART] = block.astype(bf16)


def queries_pass(order, places, normed, parts):
    return order.call(
        queries_kernel,
        [places, normed, *parts],
        [in_smem] + [in_vmem] * (1 + len(parts)),
        [shape_of((SEQ, D), bf16)],
        [in_vmem],
        scratch=[pltpu.VMEM((D, D), bf16)],
        limit=16,
        name="queries",
    )[0]


def fill_page_bias(page_row, page_column, bias):
    for index, (low, high) in enumerate(WINDOWS):
        start = index * BLOCK
        same = page_column[low:high] == page_row[:, start : start + BLOCK]
        bias[index, : high - low] = jnp.where(same, 0.0, masked_score)


def two_heads(block):
    lane = lax.broadcasted_iota(jnp.int32, block.shape, 1)
    zero = jnp.zeros_like(block)
    return jnp.concatenate(
        [jnp.where(lane < HEAD_DIM, block, zero), jnp.where(lane < HEAD_DIM, zero, block)], axis=0
    )


def head_rows(both):
    return jnp.concatenate([both[:HEAD_DIM, :BLOCK], both[HEAD_DIM:, BLOCK:]], axis=0).T


def page_bias(bias, index, size):
    block = bias[index, :size]
    return jnp.concatenate([block, block], axis=1)


def attend_kernel(
    query_first, query, own, other, page_row, page_column, context, log_total, bias
):
    fill_page_bias(page_row, page_column, bias)

    def exponents_of(step, index):
        low, high = WINDOWS[index]
        rows, lanes = slice(index * BLOCK, (index + 1) * BLOCK), slice(step * PAIR, (step + 1) * PAIR)
        query_lanes = slice((query_first + step) * PAIR, (query_first + step + 1) * PAIR)
        queries = two_heads(query[rows, query_lanes] * score_scale)
        allowed = page_bias(bias, index, high - low)
        scores = [dot_nt(side[0, low:high, lanes], queries) + allowed for side in (own, other)]
        largest = jnp.max(jnp.maximum(*scores), axis=0, keepdims=True)
        exponents = [jnp.exp(score - largest) for score in scores]
        total = column_sums(exponents[0] + exponents[1])
        log_total[step, index : index + 1] = largest + jnp.log(total)
        return exponents, 1.0 / total

    def context_of(step, index, found):
        exponents, inverse = found
        low, high = WINDOWS[index]
        rows, lanes = slice(index * BLOCK, (index + 1) * BLOCK), slice(step * PAIR, (step + 1) * PAIR)
        both = 0.0
        for side, exponent in zip((own, other), exponents):
            both += dot_tn(side[1, low:high, lanes], (exponent * inverse).astype(bf16))
        context[rows, lanes] = head_rows(both).astype(bf16)

    steps = [(k, w) for k in range(context.shape[1] // PAIR) for w in range(len(WINDOWS))]
    found = exponents_of(*steps[0])
    for place, now in enumerate(steps):
        ahead = exponents_of(*steps[place + 1]) if place + 1 < len(steps) else None
        context_of(*now, found)
        found = ahead


def attend(order, query_first, queries, own, other, page_row, page_column, waits=()):
    width = own.shape[2]
    return order.call(
        functools.partial(attend_kernel, query_first),
        [queries, own, other, page_row, page_column],
        [in_vmem] * 5,
        [
            shape_of((SEQ, width), bf16),
            shape_of((width // PAIR, len(WINDOWS), 2 * BLOCK), f32),
        ],
        [in_vmem] * 2,
        scratch=[pltpu.VMEM((len(WINDOWS), WINDOW, BLOCK), f32)],
        limit=12,
        name="attend",
        cost=60,
        waits=waits,
    )


def attend_back_kernel(
    query_first,
    query,
    own,
    other,
    context_grad,
    log_total,
    page_row,
    page_column,
    *rest,
):
    *given, query_grad, own_grad, other_grad, bias, other_sum = rest
    fill_page_bias(page_row, page_column, bias)
    own_grad[...] = jnp.zeros_like(own_grad)
    other_sum[...] = jnp.zeros_like(other_sum)

    def shares_of(step, index):
        low, high = WINDOWS[index]
        rows, lanes = slice(index * BLOCK, (index + 1) * BLOCK), slice(step * PAIR, (step + 1) * PAIR)
        query_lanes = slice((query_first + step) * PAIR, (query_first + step + 1) * PAIR)
        queries = two_heads(query[rows, query_lanes] * score_scale)
        grads = two_heads(context_grad[rows, query_lanes])
        offset = page_bias(bias, index, high - low) - log_total[step, index : index + 1]
        halves = []
        for side in (own, other):
            shares = jnp.exp(dot_nt(side[0, low:high, lanes], queries) + offset)
            halves.append((shares, dot_nt(side[1, low:high, lanes], grads)))
        centre = sum(column_sums(shares * share_grad) for shares, share_grad in halves)
        return queries, grads, halves, centre

    def grads_of(step, index, found):
        queries, grads, halves, centre = found
        low, high = WINDOWS[index]
        rows, lanes = slice(index * BLOCK, (index + 1) * BLOCK), slice(step * PAIR, (step + 1) * PAIR)
        both = 0.0
        for side, total, (shares, share_grad) in zip((own, other), (own_grad, other_sum), halves):
            score_grad = (shares * (share_grad - centre)).astype(bf16)
            total[1, low:high, lanes] += dot(shares.astype(bf16), grads)
            total[0, low:high, lanes] += dot(score_grad, queries)
            both += dot_tn(side[0, low:high, lanes], score_grad)
        query_grad[rows, lanes] = (head_rows(both) * score_scale).astype(bf16)

    steps = [(k, w) for k in range(own_grad.shape[2] // PAIR) for w in range(len(WINDOWS))]
    found = shares_of(*steps[0])
    for place, now in enumerate(steps):
        ahead = shares_of(*steps[place + 1]) if place + 1 < len(steps) else None
        grads_of(*now, found)
        found = ahead
    other_grad[:, :SEQ] = other_sum[...].astype(bf16)
    if given:
        for kind in range(2):
            line = given[0][:, kind * PART : (kind + 1) * PART]
            other_grad[kind, SEQ:] = jnp.concatenate([line] * 2, axis=0).astype(bf16)


def attend_back(
    order, query_first, queries, own, other, context_grad, logs, page_row, page_column, given
):
    return order.call(
        functools.partial(attend_back_kernel, query_first),
        [queries, own, other, context_grad, logs, page_row, page_column, *given],
        [in_vmem] * (7 + len(given)),
        [
            shape_of((SEQ, PART), bf16),
            shape_of((2, SEQ, PART), f32),
            shape_of((2, SEQ + 16 * len(given), PART), bf16),
        ],
        [in_vmem] * 3,
        scratch=[
            pltpu.VMEM((len(WINDOWS), WINDOW, BLOCK), f32),
            pltpu.VMEM((2, SEQ, PART), f32),
        ],
        limit=16,
        name="attend_back",
        cost=60,
    )


def partner_cross(pair):
    rows = pair[:, SEQ:].astype(f32)
    return jnp.concatenate([rows[0, :1], rows[1, :1]], axis=1)


def join_blocks(places, wides, downs, leads, halves, wide, down):
    rows = wide.shape[0] // (len(wides) + len(leads))
    for k, part in enumerate(wides):
        wide[pl.ds(pl.multiple_of(places[k] * rows, 16), rows)] = part[...]
        down[k] = downs[k][...]
    turn = places[4] % 2
    for k, part in enumerate(leads):
        first = places[len(wides) + k] * rows
        wide[pl.ds(pl.multiple_of(first, 16), rows), : part.shape[1]] = part[...]
        for side, half in enumerate(halves[k]):
            place = turn if side == 0 else 1 - turn
            line = rows
            for column, width in RUNS:
                runs = 2 * D // width
                height = rows // 2 // runs
                for run in range(runs):
                    start = pl.multiple_of(first + place * (rows // 2) + run * height, 16)
                    block = half[line : line + height, run * width : (run + 1) * width]
                    wide[pl.ds(start, height), D + column : D + column + width] = block
                line += height
            for run in range(2):
                start = pl.multiple_of((2 * place + run) * rows, 16)
                down[len(wides) + k, pl.ds(start, rows)] = half[:rows, run * D : (run + 1) * D]


def middle_kernel(kinds, places, rows, *rest):
    contexts, rest = rest[:GROUPS], rest[GROUPS:]
    (tangent, vectors, partner, hidden_bias), rest = rest[:4], rest[4:]
    wides, downs, leads = [], [], []
    for group, size in zip((wides, downs, leads), kinds):
        group += rest[:size]
        rest = rest[size:]
    halves = [rest[2 * k : 2 * k + 2] for k in range(kinds[2])]
    rest = rest[2 * kinds[2] :]
    middle_out, second_out, hidden_out, slope_out, modal_out, inner_out, wide, down, total = rest
    join_blocks(places, wides, downs, leads, halves, wide, down)
    count = down.shape[0]
    middle = rows[...].astype(f32)
    for group, context in enumerate(contexts):
        middle += dot(context[...], wide[group * PART : (group + 1) * PART, :D])
    middle_out[...] = middle
    scaled, _ = normalise(middle)
    second_out[...] = (scaled * vectors[2:3] + vectors[3:4]).astype(bf16)
    total[...] = middle + vectors[4:5]
    slot = FF // count
    size = 768
    def upper_of(k, first):
        start = places[k] * slot + first
        part = pl.ds(pl.multiple_of(start, 128), size)
        column = pl.ds(pl.multiple_of(D + start, 128), size)
        return part, dot(second_out[...], wide[:, column]) + hidden_bias[:, part]

    steps = [(k, first) for k in range(count) for first in range(0, slot, size)]
    found = upper_of(*steps[0])
    for place, (k, first) in enumerate(steps):
        ahead = upper_of(*steps[place + 1]) if place + 1 < len(steps) else None
        part, upper = found
        square = upper * upper
        angle = jnp.tanh(upper * (gelu_scale + (gelu_cubic * gelu_scale) * square))
        half = 0.5 + 0.5 * angle
        hidden = (upper * half).astype(bf16)
        hidden_out[:, part] = hidden
        bend = 2.0 * gelu_scale + (6.0 * gelu_cubic * gelu_scale) * square
        slope_out[:, part] = (half + half * (1.0 - half) * (upper * bend)).astype(bf16)
        total[...] += dot(hidden, down[k, first : first + size])
        found = ahead
    modal_out[...] = total[...].astype(bf16)
    modal = modal_out[...].astype(f32)
    own = jnp.sum(modal * vectors[5:6], axis=1, keepdims=True)
    cross = jnp.sum(modal * partner_cross(partner), axis=1, keepdims=True)
    met = jnp.sum(modal * tangent[...].astype(f32), axis=1, keepdims=True)
    lane = lax.broadcasted_iota(jnp.int32, (SEQ, 128), 1)
    columns = jnp.where(lane == 0, own, jnp.where(lane == 1, cross, met))
    inner_out[...] = columns.T[:8]


def middle_pass(
    order, places, rows, contexts, tangent, vectors, partner, hidden_bias, wides, downs, leads, halves
):
    count = len(wides) + len(leads)
    parts = [*wides, *downs, *leads] + [piece for pair in halves for piece in pair]
    return order.call(
        functools.partial(middle_kernel, (len(wides), len(downs), len(leads))),
        [places, rows, *contexts, tangent, vectors, partner, hidden_bias, *parts],
        [in_smem] + [in_vmem] * (5 + GROUPS + len(parts)),
        [
            shape_of((SEQ, D), f32),
            shape_of((SEQ, D), bf16),
            shape_of((SEQ, FF), bf16),
            shape_of((SEQ, FF), bf16),
            shape_of((SEQ, D), bf16),
            shape_of((8, SEQ), f32),
            shape_of((D, D + FF), bf16),
            shape_of((count, FF // count, D), bf16),
        ],
        [in_vmem] * 8,
        scratch=[pltpu.VMEM((SEQ, D), f32)],
        limit=16,
        name="middle",
    )


def gate_kernel(
    own,
    other,
    tangent,
    partner_tangent,
    vectors,
    partner,
    grad_out,
    low_out,
    columns_out,
    sums,
):
    gate = jax.nn.sigmoid(own[0:1] + other[1:2])
    gate_two = jax.nn.sigmoid(other[0:1] + own[1:2])
    logit = other[2:3] * gate * (1.0 - gate)
    logit_two = own[2:3] * gate_two * (1.0 - gate_two)
    padding = jnp.zeros((124, SEQ), f32)
    columns = jnp.concatenate([gate, logit, gate_two, logit_two, padding], axis=0).T
    columns_out[...] = columns
    grad = (
        tangent[...].astype(f32)
        + columns[:, 1:2] * vectors[5:6]
        + partner_tangent[...].astype(f32) * columns[:, 2:3]
        + columns[:, 3:4] * partner_cross(partner)
    )
    grad_out[...] = grad
    low_out[...] = grad.astype(bf16)
    sums[...] = column_sums(grad)


def gate_pass(order, own, other, tangent, partner_tangent, vectors, partner):
    return order.call(
        gate_kernel,
        [own, other, tangent, partner_tangent, vectors, partner],
        [in_vmem] * 6,
        [
            shape_of((SEQ, D), f32),
            shape_of((SEQ, D), bf16),
            shape_of((SEQ, 128), f32),
            shape_of((1, D), f32),
        ],
        [in_vmem] * 4,
        name="gate",
    )


def mix_kernel(own, other, columns, mixed):
    mixed[...] = (
        own[...].astype(f32) + columns[:, 0:1] * other[...].astype(f32)
    ).astype(bf16)


def mix_pass(order, own, other, columns, waits=()):
    return order.call(
        mix_kernel,
        [own, other, columns],
        [in_vmem] * 3,
        [shape_of((SEQ, D), bf16)],
        [in_vmem],
        name="mix",
        cost=60,
        waits=waits,
    )[0]


def gate_sums_kernel(own, columns, out):
    rows = own[...].astype(f32)
    out[...] = jnp.zeros_like(out)
    out[0:1] = column_sums(columns[:, 1:2] * rows)
    out[1:2] = column_sums(columns[:, 3:4] * rows)


def gate_sums_pass(order, own, columns):
    return order.call(
        gate_sums_kernel, [own, columns], [in_vmem] * 2, [shape_of((8, D), f32)], [in_vmem], name="gate_sums"
    )[0]


def chain_kernel(places, low, grad, slope, middle, vectors, wide, down, *rest):
    total_out, total_low_out, context_out, upper_out, upper_sums, gain_sums, bias_sums = rest[:7]
    normed_grad = rest[7]
    normed_grad[...] = jnp.zeros_like(normed_grad)
    count = down.shape[0]
    slot = FF // count
    size = 768
    def upper_of(k, first):
        start = places[k] * slot + first
        part = pl.ds(pl.multiple_of(start, 128), size)
        column = pl.ds(pl.multiple_of(D + start, 128), size)
        return part, column, dot_nt(low[...], down[k, first : first + size])

    steps = [(k, first) for k in range(count) for first in range(0, slot, size)]
    found = upper_of(*steps[0])
    for place in range(len(steps)):
        ahead = upper_of(*steps[place + 1]) if place + 1 < len(steps) else None
        part, column, upper = found
        upper = upper * slope[:, part].astype(f32)
        upper_sums[:, part] = column_sums(upper)
        upper_low = upper.astype(bf16)
        upper_out[:, part] = upper_low
        normed_grad[...] += dot_nt(upper_low, wide[:, column])
        found = ahead
    scaled, root = normalise(middle[...])
    incoming = normed_grad[...]
    gain_sums[...] = column_sums(incoming * scaled)
    bias_sums[...] = column_sums(incoming)
    total = grad[...] + norm_back(scaled, root, vectors[2:3], incoming)
    total_out[...] = total
    total_low_out[...] = total.astype(bf16)
    context_out[...] = dot_nt(total_low_out[...], wide[:, :D]).astype(bf16)


def chain_pass(order, places, low, grad, slope, middle, vectors, wide, down):
    return order.call(
        chain_kernel,
        [places, low, grad, slope, middle, vectors, wide, down],
        [in_smem] + [in_vmem] * 7,
        [
            shape_of((SEQ, D), f32),
            shape_of((SEQ, D), bf16),
            shape_of((SEQ, D), bf16),
            shape_of((SEQ, FF), bf16),
            shape_of((1, FF), f32),
            shape_of((1, D), f32),
            shape_of((1, D), f32),
        ],
        [in_vmem] * 7,
        scratch=[pltpu.VMEM((SEQ, D), f32)],
        limit=20,
        name="chain",
    )


def slots_of(count):
    return (list(range(0, count, 2)), list(range(1, count, 2)))


def block_shapes(widths, count):
    near, far = slots_of(count)
    rows = D // count
    outs = []
    for width in widths:
        outs.append(shape_of((len(near), rows, width), bf16))
        if far:
            outs.append(shape_of((len(far), rows, width), bf16))
    return outs


def store_blocks(places, count, products, widths, outs, whole):
    near, far = slots_of(count)
    rows = D // count
    products = list(products)
    each = 2 if far else 1
    for index, width in enumerate(widths):
        low = 0
        while low < width:
            left, right = products.pop(0)
            whole[:, low : low + right.shape[1]] = dot(left, right).astype(bf16)
            low += right.shape[1]
        for out, slots in zip(outs[each * index : each * index + each], (near, far)):
            for place, slot in enumerate(slots):
                begin = pl.multiple_of(places[slot] * rows, 16)
                out[place] = whole[pl.ds(begin, rows), :width]


def up_grads_kernel(count, widths, places, second, upper, *rest):
    turned = second[...].T
    products = [(turned, upper[:, k : k + 512]) for k in range(0, FF, 512)]
    store_blocks(places, count, products, widths, rest[:-1], rest[-1])


def up_grads(order, places, second, upper, widths, count):
    outs = block_shapes(widths, count)
    return order.call(
        functools.partial(up_grads_kernel, count, widths),
        [places, second, upper],
        [in_smem] + [in_vmem] * 2,
        outs,
        [in_vmem] * len(outs),
        scratch=[pltpu.VMEM((D, max(widths)), bf16)],
        limit=16,
        name="up_grads",
    )


def lead_grads_kernel(count, places, context, context_two, low, normed, *rest):
    queries, (own, returned), rest = rest[:GROUPS], rest[GROUPS : GROUPS + 2], rest[GROUPS + 2 :]
    pair_low, outs, whole = rest[0], rest[1:-1], rest[-1]
    pair_low[...] = (own[...] + returned[:, :SEQ].astype(f32)).astype(bf16)
    turned = jnp.concatenate([context[...].T, context_two[...].T], axis=0)
    products = [(turned, low[:, k : k + PART]) for k in range(0, D, PART)]
    turned = normed[...].T
    products += [(turned, query[...]) for query in queries]
    products += [(turned, pair_low[kind]) for kind in range(2)]
    store_blocks(places, count, products, [3 * D], outs, whole)


def lead_grads(order, places, contexts, low, normed, queries, own, returned, count):
    outs = block_shapes([3 * D], count)
    args = [*contexts, low, normed, *queries, own, returned]
    return order.call(
        functools.partial(lead_grads_kernel, count),
        [places, *args],
        [in_smem] + [in_vmem] * len(args),
        [shape_of(own.shape, bf16)] + outs,
        [in_vmem] * (1 + len(outs)),
        scratch=[pltpu.VMEM((D, 3 * D), bf16)],
        limit=16,
        name="lead_grads",
    )


def down_grads_kernel(count, first, height, fold, places, low, hidden, *outs):
    near, far = slots_of(count)
    width = FF // count
    turned = low[:, first : first + height].T
    rows = height // fold
    for out, slots in zip(outs, (near, far)):
        for place, slot in enumerate(slots):
            begin = pl.multiple_of(places[slot] * width, 128)
            block = dot(turned, hidden[:, pl.ds(begin, width)]).astype(bf16)
            for k in range(fold):
                out[place, :, k * width : (k + 1) * width] = block[k * rows : (k + 1) * rows]


def down_grads(order, places, low, hidden, first, height, fold, count):
    near, far = slots_of(count)
    width = FF // count
    outs = [shape_of((len(near), height // fold, fold * width), bf16)]
    if far:
        outs.append(shape_of((len(far), height // fold, fold * width), bf16))
    return order.call(
        functools.partial(down_grads_kernel, count, first, height, fold),
        [places, low, hidden],
        [in_smem, in_vmem, in_vmem],
        outs,
        [in_vmem] * len(outs),
        limit=16,
        name="down_grads",
    )


def first_kernel(count, places, total, rows, vectors, normed, own, returned, *rest):
    parts, rest = rest[:count], rest[count:]
    queries, pair, rest = rest[:GROUPS], rest[GROUPS], rest[GROUPS + 1 :]
    gain_two, bias_two, output_bias, gate_own, hidden_bias = rest[:5]
    grad_out, outs = rest[5], rest[6:-5]
    pair_low, normed_grad, weight, whole, short = rest[-5:]
    pair_low[...] = (own[...] + returned[:, :SEQ].astype(f32)).astype(bf16)
    assemble(places, parts, weight)
    for group, pairs in enumerate((pair, pair_low)):
        start = group * PART
        block = dot_nt(queries[group][...], weight[:, start : start + PART])
        for kind in range(2):
            start = (kind + 1) * D + group * PART
            block += dot_nt(pairs[kind], weight[:, start : start + PART])
        if group == 0:
            normed_grad[...] = block
        else:
            normed_grad[...] += block
    scaled, root = normalise(rows[...].astype(f32))
    incoming = normed_grad[...]
    short[...] = jnp.zeros_like(short)
    short[0:1] = column_sums(incoming * scaled)
    short[1:2] = column_sums(incoming)
    for line, member in enumerate((gain_two, bias_two, output_bias)):
        short[line + 2 : line + 3] = member[...]
    short[5:6] = gate_own[0:1]
    for kind in range(2):
        line = returned[kind, SEQ : SEQ + 8].astype(f32)
        short[6:7, kind * PART : (kind + 1) * PART] = line[1:2]
    for line in range(FF // D):
        short[line + 8 : line + 9] = hidden_bias[:, line * D : (line + 1) * D]
    grad_out[...] = total[...] + norm_back(scaled, root, vectors[0:1], incoming)
    turned = normed[...].T
    for kind in range(2):
        whole[:, kind * PART : (kind + 1) * PART] = dot(turned, pair_low[kind]).astype(bf16)
    height = D // count
    for out, slots in zip(outs, slots_of(count)):
        for place, slot in enumerate(slots):
            begin = pl.multiple_of(places[slot] * height, 16)
            out[place * height : (place + 1) * height] = whole[pl.ds(begin, height)]
        out[len(slots) * height :] = short[...].astype(bf16)


def first_pass(
    order, places, total, rows, vectors, normed, own, returned, parts, queries, pair, short
):
    count = len(parts)
    args = [total, rows, vectors, normed, own, returned, *parts, *queries, pair, *short]
    outs = [
        shape_of((len(slots) * (D // count) + 16, 2 * PART), bf16) for slots in slots_of(count) if slots
    ]
    return order.call(
        functools.partial(first_kernel, count),
        [places, *args],
        [in_smem] + [in_vmem] * len(args),
        [shape_of((SEQ, D), f32)] + outs,
        [in_vmem] * (1 + len(outs)),
        scratch=[
            pltpu.VMEM((2, SEQ, PART), bf16),
            pltpu.VMEM((SEQ, D), f32),
            pltpu.VMEM((D, 3 * D), bf16),
            pltpu.VMEM((D, 2 * PART), bf16),
            pltpu.VMEM((16, D), f32),
        ],
        limit=20,
        name="first",
    )


def settle_kernel(kind, count, outs, places, *refs):
    totals, returned, refs = refs[:count], refs[count : 2 * count], refs[2 * count :]
    targets, (scratch, sems) = refs[:outs], (refs[outs : 2 * outs], refs[2 * outs])
    copies = []

    def leave(index, *where):
        source, target = scratch[index].at[where], targets[index].at[where]
        copies.append(pltpu.make_async_copy(source, target, sems.at[len(copies)]))
        copies[-1].start()

    inner = jnp.logical_and(places[4] > 0, places[4] < 3)
    values = [jnp.where(inner, a[...], b[...]).astype(f32) for a, b in zip(totals, returned)]
    out, every = scratch[0], slice(None)
    if kind == "turn":
        first = 0
        for value in values:
            rows = value.shape[0]
            start = first
            for k in range(0, value.shape[1], D):
                out[:, first : first + rows] = value[:, k : k + D].T
                first += rows
            leave(0, every, pl.ds(start, first - start))
    elif kind == "columns":
        first = 0
        for value in values:
            out[:, first : first + value.shape[1]] = value
            leave(0, every, pl.ds(first, value.shape[1]))
            first += value.shape[1]
    else:
        scratch[1][...] = values[0][:, :D]
        leave(1, every)
        out[:, :D] = values[0][:, D:]
        for group, value in enumerate(values[1:]):
            for part in range(2):
                start = (part + 1) * D + group * PART
                out[:, start : start + PART] = value[:, part * PART : (part + 1) * PART]
        leave(0, every)
    for copy in copies:
        copy.wait()


def settle(order, kind, places, blocks, dims):
    count = len(blocks)
    found = order.call(
        functools.partial(settle_kernel, kind, count, len(dims)),
        [places] + [block[0] for block in blocks] + [block[1] for block in blocks],
        [in_smem] + [in_vmem] * (2 * count),
        [shape_of(each, f32) for each in dims],
        [in_hbm] * len(dims),
        scratch=[pltpu.VMEM(each, f32) for each in dims] + [pltpu.SemaphoreType.DMA((8,))],
        name="settle",
    )
    return found[0] if len(dims) == 1 else found


def last_settle_kernel(places, total, returned, given, out, *rest):
    short_outs, (scratch, sems) = rest[:8], rest[8:]
    inner = jnp.logical_and(places[4] > 0, places[4] < 3)
    value = jnp.where(inner, total[...], returned[...]).astype(f32)
    rows = scratch.shape[1]
    copies = []
    for part in range(2):
        scratch[part] = value[:rows, part * PART : (part + 1) * PART]
        place = out.at[:, pl.ds((part + 1) * D + PART, PART)]
        copies.append(pltpu.make_async_copy(scratch.at[part], place, sems.at[part]))
        copies[-1].start()
    short = value[rows:]
    turned = pltpu.roll(short, D - places[0] * rows, 1)
    for line in range(7):
        short_outs[line][...] = turned[line : line + 1, :rows].reshape(rows)
    line = lax.broadcasted_iota(jnp.int32, short.shape, 0)
    hidden = jnp.sum(jnp.where(line == 8 + places[0], short, 0.0), axis=0)
    short_outs[7][...] = hidden
    for copy in copies:
        copy.wait()


def last_settle(order, places, block, given):
    rows = given.shape[0]
    shorts = [shape_of((rows,), f32)] * 7 + [shape_of((D,), f32)]
    found = order.call(
        last_settle_kernel,
        [places, block[0], block[1], given],
        [in_smem, in_vmem, in_vmem, in_hbm],
        [shape_of(given.shape, f32)] + shorts,
        [in_hbm] + [in_vmem] * 8,
        scratch=[pltpu.VMEM((2, rows, PART), f32), pltpu.SemaphoreType.DMA((2,))],
        name="last_settle",
        aliases={3: 0},
    )
    return found[0], found[1:]


def swap_bit(value, axis, bit):
    size = lax.axis_size(axis)
    return lax.ppermute(value, axis, [(source, source ^ (1 << bit)) for source in range(size)])


def from_partner(value):
    size = lax.axis_size("stream")
    half = size // 2
    return lax.ppermute(value, "stream", [(source, (source + half) % size) for source in range(size)])


def along(value, pairs):
    return lax.ppermute(value, "dp", pairs)


def up_line(value, steps):
    return along(value, [(floor, floor + 1) for floor in range(steps - 1, 3)])


def down_line(value, steps):
    return along(value, [(floor, floor - 1) for floor in range(1, 5 - steps)])


def swap_outer(value):
    return along(value, [(0, 1), (1, 0), (2, 3), (3, 2)])


def to_inner(value):
    return along(value, [(0, 1), (3, 2)])


def over_middle(value):
    return along(value, [(1, 2), (2, 1)])


def to_outer(value):
    return along(value, [(1, 0), (2, 3)])


def core(value):
    return swap_bit(value, "stream", 0)


def across(value):
    return swap_bit(value, "stream", 1)


def modality_groups():
    size = lax.axis_size("stream")
    half = size // 2
    return [list(range(half)), list(range(half, size))]


def body(
    regions,
    cotangent,
    page_lens,
    qkv_weight,
    out_weight,
    up_weight,
    down_weight,
    ln1_gain,
    ln1_bias,
    ln2_gain,
    ln2_bias,
    up_bias,
    down_bias,
    gate_own,
    gate_other,
):
    half = lax.axis_size("stream") // 2
    depth = lax.axis_size("dp")
    paired = half == 4 and depth == 4
    side = lax.axis_index("stream") % half
    floor = lax.axis_index("dp")
    count = 4 if paired else 1
    slots = jnp.arange(4, dtype=jnp.int32)
    picks = jnp.bitwise_xor(side.astype(jnp.int32), slots) if paired else jnp.zeros_like(slots)
    places = jnp.concatenate([picks, floor.astype(jnp.int32)[None]])
    order = Order()
    short = (ln1_gain, ln1_bias, ln2_gain, ln2_bias, down_bias, gate_own, gate_other, up_bias)
    partner_tangent = from_partner(cotangent)

    def attend_group(group, waits=()):
        context, log_total = attend(
            order,
            group * PART // PAIR,
            queries,
            own_pairs[group],
            other_pairs[group],
            page_row,
            page_column,
            waits,
        )
        contexts.append(context)
        logs.append(log_total)

    contexts, logs = [], []
    if paired:
        qkv_shard = first_cast_pass(order, qkv_weight, short)
        qkv_across, qkv_near = across(qkv_shard), core(qkv_shard)
        wide_shard, down_shard, lead, half_own, page_row, page_column = cast_pass(
            order, places, page_lens, out_weight, up_weight, down_weight
        )
        wide_near, down_near = core(wide_shard), core(down_shard)
        (qkv_across,) = order.hold([qkv_across], waits=[partner_tangent, qkv_near])
        qkv_far, half_own = core(qkv_across), across(half_own)
        qkv_parts = [qkv_shard, qkv_near, qkv_across, qkv_far]
        own_pairs, normed, vectors, hidden_bias = pairs_pass(
            order, places, regions, qkv_parts, waits=[wide_near, down_near]
        )
        queries = queries_pass(order, places, normed, qkv_parts)
        other_pairs = [from_partner(pair) for pair in own_pairs]
        lead_across = across(lead)
        (half_own,) = order.hold([half_own])
        half_other, half_own_far = swap_outer(half_own), core(half_own)
        attend_group(0)
        (lead_across,) = order.hold([lead_across])
        vectors = order.pause(vectors)
        (half_other,) = order.hold([half_other])
        half_other_far, lead_far = core(half_other), core(lead_across)
        attend_group(1)
        wides, downs = [wide_shard, wide_near], [down_shard, down_near]
        leads = [lead_across, lead_far]
        halves = [(half_own, half_other), (half_own_far, half_other_far)]
    else:
        lengths = lax.dynamic_slice_in_dim(page_lens, side * depth + floor, 1, 0)
        positions = jnp.arange(SEQ, dtype=jnp.int32)
        page_ends = jnp.cumsum(lengths[0], dtype=jnp.int32)
        pages = jnp.sum((page_ends[:, None] <= positions[None, :]).astype(jnp.int32), axis=0)
        page_row, page_column = pages[None, :], pages[:, None]

        def gather(shard):
            return [
                lax.all_gather(shard, "stream", axis_index_groups=modality_groups(), tiled=True)
            ]

        packed = jnp.concatenate([member.astype(bf16) for member in short])[None]
        found = gather(packed)[0].astype(f32)
        shard = D // half
        rows = [found[:, k * shard : (k + 1) * shard].reshape(1, D) for k in range(7)]
        given = (
            jnp.concatenate(rows + [jnp.zeros((1, D), f32)], axis=0),
            found[:, 7 * shard :].reshape(1, FF),
        )
        qkv_parts = gather(qkv_weight.astype(bf16))
        wides = gather(jnp.concatenate([out_weight, up_weight], axis=1).astype(bf16))
        downs, leads, halves = gather(down_weight.astype(bf16)), [], []
        own_pairs, normed, vectors, hidden_bias = pairs_pass(
            order, places, regions, qkv_parts, given
        )
        queries = queries_pass(order, places, normed, qkv_parts)
        other_pairs = [from_partner(pair) for pair in own_pairs]
        for group in range(GROUPS):
            attend_group(group)

    middle, second, hidden, slope, modal, inner_own, wide, down = middle_pass(
        order,
        places,
        regions,
        contexts,
        partner_tangent,
        vectors,
        other_pairs[-1],
        hidden_bias,
        wides,
        downs,
        leads,
        halves,
    )
    inner_other = from_partner(inner_own)
    modal_grad, modal_low, columns, output_bias_grad = gate_pass(
        order, inner_own, inner_other, cotangent, partner_tangent, vectors, other_pairs[-1]
    )

    def attend_back_group(group):
        query_grad, own_grad, other_grad = attend_back(
            order,
            group * PART // PAIR,
            queries,
            own_pairs[group],
            other_pairs[group],
            context_grad,
            logs[group],
            page_row,
            page_column,
            [gate_sums] if group == GROUPS - 1 else [],
        )
        query_grads.append(query_grad)
        own_grads.append(own_grad)
        returned.append(from_partner(other_grad))

    def last_pass(pair_low):
        short_grads = (
            gain_two_grad,
            bias_two_grad,
            output_bias_grad,
            gate_sums,
            hidden_bias_grad,
        )
        return first_pass(
            order,
            places,
            middle_grad,
            regions,
            vectors,
            normed,
            own_grads[1],
            returned[1],
            qkv_parts,
            query_grads,
            pair_low,
            short_grads,
        )

    query_grads, own_grads, returned = [], [], []
    back = (order, places, modal_low, modal_grad, slope, middle, vectors, wide, down)
    if paired:
        d1, far = down_grads(order, places, modal_low, hidden, 0, 384, 2, count)
        d1_core = core(far)
        d2, far = down_grads(order, places, modal_low, hidden, 384, 384, 2, count)
        d2_core = core(far)
        d1, away = sums_pass(order, places, folds=[(d1, d1_core, [FF // 2])])
        d1_in = across(away)
        d2, d2_away = sums_pass(order, places, folds=[(d2, d2_core, [FF // 2])])
        middle_grad, middle_low, context_grad, upper_low, *rest = chain_pass(*back)
        hidden_bias_grad, gain_two_grad, bias_two_grad = rest
        d1 = sums_pass(order, places, adds=[(d1, d1_in)])
        d1_in = to_inner(d1)
        (d2_away,) = order.hold([d2_away])
        d2_in = across(d2_away)
        gate_sums = gate_sums_pass(order, modal, columns)
        u1, far_one, u2, far_two = up_grads(
            order, places, second, upper_low, [FF // 2, FF // 2], count
        )
        u1_core, u2_core = core(far_one), core(far_two)
        attend_back_group(0)
        d2, d1 = sums_pass(order, places, adds=[(d2, d2_in), (d1, d1_in)])
        d2_in, d1_mid = to_inner(d2), over_middle(d1)
        columns = order.pause(columns)
        u1, away = sums_pass(order, places, folds=[(u1, u1_core, [FF // 2])])
        u1_in = across(away)
        u2, away = sums_pass(order, places, folds=[(u2, u2_core, [FF // 2])])
        attend_back_group(1)
        d2, u1, u1_pay = sums_pass(
            order, places, adds=[(d2, d2_in)], pays=[(u1, u1_in, d1, d1_mid)]
        )
        u1_in, d2_mid = swap_outer(u1_pay), over_middle(d2)
        (away,) = order.hold([away])
        u2_in = across(away)
        pair_low, lead_near, lead_far = lead_grads(
            order, places, contexts, middle_low, normed, query_grads, own_grads[0], returned[0], count
        )
        lead_core = core(lead_far)
        u1, u2, u2_pay = sums_pass(
            order, places, adds=[(u1, u1_in)], pays=[(u2, u2_in, d2, d2_mid)]
        )
        d1_out = u1_in
        u2_in, u1_mid = swap_outer(u2_pay), over_middle(u1)
        gate_sums = order.pause(gate_sums)
        oq, away, p1, away_two = sums_pass(
            order, places, folds=[(lead_near, lead_core, [2 * D, D])]
        )
        oq_in = across(away)
        region_grad, last_near, last_far = last_pass(pair_low)
        last_core = core(last_far)
        u2, oq, oq_pay = sums_pass(
            order, places, adds=[(u2, u2_in)], pays=[(oq, oq_in, u1, u1_mid)]
        )
        d2_out = u2_in
        oq_in, u2_mid = swap_outer(oq_pay), over_middle(u2)
        (away_two,) = order.hold([away_two])
        p1_in = across(away_two)
        modal = order.pause(modal)
        p2, away = sums_pass(order, places, folds=[(last_near, last_core, [D])])
        p2_in = across(away)
        down_grad = settle(order, "turn", places, [(u1_pay, d1_out), (u2_pay, d2_out)], [(D, D)])
        oq, u2, p1 = sums_pass(
            order, places, adds=[(oq, oq_in), (u2, u2_mid), (p1, p1_in)]
        )
        u1_out = oq_in
        oq_mid, u2_out, p1_in = over_middle(oq), to_outer(u2), to_inner(p1)
        p2 = sums_pass(order, places, adds=[(p2, p2_in)])
        p2_in = to_inner(p2)
        p1 = sums_pass(order, places, adds=[(p1, p1_in)])
        p1_mid = over_middle(p1)
        (modal,) = order.hold([modal])
        partner_modal = from_partner(modal)
        oq, p2 = sums_pass(order, places, adds=[(oq, oq_mid), (p2, p2_in)], waits=[u2_out])
        oq_out, p2_mid = to_outer(oq), over_middle(p2)
        up_grad = settle(order, "columns", places, [(oq_pay, u1_out), (u2, u2_out)], [(D // 4, FF)])
        p1 = sums_pass(order, places, adds=[(p1, p1_mid)])
        p1_out = to_outer(p1)
        p2 = sums_pass(order, places, adds=[(p2, p2_mid)])
        p2_out = to_outer(p2)
        mixed_rows = mix_pass(order, modal, partner_modal, columns, [oq_out])
        qkv_grad, out_grad = settle(
            order,
            "pairs",
            places,
            [(oq, oq_out), (p1, p1_out)],
            [(D // 4, 3 * D), (D // 4, D)],
        )
        qkv_grad, shorts = last_settle(order, places, (p2, p2_out), qkv_grad)
    else:
        (down_block,) = down_grads(order, places, modal_low, hidden, 0, D, 1, count)
        middle_grad, middle_low, context_grad, upper_low, *rest = chain_pass(*back)
        hidden_bias_grad, gain_two_grad, bias_two_grad = rest
        (up_block,) = up_grads(order, places, second, upper_low, [FF], count)
        gate_sums = gate_sums_pass(order, modal, columns)
        for group in range(GROUPS):
            attend_back_group(group)
        mixed_rows = mix_pass(order, modal, from_partner(modal), columns)
        pair_low, lead_block = lead_grads(
            order, places, contexts, middle_low, normed, query_grads, own_grads[0], returned[0], count
        )
        region_grad, last_block = last_pass(pair_low)
        lead_block = lead_block[0]
        short_rows = last_block[D:].astype(f32)

        def total(block):
            groups = modality_groups()
            owned = lax.psum_scatter(
                block.astype(f32), "stream", axis_index_groups=groups, tiled=True
            )
            return lax.psum(owned, "dp")

        down_grad = total(down_block[0].T)
        up_grad, out_grad = total(up_block[0]), total(lead_block[:, :D])
        qkv_grad = total(
            jnp.concatenate(
                [
                    lead_block[:, D : 2 * D + PART],
                    last_block[:D, :PART],
                    lead_block[:, 2 * D + PART :],
                    last_block[:D, PART:],
                ],
                axis=1,
            )
        )
        short_rows = lax.psum(
            lax.psum(short_rows, "stream", axis_index_groups=modality_groups()), "dp"
        )

        shard = D // half
        own_rows = lax.dynamic_slice_in_dim(short_rows, side * shard, shard, 1)
        hidden_rows = short_rows[8 : 8 + FF // D].reshape(FF)
        own_hidden = lax.dynamic_slice_in_dim(hidden_rows, side * (FF // half), FF // half, 0)
        shorts = [own_rows[k] for k in range(7)] + [own_hidden]
    return (
        mixed_rows,
        region_grad,
        qkv_grad,
        out_grad,
        up_grad,
        down_grad,
        shorts[0],
        shorts[1],
        shorts[2],
        shorts[3],
        shorts[7],
        shorts[4],
        shorts[5],
        shorts[6],
    )


def solution(mesh):
    in_specs = (
        P(("stream", "dp"), None),
        P(("stream", "dp"), None),
        P(),
        P("stream", None),
        P("stream", None),
        P("stream", None),
        P("stream", None),
        P("stream"),
        P("stream"),
        P("stream"),
        P("stream"),
        P("stream"),
        P("stream"),
        P("stream"),
        P("stream"),
    )
    out_specs = (
        P(("stream", "dp"), None),
        P(("stream", "dp"), None),
        P("stream", None),
        P("stream", None),
        P("stream", None),
        P("stream", None),
        P("stream"),
        P("stream"),
        P("stream"),
        P("stream"),
        P("stream"),
        P("stream"),
        P("stream"),
        P("stream"),
    )
    return jax.shard_map(body, mesh=mesh, in_specs=in_specs, out_specs=out_specs, check_vma=False)
```

```python
import functools
import math

import jax
import jax.numpy as jnp
from jax import lax
from jax.experimental import pallas as pl
from jax.experimental.pallas import tpu as pltpu
from jax.sharding import PartitionSpec as P

D = 768
HEADS = 12
HEAD_DIM = 64
FF = 3072
LEAD = FF - 1280
RUNS = ((LEAD, 768), (LEAD + 768, 512))
SEQ = 512
GROUPS = 2
PART = D // GROUPS
PAIR = 2 * HEAD_DIM
BLOCK = 128
REACH = 96
ROWS = 256
MIB = 1024 * 1024

epsilon = 1e-05
masked_score = -1e30
score_scale = HEAD_DIM ** (-0.5)
gelu_scale = math.sqrt(2.0 / math.pi)
gelu_cubic = 0.044715

f32 = jnp.float32
bf16 = jnp.bfloat16

WINDOWS = [
    (max(0, start - REACH), min(SEQ, start + BLOCK + REACH)) for start in range(0, SEQ, BLOCK)
]
WINDOW = BLOCK + 2 * REACH

in_smem = pl.BlockSpec(memory_space=pltpu.SMEM)
in_vmem = pl.BlockSpec(memory_space=pltpu.VMEM)
in_any = pl.BlockSpec(memory_space=pl.ANY)
in_hbm = pl.BlockSpec(memory_space=pltpu.HBM)


def shape_of(dims, dtype):
    return jax.ShapeDtypeStruct(dims, dtype)


def dot(left, right):
    return lax.dot_general(left, right, (((1,), (0,)), ((), ())), preferred_element_type=f32)


def dot_nt(left, right):
    return lax.dot_general(left, right, (((1,), (1,)), ((), ())), preferred_element_type=f32)


def dot_tn(left, right):
    return lax.dot_general(left, right, (((0,), (0,)), ((), ())), preferred_element_type=f32)


def normalise(values):
    average = jnp.mean(values, axis=-1, keepdims=True)
    centred = values - average
    spread = jnp.mean(centred * centred, axis=-1, keepdims=True)
    root = lax.rsqrt(spread + epsilon)
    return centred * root, root


def norm_back(scaled, root, gain, incoming):
    weighted = incoming * gain
    average = jnp.mean(weighted, axis=-1, keepdims=True)
    slope = jnp.mean(weighted * scaled, axis=-1, keepdims=True)
    return root * (weighted - average - scaled * slope)


def column_sums(values):
    return jnp.sum(values, axis=0, keepdims=True)


class Order:
    def __init__(self):
        self.token = []

    def call(
        self,
        kernel,
        args,
        in_specs,
        outs,
        out_specs,
        scratch=(),
        grid=(),
        limit=16,
        name=None,
        prefetch=None,
        waits=(),
        aliases=None,
        cost=0,
    ):
        given = len(args)
        extra = list(self.token) + list(waits)
        ahead = [] if prefetch is None else [prefetch]
        count = len(ahead)
        smallest = min(math.prod(out.shape) for out in outs)
        marked = smallest > 4096 and not aliases
        outs, out_specs = list(outs), list(out_specs)
        if marked:
            outs.append(shape_of((8, 128), f32))
            out_specs.append(in_vmem)
        place = count + given + len(extra) + len(outs) - 1

        def wrapped(*refs):
            used = list(refs[: count + given]) + list(refs[count + given + len(extra) :])
            if marked:
                refs[place][...] = jnp.zeros((8, 128), f32)
                used.pop(count + given + len(outs) - 1)
            kernel(*used)

        results = pl.pallas_call(
            wrapped,
            out_shape=outs,
            grid_spec=pltpu.PrefetchScalarGridSpec(
                num_scalar_prefetch=count,
                grid=grid,
                in_specs=list(in_specs) + [in_any] * len(extra),
                out_specs=out_specs,
                scratch_shapes=list(scratch),
            ),
            compiler_params=pltpu.CompilerParams(vmem_limit_bytes=limit * MIB),
            cost_estimate=pl.CostEstimate(flops=1 + cost * 10**9, bytes_accessed=1 + cost * MIB, transcendentals=cost * 10**6),
            input_output_aliases=aliases or {},
            name=name,
        )(*ahead, *args, *extra)
        self.token = [min(results, key=lambda out: out.size)]
        return list(results)[:-1] if marked else results

    def hold(self, arrays, waits=()):
        return self.call(
            lambda *refs: None,
            arrays,
            [in_any] * len(arrays),
            [shape_of(array.shape, array.dtype) for array in arrays],
            [in_any] * len(arrays),
            name="hold",
            cost=0,
            waits=waits,
            aliases={k: k for k in range(len(arrays))},
        )

    def pause(self, value):
        return self.call(
            lambda *refs: None,
            [value],
            [in_any],
            [shape_of(value.shape, value.dtype)],
            [in_any],
            name="pause",
            cost=60,
            aliases={0: 0},
        )[0]


def assemble(places, parts, whole):
    rows = whole.shape[0] // len(parts)
    for k, part in enumerate(parts):
        whole[pl.ds(pl.multiple_of(places[k] * rows, 16), rows)] = part[:rows]


def sums_pass(order, places, folds=(), adds=(), pays=(), waits=(), extra=0):
    args, outs, steps = [], [], []

    def give(*arrays):
        args.extend(arrays)
        return list(range(len(args) - len(arrays), len(args)))

    def make(dims, dtype):
        outs.append(shape_of(dims, dtype))
        return len(outs) - 1

    for near, received, widths in folds:
        made = []
        for width in widths:
            rows = near.shape[1] if len(near.shape) == 3 else (near.shape[0] + 16) // 2
            made += [make((rows + add, width), near.dtype) for add in (0, extra)]
        steps.append(("fold", give(near, received), made))
    for left, right in adds:
        steps.append(("add", give(left, right), [make(left.shape, left.dtype)]))
    for mine, received, older, crossed in pays:
        given = give(mine, received, older, crossed)
        steps.append(("pay", given, [make(mine.shape, mine.dtype) for _ in range(2)]))
    count = len(args)

    def kernel(places_ref, *refs):
        ins, results = refs[:count], refs[count:]
        inner = jnp.logical_and(places_ref[4] > 0, places_ref[4] < 3)
        for kind, given, made in steps:
            if kind == "fold" and len(ins[given[0]].shape) == 3:
                first = 0
                for k in range(0, len(made), 2):
                    width = results[made[k]].shape[1]
                    part = slice(first, first + width)
                    for slot in range(2):
                        total = ins[given[0]][slot, :, part].astype(f32)
                        total += ins[given[1]][slot, :, part].astype(f32)
                        results[made[k + slot]][: total.shape[0]] = total.astype(bf16)
                    if extra:
                        results[made[k + 1]][total.shape[0] :] = jnp.zeros((extra, width), bf16)
                    first += width
            elif kind == "fold":
                total = (ins[given[0]][...].astype(f32) + ins[given[1]][...].astype(f32)).astype(bf16)
                rows = results[made[0]].shape[0] - 16
                for slot in range(2):
                    results[made[slot]][:rows] = total[slot * rows : (slot + 1) * rows]
                    results[made[slot]][rows:] = total[2 * rows :]
            elif kind == "add":
                rows = ins[given[0]].shape[0]
                total = ins[given[0]][...].astype(f32) + ins[given[1]][:rows].astype(f32)
                results[made[0]][...] = total.astype(results[made[0]].dtype)
            else:
                rows = ins[given[0]].shape[0]
                fresh = ins[given[0]][...].astype(f32) + ins[given[1]][:rows].astype(f32)
                older = ins[given[2]][...].astype(f32) + ins[given[3]][...].astype(f32)
                results[made[0]][...] = fresh.astype(results[made[0]].dtype)
                results[made[1]][...] = jnp.where(inner, older, fresh).astype(results[made[1]].dtype)

    found = order.call(
        kernel,
        [places, *args],
        [in_smem] + [in_vmem] * len(args),
        outs,
        [in_vmem] * len(outs),
        limit=12,
        name="sums",
        waits=waits,
    )
    found = list(found)
    return found[0] if len(found) == 1 else found


def first_cast_kernel(sizes, qkv, short, out, rows):
    rows[...] = jnp.zeros_like(rows)
    offset = 0
    for line, size in enumerate(sizes):
        rows[line : line + 1, :size] = short[:, offset : offset + size]
        offset += size
    height = qkv.shape[0]
    out[height:] = rows[...].astype(bf16)
    out[:height] = qkv[...].astype(bf16)


def first_cast_pass(order, qkv, members):
    return order.call(
        functools.partial(first_cast_kernel, [member.size for member in members]),
        [qkv, jnp.concatenate(members)[None]],
        [in_vmem] * 2,
        [shape_of((qkv.shape[0] + 16, 3 * D), bf16)],
        [in_vmem],
        scratch=[pltpu.VMEM((16, 3 * D), f32)],
        limit=16,
        name="first_cast",
    )[0]


def cast_kernel(
    places,
    lengths,
    left,
    right,
    down,
    wide_out,
    down_out,
    lead_out,
    half_out,
    row_out,
    column_out,
):
    wide_out[:, :D] = left[...].astype(bf16)
    wide_out[:, D:] = right[...].astype(bf16)
    down_out[...] = down[...].astype(bf16)
    lead_out[...] = wide_out[:, : lead_out.shape[1]]
    rows = left.shape[0]
    turn = places[4] % 2
    first = turn * 2 * rows
    for run in range(2):
        start = pl.multiple_of(first + run * rows, 16)
        half_out[:rows, run * D : (run + 1) * D] = down_out[pl.ds(start, rows)]
    start = pl.multiple_of(turn * (rows // 2), 16)
    line = rows
    for column, width in RUNS:
        count = 2 * D // width
        height = rows // 2 // count
        for run in range(count):
            part = pl.ds(pl.multiple_of(start + run * height, 16), height)
            block = wide_out[part, D + column : D + column + width]
            half_out[line : line + height, run * width : (run + 1) * width] = block
        line += height
    pack = places[0] * 4 + places[4]
    row_places = lax.broadcasted_iota(jnp.int32, (1, SEQ), 1)
    column_places = lax.broadcasted_iota(jnp.int32, (SEQ, 1), 0)
    page_row, page_column = jnp.zeros_like(row_places), jnp.zeros_like(column_places)
    end = jnp.int32(0)
    for page in range(lengths.shape[1]):
        end += lengths[pack, page]
        page_row += (row_places >= end).astype(jnp.int32)
        page_column += (column_places >= end).astype(jnp.int32)
    row_out[...] = page_row
    column_out[...] = page_column


def cast_pass(order, places, lengths, left, right, down):
    rows = left.shape[0]
    return order.call(
        cast_kernel,
        [places, lengths, left, right, down],
        [in_smem] * 2 + [in_vmem] * 3,
        [
            shape_of((rows, D + FF), bf16),
            shape_of(down.shape, bf16),
            shape_of((rows, D + LEAD), bf16),
            shape_of((rows + sum(rows * width // (4 * D) for _, width in RUNS), 2 * D), bf16),
            shape_of((1, SEQ), jnp.int32),
            shape_of((SEQ, 1), jnp.int32),
        ],
        [in_vmem] * 6,
        limit=16,
        name="cast",
    )


def pairs_kernel(count, packed, places, rows, *rest):
    given, rest = ((), rest) if packed else (rest[:2], rest[2:])
    parts, rest = rest[:count], rest[count:]
    pair_outs, rest = rest[:GROUPS], rest[GROUPS:]
    normed_out, vectors_out, hidden_out, weight, wide_pair, last_pair, sems = rest
    pairs = [wide_pair.at[k] for k in range(GROUPS - 1)] + [last_pair]
    shard = D // count
    if packed:
        vectors = jnp.zeros((8, D), f32)
        line = lax.broadcasted_iota(jnp.int32, (8, D), 0)
        for k in range(count):
            block = parts[k][shard : shard + 16, :D].astype(f32)[:8]
            vectors += pltpu.roll(jnp.where(line < 7, block, 0.0), places[k] * shard, 1)
            start = pl.multiple_of(places[k] * D, 128)
            hidden_out[:, pl.ds(start, D)] = block[7:8]
    else:
        vectors = given[0][...]
        hidden_out[...] = given[1][...]
    vectors_out[...] = vectors
    for k, part in enumerate(parts):
        weight[pl.ds(pl.multiple_of(places[k] * shard, 16), shard)] = part[:shard, D:]
    scaled, _ = normalise(rows[...].astype(f32))
    normed_out[...] = (scaled * vectors[0:1] + vectors[1:2]).astype(bf16)
    for kind in range(2):
        line = vectors[6:7, kind * PART : (kind + 1) * PART]
        last_pair[kind, SEQ:] = jnp.concatenate([line] * 16, axis=0).astype(bf16)
    copies = []
    for group in range(GROUPS):
        for kind in range(2):
            first = kind * D + group * PART
            block = dot(normed_out[...], weight[:, first : first + PART])
            pairs[group][kind, :SEQ] = block.astype(bf16)
        copies.append(pltpu.make_async_copy(pairs[group], pair_outs[group], sems.at[group]))
        copies[-1].start()
    for copy in copies:
        copy.wait()


def pairs_pass(order, places, rows, parts, given=(), waits=()):
    count = len(parts)
    outs = order.call(
        functools.partial(pairs_kernel, count, not given),
        [places, rows, *given, *parts],
        [in_smem] + [in_vmem] * (1 + len(given) + count),
        [shape_of((2, SEQ, PART), bf16)] * (GROUPS - 1)
        + [
            shape_of((2, SEQ + 16, PART), bf16),
            shape_of((SEQ, D), bf16),
            shape_of((8, D), f32),
            shape_of((1, FF), f32),
        ],
        [in_hbm] * GROUPS + [in_vmem] * 3,
        scratch=[
            pltpu.VMEM((D, 2 * D), bf16),
            pltpu.VMEM((GROUPS - 1, 2, SEQ, PART), bf16),
            pltpu.VMEM((2, SEQ + 16, PART), bf16),
            pltpu.SemaphoreType.DMA((GROUPS,)),
        ],
        limit=16,
        name="pairs",
        waits=waits,
    )
    return outs[:GROUPS], *outs[GROUPS:]


def queries_kernel(places, normed, *rest):
    parts, (out, weight) = rest[:-2], rest[-2:]
    shard = D // len(parts)
    for k, part in enumerate(parts):
        weight[pl.ds(pl.multiple_of(places[k] * shard, 16), shard)] = part[:shard, :D]
    for first in range(0, D, PART):
        block = dot(normed[...], weight[:, first : first + PART])
        out[:, first : first + PART] = block.astype(bf16)


def queries_pass(order, places, normed, parts):
    return order.call(
        queries_kernel,
        [places, normed, *parts],
        [in_smem] + [in_vmem] * (1 + len(parts)),
        [shape_of((SEQ, D), bf16)],
        [in_vmem],
        scratch=[pltpu.VMEM((D, D), bf16)],
        limit=16,
        name="queries",
    )[0]


def fill_page_bias(page_row, page_column, bias):
    for index, (low, high) in enumerate(WINDOWS):
        start = index * BLOCK
        same = page_column[low:high] == page_row[:, start : start + BLOCK]
        bias[index, : high - low] = jnp.where(same, 0.0, masked_score)


def two_heads(block):
    lane = lax.broadcasted_iota(jnp.int32, block.shape, 1)
    zero = jnp.zeros_like(block)
    return jnp.concatenate(
        [jnp.where(lane < HEAD_DIM, block, zero), jnp.where(lane < HEAD_DIM, zero, block)], axis=0
    )


def head_rows(both):
    return jnp.concatenate([both[:HEAD_DIM, :BLOCK], both[HEAD_DIM:, BLOCK:]], axis=0).T


def page_bias(bias, index, size):
    block = bias[index, :size]
    return jnp.concatenate([block, block], axis=1)


def attend_kernel(
    query_first, query, own, other, page_row, page_column, context, log_total, bias
):
    fill_page_bias(page_row, page_column, bias)

    def exponents_of(step, index):
        low, high = WINDOWS[index]
        rows, lanes = slice(index * BLOCK, (index + 1) * BLOCK), slice(step * PAIR, (step + 1) * PAIR)
        query_lanes = slice((query_first + step) * PAIR, (query_first + step + 1) * PAIR)
        queries = two_heads(query[rows, query_lanes] * score_scale)
        allowed = page_bias(bias, index, high - low)
        scores = [dot_nt(side[0, low:high, lanes], queries) + allowed for side in (own, other)]
        largest = jnp.max(jnp.maximum(*scores), axis=0, keepdims=True)
        exponents = [jnp.exp(score - largest) for score in scores]
        total = column_sums(exponents[0] + exponents[1])
        log_total[step, index : index + 1] = largest + jnp.log(total)
        return exponents, 1.0 / total

    def context_of(step, index, found):
        exponents, inverse = found
        low, high = WINDOWS[index]
        rows, lanes = slice(index * BLOCK, (index + 1) * BLOCK), slice(step * PAIR, (step + 1) * PAIR)
        both = 0.0
        for side, exponent in zip((own, other), exponents):
            both += dot_tn(side[1, low:high, lanes], (exponent * inverse).astype(bf16))
        context[rows, lanes] = head_rows(both).astype(bf16)

    steps = [(k, w) for k in range(context.shape[1] // PAIR) for w in range(len(WINDOWS))]
    found = exponents_of(*steps[0])
    for place, now in enumerate(steps):
        ahead = exponents_of(*steps[place + 1]) if place + 1 < len(steps) else None
        context_of(*now, found)
        found = ahead


def attend(order, query_first, queries, own, other, page_row, page_column, waits=()):
    width = own.shape[2]
    return order.call(
        functools.partial(attend_kernel, query_first),
        [queries, own, other, page_row, page_column],
        [in_vmem] * 5,
        [
            shape_of((SEQ, width), bf16),
            shape_of((width // PAIR, len(WINDOWS), 2 * BLOCK), f32),
        ],
        [in_vmem] * 2,
        scratch=[pltpu.VMEM((len(WINDOWS), WINDOW, BLOCK), f32)],
        limit=12,
        name="attend",
        cost=60,
        waits=waits,
    )


def attend_back_kernel(
    query_first,
    query,
    own,
    other,
    context_grad,
    log_total,
    page_row,
    page_column,
    *rest,
):
    *given, query_grad, own_grad, other_grad, bias, other_sum = rest
    fill_page_bias(page_row, page_column, bias)
    own_grad[...] = jnp.zeros_like(own_grad)
    other_sum[...] = jnp.zeros_like(other_sum)

    def shares_of(step, index):
        low, high = WINDOWS[index]
        rows, lanes = slice(index * BLOCK, (index + 1) * BLOCK), slice(step * PAIR, (step + 1) * PAIR)
        query_lanes = slice((query_first + step) * PAIR, (query_first + step + 1) * PAIR)
        queries = two_heads(query[rows, query_lanes] * score_scale)
        grads = two_heads(context_grad[rows, query_lanes])
        offset = page_bias(bias, index, high - low) - log_total[step, index : index + 1]
        halves = []
        for side in (own, other):
            shares = jnp.exp(dot_nt(side[0, low:high, lanes], queries) + offset)
            halves.append((shares, dot_nt(side[1, low:high, lanes], grads)))
        centre = sum(column_sums(shares * share_grad) for shares, share_grad in halves)
        return queries, grads, halves, centre

    def grads_of(step, index, found):
        queries, grads, halves, centre = found
        low, high = WINDOWS[index]
        rows, lanes = slice(index * BLOCK, (index + 1) * BLOCK), slice(step * PAIR, (step + 1) * PAIR)
        both = 0.0
        for side, total, (shares, share_grad) in zip((own, other), (own_grad, other_sum), halves):
            score_grad = (shares * (share_grad - centre)).astype(bf16)
            total[1, low:high, lanes] += dot(shares.astype(bf16), grads)
            total[0, low:high, lanes] += dot(score_grad, queries)
            both += dot_tn(side[0, low:high, lanes], score_grad)
        query_grad[rows, lanes] = (head_rows(both) * score_scale).astype(bf16)

    steps = [(k, w) for k in range(own_grad.shape[2] // PAIR) for w in range(len(WINDOWS))]
    found = shares_of(*steps[0])
    for place, now in enumerate(steps):
        ahead = shares_of(*steps[place + 1]) if place + 1 < len(steps) else None
        grads_of(*now, found)
        found = ahead
    other_grad[:, :SEQ] = other_sum[...].astype(bf16)
    if given:
        for kind in range(2):
            line = given[0][:, kind * PART : (kind + 1) * PART]
            other_grad[kind, SEQ:] = jnp.concatenate([line] * 2, axis=0).astype(bf16)


def attend_back(
    order, query_first, queries, own, other, context_grad, logs, page_row, page_column, given
):
    return order.call(
        functools.partial(attend_back_kernel, query_first),
        [queries, own, other, context_grad, logs, page_row, page_column, *given],
        [in_vmem] * (7 + len(given)),
        [
            shape_of((SEQ, PART), bf16),
            shape_of((2, SEQ, PART), f32),
            shape_of((2, SEQ + 16 * len(given), PART), bf16),
        ],
        [in_vmem] * 3,
        scratch=[
            pltpu.VMEM((len(WINDOWS), WINDOW, BLOCK), f32),
            pltpu.VMEM((2, SEQ, PART), f32),
        ],
        limit=16,
        name="attend_back",
        cost=60,
    )


def partner_cross(pair):
    rows = pair[:, SEQ:].astype(f32)
    return jnp.concatenate([rows[0, :1], rows[1, :1]], axis=1)


def join_blocks(places, wides, downs, leads, halves, wide, down):
    rows = wide.shape[0] // (len(wides) + len(leads))
    for k, part in enumerate(wides):
        wide[pl.ds(pl.multiple_of(places[k] * rows, 16), rows)] = part[...]
        down[k] = downs[k][...]
    turn = places[4] % 2
    for k, part in enumerate(leads):
        first = places[len(wides) + k] * rows
        wide[pl.ds(pl.multiple_of(first, 16), rows), : part.shape[1]] = part[...]
        for side, half in enumerate(halves[k]):
            place = turn if side == 0 else 1 - turn
            line = rows
            for column, width in RUNS:
                runs = 2 * D // width
                height = rows // 2 // runs
                for run in range(runs):
                    start = pl.multiple_of(first + place * (rows // 2) + run * height, 16)
                    block = half[line : line + height, run * width : (run + 1) * width]
                    wide[pl.ds(start, height), D + column : D + column + width] = block
                line += height
            for run in range(2):
                start = pl.multiple_of((2 * place + run) * rows, 16)
                down[len(wides) + k, pl.ds(start, rows)] = half[:rows, run * D : (run + 1) * D]


def middle_kernel(kinds, places, rows, *rest):
    contexts, rest = rest[:GROUPS], rest[GROUPS:]
    (tangent, vectors, partner, hidden_bias), rest = rest[:4], rest[4:]
    wides, downs, leads = [], [], []
    for group, size in zip((wides, downs, leads), kinds):
        group += rest[:size]
        rest = rest[size:]
    halves = [rest[2 * k : 2 * k + 2] for k in range(kinds[2])]
    rest = rest[2 * kinds[2] :]
    middle_out, second_out, hidden_out, slope_out, modal_out, inner_out, wide, down, total = rest
    join_blocks(places, wides, downs, leads, halves, wide, down)
    count = down.shape[0]
    middle = rows[...].astype(f32)
    for group, context in enumerate(contexts):
        middle += dot(context[...], wide[group * PART : (group + 1) * PART, :D])
    middle_out[...] = middle
    scaled, _ = normalise(middle)
    second_out[...] = (scaled * vectors[2:3] + vectors[3:4]).astype(bf16)
    total[...] = middle + vectors[4:5]
    slot = FF // count
    size = 768
    def upper_of(k, first):
        start = places[k] * slot + first
        part = pl.ds(pl.multiple_of(start, 128), size)
        column = pl.ds(pl.multiple_of(D + start, 128), size)
        return part, dot(second_out[...], wide[:, column]) + hidden_bias[:, part]

    steps = [(k, first) for k in range(count) for first in range(0, slot, size)]
    found = upper_of(*steps[0])
    for place, (k, first) in enumerate(steps):
        ahead = upper_of(*steps[place + 1]) if place + 1 < len(steps) else None
        part, upper = found
        square = upper * upper
        angle = jnp.tanh(upper * (gelu_scale + (gelu_cubic * gelu_scale) * square))
        half = 0.5 + 0.5 * angle
        hidden = (upper * half).astype(bf16)
        hidden_out[:, part] = hidden
        bend = 2.0 * gelu_scale + (6.0 * gelu_cubic * gelu_scale) * square
        slope_out[:, part] = (half + half * (1.0 - half) * (upper * bend)).astype(bf16)
        total[...] += dot(hidden, down[k, first : first + size])
        found = ahead
    modal_out[...] = total[...].astype(bf16)
    modal = modal_out[...].astype(f32)
    own = jnp.sum(modal * vectors[5:6], axis=1, keepdims=True)
    cross = jnp.sum(modal * partner_cross(partner), axis=1, keepdims=True)
    met = jnp.sum(modal * tangent[...].astype(f32), axis=1, keepdims=True)
    lane = lax.broadcasted_iota(jnp.int32, (SEQ, 128), 1)
    columns = jnp.where(lane == 0, own, jnp.where(lane == 1, cross, met))
    inner_out[...] = columns.T[:8]


def middle_pass(
    order, places, rows, contexts, tangent, vectors, partner, hidden_bias, wides, downs, leads, halves
):
    count = len(wides) + len(leads)
    parts = [*wides, *downs, *leads] + [piece for pair in halves for piece in pair]
    return order.call(
        functools.partial(middle_kernel, (len(wides), len(downs), len(leads))),
        [places, rows, *contexts, tangent, vectors, partner, hidden_bias, *parts],
        [in_smem] + [in_vmem] * (5 + GROUPS + len(parts)),
        [
            shape_of((SEQ, D), f32),
            shape_of((SEQ, D), bf16),
            shape_of((SEQ, FF), bf16),
            shape_of((SEQ, FF), bf16),
            shape_of((SEQ, D), bf16),
            shape_of((8, SEQ), f32),
            shape_of((D, D + FF), bf16),
            shape_of((count, FF // count, D), bf16),
        ],
        [in_vmem] * 8,
        scratch=[pltpu.VMEM((SEQ, D), f32)],
        limit=16,
        name="middle",
    )


def gate_kernel(
    own,
    other,
    tangent,
    partner_tangent,
    vectors,
    partner,
    grad_out,
    low_out,
    columns_out,
    sums,
):
    gate = jax.nn.sigmoid(own[0:1] + other[1:2])
    gate_two = jax.nn.sigmoid(other[0:1] + own[1:2])
    logit = other[2:3] * gate * (1.0 - gate)
    logit_two = own[2:3] * gate_two * (1.0 - gate_two)
    padding = jnp.zeros((124, SEQ), f32)
    columns = jnp.concatenate([gate, logit, gate_two, logit_two, padding], axis=0).T
    columns_out[...] = columns
    grad = (
        tangent[...].astype(f32)
        + columns[:, 1:2] * vectors[5:6]
        + partner_tangent[...].astype(f32) * columns[:, 2:3]
        + columns[:, 3:4] * partner_cross(partner)
    )
    grad_out[...] = grad
    low_out[...] = grad.astype(bf16)
    sums[...] = column_sums(grad)


def gate_pass(order, own, other, tangent, partner_tangent, vectors, partner):
    return order.call(
        gate_kernel,
        [own, other, tangent, partner_tangent, vectors, partner],
        [in_vmem] * 6,
        [
            shape_of((SEQ, D), f32),
            shape_of((SEQ, D), bf16),
            shape_of((SEQ, 128), f32),
            shape_of((1, D), f32),
        ],
        [in_vmem] * 4,
        name="gate",
    )


def mix_kernel(own, other, columns, mixed):
    mixed[...] = (
        own[...].astype(f32) + columns[:, 0:1] * other[...].astype(f32)
    ).astype(bf16)


def mix_pass(order, own, other, columns, waits=()):
    return order.call(
        mix_kernel,
        [own, other, columns],
        [in_vmem] * 3,
        [shape_of((SEQ, D), bf16)],
        [in_vmem],
        name="mix",
        cost=60,
        waits=waits,
    )[0]


def gate_sums_kernel(own, columns, out):
    rows = own[...].astype(f32)
    out[...] = jnp.zeros_like(out)
    out[0:1] = column_sums(columns[:, 1:2] * rows)
    out[1:2] = column_sums(columns[:, 3:4] * rows)


def gate_sums_pass(order, own, columns):
    return order.call(
        gate_sums_kernel, [own, columns], [in_vmem] * 2, [shape_of((8, D), f32)], [in_vmem], name="gate_sums"
    )[0]


def chain_kernel(places, low, grad, slope, middle, vectors, wide, down, *rest):
    total_out, total_low_out, context_out, upper_out, upper_sums, gain_sums, bias_sums = rest[:7]
    normed_grad = rest[7]
    normed_grad[...] = jnp.zeros_like(normed_grad)
    count = down.shape[0]
    slot = FF // count
    size = 768
    def upper_of(k, first):
        start = places[k] * slot + first
        part = pl.ds(pl.multiple_of(start, 128), size)
        column = pl.ds(pl.multiple_of(D + start, 128), size)
        return part, column, dot_nt(low[...], down[k, first : first + size])

    steps = [(k, first) for k in range(count) for first in range(0, slot, size)]
    found = upper_of(*steps[0])
    for place in range(len(steps)):
        ahead = upper_of(*steps[place + 1]) if place + 1 < len(steps) else None
        part, column, upper = found
        upper = upper * slope[:, part].astype(f32)
        upper_sums[:, part] = column_sums(upper)
        upper_low = upper.astype(bf16)
        upper_out[:, part] = upper_low
        normed_grad[...] += dot_nt(upper_low, wide[:, column])
        found = ahead
    scaled, root = normalise(middle[...])
    incoming = normed_grad[...]
    gain_sums[...] = column_sums(incoming * scaled)
    bias_sums[...] = column_sums(incoming)
    total = grad[...] + norm_back(scaled, root, vectors[2:3], incoming)
    total_out[...] = total
    total_low_out[...] = total.astype(bf16)
    context_out[...] = dot_nt(total_low_out[...], wide[:, :D]).astype(bf16)


def chain_pass(order, places, low, grad, slope, middle, vectors, wide, down):
    return order.call(
        chain_kernel,
        [places, low, grad, slope, middle, vectors, wide, down],
        [in_smem] + [in_vmem] * 7,
        [
            shape_of((SEQ, D), f32),
            shape_of((SEQ, D), bf16),
            shape_of((SEQ, D), bf16),
            shape_of((SEQ, FF), bf16),
            shape_of((1, FF), f32),
            shape_of((1, D), f32),
            shape_of((1, D), f32),
        ],
        [in_vmem] * 7,
        scratch=[pltpu.VMEM((SEQ, D), f32)],
        limit=20,
        name="chain",
    )


def slots_of(count):
    return (list(range(0, count, 2)), list(range(1, count, 2)))


def block_shapes(widths, count):
    near, far = slots_of(count)
    rows = D // count
    outs = []
    for width in widths:
        outs.append(shape_of((len(near), rows, width), bf16))
        if far:
            outs.append(shape_of((len(far), rows, width), bf16))
    return outs


def store_blocks(places, count, products, widths, outs, whole):
    near, far = slots_of(count)
    rows = D // count
    products = list(products)
    each = 2 if far else 1
    for index, width in enumerate(widths):
        low = 0
        while low < width:
            left, right = products.pop(0)
            whole[:, low : low + right.shape[1]] = dot(left, right).astype(bf16)
            low += right.shape[1]
        for out, slots in zip(outs[each * index : each * index + each], (near, far)):
            for place, slot in enumerate(slots):
                begin = pl.multiple_of(places[slot] * rows, 16)
                out[place] = whole[pl.ds(begin, rows), :width]


def up_grads_kernel(count, widths, places, second, upper, *rest):
    turned = second[...].T
    products = [(turned, upper[:, k : k + 512]) for k in range(0, FF, 512)]
    store_blocks(places, count, products, widths, rest[:-1], rest[-1])


def up_grads(order, places, second, upper, widths, count):
    outs = block_shapes(widths, count)
    return order.call(
        functools.partial(up_grads_kernel, count, widths),
        [places, second, upper],
        [in_smem] + [in_vmem] * 2,
        outs,
        [in_vmem] * len(outs),
        scratch=[pltpu.VMEM((D, max(widths)), bf16)],
        limit=16,
        name="up_grads",
    )


def lead_grads_kernel(count, places, context, context_two, low, normed, *rest):
    queries, (own, returned), rest = rest[:GROUPS], rest[GROUPS : GROUPS + 2], rest[GROUPS + 2 :]
    pair_low, outs, whole = rest[0], rest[1:-1], rest[-1]
    pair_low[...] = (own[...] + returned[:, :SEQ].astype(f32)).astype(bf16)
    turned = jnp.concatenate([context[...].T, context_two[...].T], axis=0)
    products = [(turned, low[:, k : k + PART]) for k in range(0, D, PART)]
    turned = normed[...].T
    products += [(turned, query[...]) for query in queries]
    products += [(turned, pair_low[kind]) for kind in range(2)]
    store_blocks(places, count, products, [3 * D], outs, whole)


def lead_grads(order, places, contexts, low, normed, queries, own, returned, count):
    outs = block_shapes([3 * D], count)
    args = [*contexts, low, normed, *queries, own, returned]
    return order.call(
        functools.partial(lead_grads_kernel, count),
        [places, *args],
        [in_smem] + [in_vmem] * len(args),
        [shape_of(own.shape, bf16)] + outs,
        [in_vmem] * (1 + len(outs)),
        scratch=[pltpu.VMEM((D, 3 * D), bf16)],
        limit=16,
        name="lead_grads",
    )


def down_grads_kernel(count, first, height, fold, places, low, hidden, *outs):
    near, far = slots_of(count)
    width = FF // count
    turned = low[:, first : first + height].T
    rows = height // fold
    for out, slots in zip(outs, (near, far)):
        for place, slot in enumerate(slots):
            begin = pl.multiple_of(places[slot] * width, 128)
            block = dot(turned, hidden[:, pl.ds(begin, width)]).astype(bf16)
            for k in range(fold):
                out[place, :, k * width : (k + 1) * width] = block[k * rows : (k + 1) * rows]


def gate_lead_kernel(count, height, fold, places, hidden, *rest):
    gate_kernel(*rest[:10])
    down_grads_kernel(count, 0, height, fold, places, rest[7], hidden, *rest[10:])


def gate_lead_pass(
    order, places, hidden, own, other, tangent, partner_tangent, vectors, partner, height, fold, count
):
    near, far = slots_of(count)
    dims = (height // fold, fold * (FF // count))
    return order.call(
        functools.partial(gate_lead_kernel, count, height, fold),
        [places, hidden, own, other, tangent, partner_tangent, vectors, partner],
        [in_smem] + [in_vmem] * 7,
        [
            shape_of((SEQ, D), f32),
            shape_of((SEQ, D), bf16),
            shape_of((SEQ, 128), f32),
            shape_of((1, D), f32),
            shape_of((len(near), *dims), bf16),
            shape_of((len(far), *dims), bf16),
        ],
        [in_vmem] * 6,
        limit=16,
        name="gate_lead",
    )


def down_grads(order, places, low, hidden, first, height, fold, count):
    near, far = slots_of(count)
    width = FF // count
    outs = [shape_of((len(near), height // fold, fold * width), bf16)]
    if far:
        outs.append(shape_of((len(far), height // fold, fold * width), bf16))
    return order.call(
        functools.partial(down_grads_kernel, count, first, height, fold),
        [places, low, hidden],
        [in_smem, in_vmem, in_vmem],
        outs,
        [in_vmem] * len(outs),
        limit=16,
        name="down_grads",
    )


def first_kernel(count, places, total, rows, vectors, normed, own, returned, *rest):
    parts, rest = rest[:count], rest[count:]
    queries, pair, rest = rest[:GROUPS], rest[GROUPS], rest[GROUPS + 1 :]
    gain_two, bias_two, output_bias, gate_own, hidden_bias = rest[:5]
    grad_out, outs = rest[5], rest[6:-5]
    pair_low, normed_grad, weight, whole, short = rest[-5:]
    pair_low[...] = (own[...] + returned[:, :SEQ].astype(f32)).astype(bf16)
    assemble(places, parts, weight)
    for group, pairs in enumerate((pair, pair_low)):
        start = group * PART
        block = dot_nt(queries[group][...], weight[:, start : start + PART])
        for kind in range(2):
            start = (kind + 1) * D + group * PART
            block += dot_nt(pairs[kind], weight[:, start : start + PART])
        if group == 0:
            normed_grad[...] = block
        else:
            normed_grad[...] += block
    scaled, root = normalise(rows[...].astype(f32))
    incoming = normed_grad[...]
    short[...] = jnp.zeros_like(short)
    short[0:1] = column_sums(incoming * scaled)
    short[1:2] = column_sums(incoming)
    for line, member in enumerate((gain_two, bias_two, output_bias)):
        short[line + 2 : line + 3] = member[...]
    short[5:6] = gate_own[0:1]
    for kind in range(2):
        line = returned[kind, SEQ : SEQ + 8].astype(f32)
        short[6:7, kind * PART : (kind + 1) * PART] = line[1:2]
    for line in range(FF // D):
        short[line + 8 : line + 9] = hidden_bias[:, line * D : (line + 1) * D]
    grad_out[...] = total[...] + norm_back(scaled, root, vectors[0:1], incoming)
    turned = normed[...].T
    for kind in range(2):
        whole[:, kind * PART : (kind + 1) * PART] = dot(turned, pair_low[kind]).astype(bf16)
    height = D // count
    for out, slots in zip(outs, slots_of(count)):
        for place, slot in enumerate(slots):
            begin = pl.multiple_of(places[slot] * height, 16)
            out[place * height : (place + 1) * height] = whole[pl.ds(begin, height)]
        out[len(slots) * height :] = short[...].astype(bf16)


def first_pass(
    order, places, total, rows, vectors, normed, own, returned, parts, queries, pair, short
):
    count = len(parts)
    args = [total, rows, vectors, normed, own, returned, *parts, *queries, pair, *short]
    outs = [
        shape_of((len(slots) * (D // count) + 16, 2 * PART), bf16) for slots in slots_of(count) if slots
    ]
    return order.call(
        functools.partial(first_kernel, count),
        [places, *args],
        [in_smem] + [in_vmem] * len(args),
        [shape_of((SEQ, D), f32)] + outs,
        [in_vmem] * (1 + len(outs)),
        scratch=[
            pltpu.VMEM((2, SEQ, PART), bf16),
            pltpu.VMEM((SEQ, D), f32),
            pltpu.VMEM((D, 3 * D), bf16),
            pltpu.VMEM((D, 2 * PART), bf16),
            pltpu.VMEM((16, D), f32),
        ],
        limit=20,
        name="first",
    )


def settle_kernel(kind, count, outs, places, *refs):
    totals, returned, refs = refs[:count], refs[count : 2 * count], refs[2 * count :]
    targets, (scratch, sems) = refs[:outs], (refs[outs : 2 * outs], refs[2 * outs])
    copies = []

    def leave(index, *where):
        source, target = scratch[index].at[where], targets[index].at[where]
        copies.append(pltpu.make_async_copy(source, target, sems.at[len(copies)]))
        copies[-1].start()

    inner = jnp.logical_and(places[4] > 0, places[4] < 3)
    values = [jnp.where(inner, a[...], b[...]).astype(f32) for a, b in zip(totals, returned)]
    out, every = scratch[0], slice(None)
    if kind == "turn":
        first = 0
        for value in values:
            rows = value.shape[0]
            start = first
            for k in range(0, value.shape[1], D):
                out[:, first : first + rows] = value[:, k : k + D].T
                first += rows
            leave(0, every, pl.ds(start, first - start))
    elif kind == "columns":
        first = 0
        for value in values:
            out[:, first : first + value.shape[1]] = value
            leave(0, every, pl.ds(first, value.shape[1]))
            first += value.shape[1]
    else:
        scratch[1][...] = values[0][:, :D]
        leave(1, every)
        out[:, :D] = values[0][:, D:]
        for group, value in enumerate(values[1:]):
            for part in range(2):
                start = (part + 1) * D + group * PART
                out[:, start : start + PART] = value[:, part * PART : (part + 1) * PART]
        leave(0, every)
    for copy in copies:
        copy.wait()


def settle(order, kind, places, blocks, dims):
    count = len(blocks)
    found = order.call(
        functools.partial(settle_kernel, kind, count, len(dims)),
        [places] + [block[0] for block in blocks] + [block[1] for block in blocks],
        [in_smem] + [in_vmem] * (2 * count),
        [shape_of(each, f32) for each in dims],
        [in_hbm] * len(dims),
        scratch=[pltpu.VMEM(each, f32) for each in dims] + [pltpu.SemaphoreType.DMA((8,))],
        name="settle",
    )
    return found[0] if len(dims) == 1 else found


def last_settle_kernel(places, total, returned, given, out, *rest):
    short_outs, (scratch, sems) = rest[:8], rest[8:]
    inner = jnp.logical_and(places[4] > 0, places[4] < 3)
    value = jnp.where(inner, total[...], returned[...]).astype(f32)
    rows = scratch.shape[1]
    copies = []
    for part in range(2):
        scratch[part] = value[:rows, part * PART : (part + 1) * PART]
        place = out.at[:, pl.ds((part + 1) * D + PART, PART)]
        copies.append(pltpu.make_async_copy(scratch.at[part], place, sems.at[part]))
        copies[-1].start()
    short = value[rows:]
    turned = pltpu.roll(short, D - places[0] * rows, 1)
    for line in range(7):
        short_outs[line][...] = turned[line : line + 1, :rows].reshape(rows)
    line = lax.broadcasted_iota(jnp.int32, short.shape, 0)
    hidden = jnp.sum(jnp.where(line == 8 + places[0], short, 0.0), axis=0)
    short_outs[7][...] = hidden
    for copy in copies:
        copy.wait()


def last_settle(order, places, block, given):
    rows = given.shape[0]
    shorts = [shape_of((rows,), f32)] * 7 + [shape_of((D,), f32)]
    found = order.call(
        last_settle_kernel,
        [places, block[0], block[1], given],
        [in_smem, in_vmem, in_vmem, in_hbm],
        [shape_of(given.shape, f32)] + shorts,
        [in_hbm] + [in_vmem] * 8,
        scratch=[pltpu.VMEM((2, rows, PART), f32), pltpu.SemaphoreType.DMA((2,))],
        name="last_settle",
        aliases={3: 0},
    )
    return found[0], found[1:]


def swap_bit(value, axis, bit):
    size = lax.axis_size(axis)
    return lax.ppermute(value, axis, [(source, source ^ (1 << bit)) for source in range(size)])


def from_partner(value):
    size = lax.axis_size("stream")
    half = size // 2
    return lax.ppermute(value, "stream", [(source, (source + half) % size) for source in range(size)])


def along(value, pairs):
    return lax.ppermute(value, "dp", pairs)


def up_line(value, steps):
    return along(value, [(floor, floor + 1) for floor in range(steps - 1, 3)])


def down_line(value, steps):
    return along(value, [(floor, floor - 1) for floor in range(1, 5 - steps)])


def swap_outer(value):
    return along(value, [(0, 1), (1, 0), (2, 3), (3, 2)])


def to_inner(value):
    return along(value, [(0, 1), (3, 2)])


def over_middle(value):
    return along(value, [(1, 2), (2, 1)])


def to_outer(value):
    return along(value, [(1, 0), (2, 3)])


def core(value):
    return swap_bit(value, "stream", 0)


def across(value):
    return swap_bit(value, "stream", 1)


def modality_groups():
    size = lax.axis_size("stream")
    half = size // 2
    return [list(range(half)), list(range(half, size))]


def body(
    regions,
    cotangent,
    page_lens,
    qkv_weight,
    out_weight,
    up_weight,
    down_weight,
    ln1_gain,
    ln1_bias,
    ln2_gain,
    ln2_bias,
    up_bias,
    down_bias,
    gate_own,
    gate_other,
):
    half = lax.axis_size("stream") // 2
    depth = lax.axis_size("dp")
    paired = half == 4 and depth == 4
    side = lax.axis_index("stream") % half
    floor = lax.axis_index("dp")
    count = 4 if paired else 1
    slots = jnp.arange(4, dtype=jnp.int32)
    picks = jnp.bitwise_xor(side.astype(jnp.int32), slots) if paired else jnp.zeros_like(slots)
    places = jnp.concatenate([picks, floor.astype(jnp.int32)[None]])
    order = Order()
    short = (ln1_gain, ln1_bias, ln2_gain, ln2_bias, down_bias, gate_own, gate_other, up_bias)
    partner_tangent = from_partner(cotangent)

    def attend_group(group, waits=()):
        context, log_total = attend(
            order,
            group * PART // PAIR,
            queries,
            own_pairs[group],
            other_pairs[group],
            page_row,
            page_column,
            waits,
        )
        contexts.append(context)
        logs.append(log_total)

    contexts, logs = [], []
    if paired:
        qkv_shard = first_cast_pass(order, qkv_weight, short)
        qkv_across, qkv_near = across(qkv_shard), core(qkv_shard)
        wide_shard, down_shard, lead, half_own, page_row, page_column = cast_pass(
            order, places, page_lens, out_weight, up_weight, down_weight
        )
        wide_near, down_near = core(wide_shard), core(down_shard)
        (qkv_across,) = order.hold([qkv_across], waits=[partner_tangent, qkv_near])
        qkv_far, half_own = core(qkv_across), across(half_own)
        qkv_parts = [qkv_shard, qkv_near, qkv_across, qkv_far]
        own_pairs, normed, vectors, hidden_bias = pairs_pass(
            order, places, regions, qkv_parts, waits=[wide_near, down_near]
        )
        queries = queries_pass(order, places, normed, qkv_parts)
        other_pairs = [from_partner(pair) for pair in own_pairs]
        lead_across = across(lead)
        (half_own,) = order.hold([half_own])
        half_other, half_own_far = swap_outer(half_own), core(half_own)
        attend_group(0)
        (lead_across,) = order.hold([lead_across])
        vectors = order.pause(vectors)
        (half_other,) = order.hold([half_other])
        half_other_far, lead_far = core(half_other), core(lead_across)
        attend_group(1)
        wides, downs = [wide_shard, wide_near], [down_shard, down_near]
        leads = [lead_across, lead_far]
        halves = [(half_own, half_other), (half_own_far, half_other_far)]
    else:
        lengths = lax.dynamic_slice_in_dim(page_lens, side * depth + floor, 1, 0)
        positions = jnp.arange(SEQ, dtype=jnp.int32)
        page_ends = jnp.cumsum(lengths[0], dtype=jnp.int32)
        pages = jnp.sum((page_ends[:, None] <= positions[None, :]).astype(jnp.int32), axis=0)
        page_row, page_column = pages[None, :], pages[:, None]

        def gather(shard):
            return [
                lax.all_gather(shard, "stream", axis_index_groups=modality_groups(), tiled=True)
            ]

        packed = jnp.concatenate([member.astype(bf16) for member in short])[None]
        found = gather(packed)[0].astype(f32)
        shard = D // half
        rows = [found[:, k * shard : (k + 1) * shard].reshape(1, D) for k in range(7)]
        given = (
            jnp.concatenate(rows + [jnp.zeros((1, D), f32)], axis=0),
            found[:, 7 * shard :].reshape(1, FF),
        )
        qkv_parts = gather(qkv_weight.astype(bf16))
        wides = gather(jnp.concatenate([out_weight, up_weight], axis=1).astype(bf16))
        downs, leads, halves = gather(down_weight.astype(bf16)), [], []
        own_pairs, normed, vectors, hidden_bias = pairs_pass(
            order, places, regions, qkv_parts, given
        )
        queries = queries_pass(order, places, normed, qkv_parts)
        other_pairs = [from_partner(pair) for pair in own_pairs]
        for group in range(GROUPS):
            attend_group(group)

    middle, second, hidden, slope, modal, inner_own, wide, down = middle_pass(
        order,
        places,
        regions,
        contexts,
        partner_tangent,
        vectors,
        other_pairs[-1],
        hidden_bias,
        wides,
        downs,
        leads,
        halves,
    )
    inner_other = from_partner(inner_own)
    if paired:
        modal_grad, modal_low, columns, output_bias_grad, d1, d1_far = gate_lead_pass(
            order, places, hidden, inner_own, inner_other, cotangent, partner_tangent, vectors, other_pairs[-1], 384, 2, count
        )
    else:
        modal_grad, modal_low, columns, output_bias_grad = gate_pass(
            order, inner_own, inner_other, cotangent, partner_tangent, vectors, other_pairs[-1]
        )

    def attend_back_group(group):
        query_grad, own_grad, other_grad = attend_back(
            order,
            group * PART // PAIR,
            queries,
            own_pairs[group],
            other_pairs[group],
            context_grad,
            logs[group],
            page_row,
            page_column,
            [gate_sums] if group == GROUPS - 1 else [],
        )
        query_grads.append(query_grad)
        own_grads.append(own_grad)
        returned.append(from_partner(other_grad))

    def last_pass(pair_low):
        short_grads = (
            gain_two_grad,
            bias_two_grad,
            output_bias_grad,
            gate_sums,
            hidden_bias_grad,
        )
        return first_pass(
            order,
            places,
            middle_grad,
            regions,
            vectors,
            normed,
            own_grads[1],
            returned[1],
            qkv_parts,
            query_grads,
            pair_low,
            short_grads,
        )

    query_grads, own_grads, returned = [], [], []
    back = (order, places, modal_low, modal_grad, slope, middle, vectors, wide, down)
    if paired:
        d1_core = core(d1_far)
        d2, far = down_grads(order, places, modal_low, hidden, 384, 384, 2, count)
        d2_core = core(far)
        d1, away = sums_pass(order, places, folds=[(d1, d1_core, [FF // 2])])
        d1_in = across(away)
        d2, d2_away = sums_pass(order, places, folds=[(d2, d2_core, [FF // 2])])
        middle_grad, middle_low, context_grad, upper_low, *rest = chain_pass(*back)
        hidden_bias_grad, gain_two_grad, bias_two_grad = rest
        d1 = sums_pass(order, places, adds=[(d1, d1_in)])
        d1_in = to_inner(d1)
        (d2_away,) = order.hold([d2_away])
        d2_in = across(d2_away)
        gate_sums = gate_sums_pass(order, modal, columns)
        u1, far_one, u2, far_two = up_grads(
            order, places, second, upper_low, [FF // 2, FF // 2], count
        )
        u1_core, u2_core = core(far_one), core(far_two)
        attend_back_group(0)
        d2, d1 = sums_pass(order, places, adds=[(d2, d2_in), (d1, d1_in)])
        d2_in, d1_mid = to_inner(d2), over_middle(d1)
        columns = order.pause(columns)
        u1, away = sums_pass(order, places, folds=[(u1, u1_core, [FF // 2])])
        u1_in = across(away)
        u2, away = sums_pass(order, places, folds=[(u2, u2_core, [FF // 2])])
        attend_back_group(1)
        d2, u1, u1_pay = sums_pass(
            order, places, adds=[(d2, d2_in)], pays=[(u1, u1_in, d1, d1_mid)]
        )
        u1_in, d2_mid = swap_outer(u1_pay), over_middle(d2)
        (away,) = order.hold([away])
        u2_in = across(away)
        pair_low, lead_near, lead_far = lead_grads(
            order, places, contexts, middle_low, normed, query_grads, own_grads[0], returned[0], count
        )
        lead_core = core(lead_far)
        u1, u2, u2_pay = sums_pass(
            order, places, adds=[(u1, u1_in)], pays=[(u2, u2_in, d2, d2_mid)]
        )
        d1_out = u1_in
        u2_in, u1_mid = swap_outer(u2_pay), over_middle(u1)
        gate_sums = order.pause(gate_sums)
        oq, away, p1, away_two = sums_pass(
            order, places, folds=[(lead_near, lead_core, [2 * D, D])]
        )
        oq_in = across(away)
        region_grad, last_near, last_far = last_pass(pair_low)
        last_core = core(last_far)
        u2, oq, oq_pay = sums_pass(
            order, places, adds=[(u2, u2_in)], pays=[(oq, oq_in, u1, u1_mid)]
        )
        d2_out = u2_in
        oq_in, u2_mid = swap_outer(oq_pay), over_middle(u2)
        (away_two,) = order.hold([away_two])
        p1_in = across(away_two)
        modal = order.pause(modal)
        p2, away = sums_pass(order, places, folds=[(last_near, last_core, [D])])
        p2_in = across(away)
        down_grad = settle(order, "turn", places, [(u1_pay, d1_out), (u2_pay, d2_out)], [(D, D)])
        oq, u2, p1 = sums_pass(
            order, places, adds=[(oq, oq_in), (u2, u2_mid), (p1, p1_in)]
        )
        u1_out = oq_in
        oq_mid, u2_out, p1_in = over_middle(oq), to_outer(u2), to_inner(p1)
        p2 = sums_pass(order, places, adds=[(p2, p2_in)])
        p2_in = to_inner(p2)
        p1 = sums_pass(order, places, adds=[(p1, p1_in)])
        p1_mid = over_middle(p1)
        (modal,) = order.hold([modal])
        partner_modal = from_partner(modal)
        oq, p2 = sums_pass(order, places, adds=[(oq, oq_mid), (p2, p2_in)], waits=[u2_out])
        oq_out, p2_mid = to_outer(oq), over_middle(p2)
        up_grad = settle(order, "columns", places, [(oq_pay, u1_out), (u2, u2_out)], [(D // 4, FF)])
        p1 = sums_pass(order, places, adds=[(p1, p1_mid)])
        p1_out = to_outer(p1)
        p2 = sums_pass(order, places, adds=[(p2, p2_mid)])
        p2_out = to_outer(p2)
        mixed_rows = mix_pass(order, modal, partner_modal, columns, [oq_out])
        qkv_grad, out_grad = settle(
            order,
            "pairs",
            places,
            [(oq, oq_out), (p1, p1_out)],
            [(D // 4, 3 * D), (D // 4, D)],
        )
        qkv_grad, shorts = last_settle(order, places, (p2, p2_out), qkv_grad)
    else:
        (down_block,) = down_grads(order, places, modal_low, hidden, 0, D, 1, count)
        middle_grad, middle_low, context_grad, upper_low, *rest = chain_pass(*back)
        hidden_bias_grad, gain_two_grad, bias_two_grad = rest
        (up_block,) = up_grads(order, places, second, upper_low, [FF], count)
        gate_sums = gate_sums_pass(order, modal, columns)
        for group in range(GROUPS):
            attend_back_group(group)
        mixed_rows = mix_pass(order, modal, from_partner(modal), columns)
        pair_low, lead_block = lead_grads(
            order, places, contexts, middle_low, normed, query_grads, own_grads[0], returned[0], count
        )
        region_grad, last_block = last_pass(pair_low)
        lead_block = lead_block[0]
        short_rows = last_block[D:].astype(f32)

        def total(block):
            groups = modality_groups()
            owned = lax.psum_scatter(
                block.astype(f32), "stream", axis_index_groups=groups, tiled=True
            )
            return lax.psum(owned, "dp")

        down_grad = total(down_block[0].T)
        up_grad, out_grad = total(up_block[0]), total(lead_block[:, :D])
        qkv_grad = total(
            jnp.concatenate(
                [
                    lead_block[:, D : 2 * D + PART],
                    last_block[:D, :PART],
                    lead_block[:, 2 * D + PART :],
                    last_block[:D, PART:],
                ],
                axis=1,
            )
        )
        short_rows = lax.psum(
            lax.psum(short_rows, "stream", axis_index_groups=modality_groups()), "dp"
        )

        shard = D // half
        own_rows = lax.dynamic_slice_in_dim(short_rows, side * shard, shard, 1)
        hidden_rows = short_rows[8 : 8 + FF // D].reshape(FF)
        own_hidden = lax.dynamic_slice_in_dim(hidden_rows, side * (FF // half), FF // half, 0)
        shorts = [own_rows[k] for k in range(7)] + [own_hidden]
    return (
        mixed_rows,
        region_grad,
        qkv_grad,
        out_grad,
        up_grad,
        down_grad,
        shorts[0],
        shorts[1],
        shorts[2],
        shorts[3],
        shorts[7],
        shorts[4],
        shorts[5],
        shorts[6],
    )


def solution(mesh):
    in_specs = (
        P(("stream", "dp"), None),
        P(("stream", "dp"), None),
        P(),
        P("stream", None),
        P("stream", None),
        P("stream", None),
        P("stream", None),
        P("stream"),
        P("stream"),
        P("stream"),
        P("stream"),
        P("stream"),
        P("stream"),
        P("stream"),
        P("stream"),
    )
    out_specs = (
        P(("stream", "dp"), None),
        P(("stream", "dp"), None),
        P("stream", None),
        P("stream", None),
        P("stream", None),
        P("stream", None),
        P("stream"),
        P("stream"),
        P("stream"),
        P("stream"),
        P("stream"),
        P("stream"),
        P("stream"),
        P("stream"),
    )
    return jax.shard_map(body, mesh=mesh, in_specs=in_specs, out_specs=out_specs, check_vma=False)
```
